512 devices in a mesh: px: 32 (over x, z), py: 16 (over y, core).
Axes of the slice: x: 4, y: 8, z: 8, core: 2. Of those that a mesh axis runs over, the one named last changes fastest.
Arguments:
- field: bfloat16 [32, 256, 256, 128], P(None, 'px', 'py'), may hold values from -6 to 6
- spec_weight: bfloat16 [1, 2, 32, 32, 32, 32, 32], P(None, None, None, None, None, 'px', 'py'), may hold values from -0.5 to 0.5
- w_in: bfloat16 [1, 32, 128], replicated, may hold values from -1 to 1
- b_in: float32 [1, 128], replicated, may hold values from -4 to 4
- w_out: bfloat16 [1, 128, 32], replicated, may hold values from -0.5 to 0.5
Outputs:
- result: bfloat16 [32, 256, 256, 128], P(None, 'px', 'py')
The draws below stay inside these ranges and needn't reach their ends.
All inputs are finite; a program needn't handle non-finite values.
Results may differ from the reference program's by a relative error of at most 0.015.
Values may be sent and summed in bfloat16 or wider, within the bound.
A program may use at most 64 MiB of HBM per device.

```python
import math
import jax
import jax.numpy as jnp
from jax import lax

C = 32
HID = 128
NX = 256
NY = 256
NZ = 128
MX = 32
MY = 32
MZ = 32
LAYERS = 1


def block_scale(own_key, shape, shards, low, high):
    gain, own = 1.0, jax.random.fold_in(own_key, 6)
    for position, blocks in shards:
        steps = jnp.exp(jax.random.uniform(jax.random.fold_in(own, position), (blocks,), jnp.float32, low / len(shards), high / len(shards)))
        gain = gain * jnp.repeat(steps, shape[position] // blocks).reshape([-1 if axis == position else 1 for axis in range(len(shape))])
    return gain


def bell_draw(rng, shape, scale, reach, cuts=(), held_as=jnp.bfloat16):
    drawn = scale * jax.random.normal(rng, shape, jnp.float32)
    if cuts:
        drawn = drawn * block_scale(rng, shape, cuts, -0.22, 0.18)
    return jnp.clip(drawn, -reach, reach).astype(held_as)


def setup_inputs(seed: int = 0) -> dict:
    seeds = jax.random.split(jax.random.key(seed), 6)
    return {
        "field": bell_draw(seeds[0], (C, NX, NY, NZ), 1.0, 6.0, ((1, 32), (2, 16))),
        "spec_weight": bell_draw(seeds[1], (LAYERS, 2, C, C, MX, MY, MZ), (4 * C) ** -0.5, 0.5, ((5, 32), (6, 16))),
        "w_in": bell_draw(seeds[2], (LAYERS, C, HID), C ** -0.5, 1.0),
        "b_in": bell_draw(seeds[3], (LAYERS, HID), 1.0, 4.0, (), jnp.float32),
        "w_out": bell_draw(seeds[4], (LAYERS, HID, C), HID ** -0.5, 0.5),
    }


HIGH_PRECISION = lax.Precision.HIGHEST

def trig_table(positions, freqs, length):
    phase = positions[:, None] * freqs[None, :] % length
    angle = phase.astype(jnp.float32) * (2.0 * math.pi / length)
    return (jnp.cos(angle), jnp.sin(angle))

def signed_modes(count, length):
    index = jnp.arange(count, dtype=jnp.int32)
    return jnp.where(index < count // 2, index, index - count + length).astype(jnp.int32)

def to_half(value):
    return lax.optimization_barrier(value.astype(jnp.bfloat16))

def spectral_block(field, spectral_weight, w_in, b_in, w_out, tables):
    cos_z, sin_z, cos_y, sin_y, cosine_table_x, sine_table_x, weight_z = tables

    def forward_z(index):
        plane = lax.dynamic_index_in_dim(field, index, 1, keepdims=False).astype(jnp.float32)
        real_part = jnp.einsum('cyz,zk->cyk', plane, cos_z, precision=HIGH_PRECISION) * (1.0 / math.sqrt(NZ))
        imaginary_part = -jnp.einsum('cyz,zk->cyk', plane, sin_z, precision=HIGH_PRECISION) * (1.0 / math.sqrt(NZ))
        return to_half(jnp.stack([real_part, imaginary_part]))
    zspec = lax.map(forward_z, jnp.arange(NX, dtype=jnp.int32))
    real_part = zspec[:, 0].astype(jnp.float32)
    imaginary_part = zspec[:, 1].astype(jnp.float32)
    scale_y = 1.0 / math.sqrt(NY)
    real_part, imaginary_part = ((jnp.einsum('xcyk,yf->xcfk', real_part, cos_y, precision=HIGH_PRECISION) + jnp.einsum('xcyk,yf->xcfk', imaginary_part, sin_y, precision=HIGH_PRECISION)) * scale_y, (jnp.einsum('xcyk,yf->xcfk', imaginary_part, cos_y, precision=HIGH_PRECISION) - jnp.einsum('xcyk,yf->xcfk', real_part, sin_y, precision=HIGH_PRECISION)) * scale_y)
    scale_x = 1.0 / math.sqrt(NX)
    input_real = (jnp.einsum('xcfk,xg->cgfk', real_part, cosine_table_x, precision=HIGH_PRECISION) + jnp.einsum('xcfk,xg->cgfk', imaginary_part, sine_table_x, precision=HIGH_PRECISION)) * scale_x
    input_imaginary = (jnp.einsum('xcfk,xg->cgfk', imaginary_part, cosine_table_x, precision=HIGH_PRECISION) - jnp.einsum('xcfk,xg->cgfk', real_part, sine_table_x, precision=HIGH_PRECISION)) * scale_x
    weight_real = spectral_weight[0].astype(jnp.float32)
    weight_imaginary = spectral_weight[1].astype(jnp.float32)
    value_real = jnp.einsum('yjur,yzjur->zjur', input_real, weight_real, precision=HIGH_PRECISION) - jnp.einsum('yjur,yzjur->zjur', input_imaginary, weight_imaginary, precision=HIGH_PRECISION)
    value_imaginary = jnp.einsum('yjur,yzjur->zjur', input_real, weight_imaginary, precision=HIGH_PRECISION) + jnp.einsum('yjur,yzjur->zjur', input_imaginary, weight_real, precision=HIGH_PRECISION)
    inverse_scale_x = 1.0 / math.sqrt(MX)
    real_part = (jnp.einsum('phcy,ih->ipcy', value_real, cosine_table_x, precision=HIGH_PRECISION) - jnp.einsum('phcy,ih->ipcy', value_imaginary, sine_table_x, precision=HIGH_PRECISION)) * inverse_scale_x
    imaginary_part = (jnp.einsum('phcy,ih->ipcy', value_real, sine_table_x, precision=HIGH_PRECISION) + jnp.einsum('phcy,ih->ipcy', value_imaginary, cosine_table_x, precision=HIGH_PRECISION)) * inverse_scale_x
    iscale_y = 1.0 / math.sqrt(MY)
    cre = (jnp.einsum('xcfk,yf->xcyk', real_part, cos_y, precision=HIGH_PRECISION) - jnp.einsum('xcfk,yf->xcyk', imaginary_part, sin_y, precision=HIGH_PRECISION)) * iscale_y
    cim = (jnp.einsum('xcfk,yf->xcyk', real_part, sin_y, precision=HIGH_PRECISION) + jnp.einsum('xcfk,yf->xcyk', imaginary_part, cos_y, precision=HIGH_PRECISION)) * iscale_y
    back_re = to_half(cre)
    back_im = to_half(cim)
    win = w_in.astype(jnp.float32)
    wout = w_out.astype(jnp.float32)

    def finish(index):
        real_z = lax.dynamic_index_in_dim(back_re, index, 0, keepdims=False).astype(jnp.float32)
        imag_z = lax.dynamic_index_in_dim(back_im, index, 0, keepdims=False).astype(jnp.float32)
        spectral = (jnp.einsum('cyk,zk->cyz', real_z * weight_z, cos_z, precision=HIGH_PRECISION) - jnp.einsum('cyk,zk->cyz', imag_z * weight_z, sin_z, precision=HIGH_PRECISION)) * (1.0 / math.sqrt(MZ))
        plane = lax.dynamic_index_in_dim(field, index, 1, keepdims=False).astype(jnp.float32)
        before = jnp.einsum('ch,cyz->hyz', win, plane, precision=HIGH_PRECISION) + b_in[:, None, None]
        hidden = to_half(jax.nn.gelu(before, approximate=True)).astype(jnp.float32)
        channel = jnp.einsum('hc,hyz->cyz', wout, hidden, precision=HIGH_PRECISION)
        return jax.nn.gelu(spectral + channel, approximate=True).astype(jnp.bfloat16)
    planes = lax.map(finish, jnp.arange(NX, dtype=jnp.int32))
    return jnp.moveaxis(planes, 0, 1)

def reference(field, spec_weight, w_in, b_in, w_out):
    cos_z, sin_z = trig_table(jnp.arange(NZ, dtype=jnp.int32), jnp.arange(MZ, dtype=jnp.int32), NZ)
    cos_y, sin_y = trig_table(jnp.arange(NY, dtype=jnp.int32), signed_modes(MY, NY), NY)
    cosine_table_x, sine_table_x = trig_table(jnp.arange(NX, dtype=jnp.int32), signed_modes(MX, NX), NX)
    weight_z = jnp.where(jnp.arange(MZ, dtype=jnp.int32) == 0, 1.0, 2.0).astype(jnp.float32)
    tables = (cos_z, sin_z, cos_y, sin_y, cosine_table_x, sine_table_x, weight_z)
    for layer in range(LAYERS):
        field = spectral_block(field, spec_weight[layer], w_in[layer], b_in[layer], w_out[layer], tables)
    return field
```

```python
import functools
import math

import jax
import jax.numpy as jnp
import ml_dtypes
import numpy as np
from jax import lax
from jax.experimental import pallas as pl
from jax.experimental.pallas import tpu as pltpu
from jax.sharding import PartitionSpec as P

MESH = pl.DeviceIdType.MESH
BF = jnp.bfloat16
F32 = jnp.float32
C = 32
HID = 128
XL = 8
YL = 16
NZ = 128
K2 = 2
NT = (((1,), (1,)), ((), ()))
NN = (((1,), (0,)), ((), ()))
TN = (((0,), (0,)), ((), ()))


def dot(a, b, dims):
    return lax.dot_general(a, b, dims, preferred_element_type=F32)


def signed(count, length):
    index = np.arange(count)
    return np.where(index < count // 2, index, index - count + length)


def angles(positions, freqs, length):
    return 2.0 * math.pi * ((positions[:, None] * freqs[None, :]) % length) / length


def tables(npx, npy, mx):
    nx, ny, my, mz = XL * npx, YL * npy, npx, K2 * npy
    ang = angles(np.arange(NZ), np.arange(mz), NZ)
    fwd = np.stack([np.cos(ang), -np.sin(ang)]) * 0.125
    fwd = fwd.reshape(2, NZ, npy, K2).transpose(2, 0, 3, 1)
    a1 = np.zeros((2, npy, 2, 4, K2, 2, NZ))
    for q in range(2):
        for c in range(2):
            a1[q, :, :, 2 * q + c, :, c, :] = fwd
    a1 = a1.reshape(2, npy * 16, 2 * NZ)
    ang = angles(np.arange(ny), signed(my, ny), ny)
    cs = np.stack([np.cos(ang), np.sin(ang)]).reshape(2, npy // 2, 2, YL, my)
    a2 = np.zeros((npy // 2, 2, my, XL, 2, XL, YL))
    for x in range(XL):
        a2[:, :, :, x, :, x, :] = cs.transpose(1, 0, 4, 2, 3)
    a2 = a2.reshape(npy // 2, 2 * my * XL, 2 * XL * YL)
    ang = angles(np.arange(nx), signed(mx, nx), nx)
    cs = np.stack([np.cos(ang), np.sin(ang)])
    tx = cs.transpose(0, 2, 1).reshape(2 * mx, nx) / math.sqrt(nx * ny)
    tix = cs.reshape(2 * nx, mx) / math.sqrt(mx * my)
    ang = angles(np.arange(NZ), np.arange(mz), NZ)
    weight = np.where(np.arange(mz) == 0, 1.0, 2.0) * (8.0 / math.sqrt(NZ * mz))
    inv = np.stack([np.cos(ang), -np.sin(ang)]) * weight
    inv = inv.reshape(2, NZ, npy, K2).transpose(2, 0, 3, 1)
    b7 = np.zeros((npy, 2, 8, K2, 8, NZ))
    for o in range(8):
        b7[:, :, o, :, o, :] = inv
    b7 = b7.reshape(npy * 32, 8 * NZ)
    e8 = np.zeros((2 * C, 8, 2 * C, K2))
    for r in range(8):
        e8[np.arange(2 * C), r, np.arange(2 * C), r % 2] = 1.0
    e8 = e8.reshape(2 * C * 8, 2 * C * K2)

    def half(t):
        return t.astype(np.float32).astype(ml_dtypes.bfloat16)

    def two(t):
        high = half(t)
        return np.stack([high, half(t - high.astype(np.float64))])

    return half(a1), half(a2), two(tx), two(tix), half(b7), half(e8)


def split(value):
    high = value.astype(BF)
    return high, (value - high.astype(F32)).astype(BF)


def dot3(table, value, dims):
    high, low = split(value)
    return dot(table[0], high, dims) + dot(table[0], low, dims) + dot(table[1], high, dims)


def gelu(v):
    k = math.sqrt(2.0 / math.pi)
    half = 0.5 * v
    return half + half * jnp.tanh(v * (k + (k * 0.044715) * (v * v)))


def kernel(
    npx, npy,
    f_ref, a1_ref, win_ref, bin_ref, wout_ref, w_hbm, a2_hbm, tx_hbm, tix_hbm, b7_hbm, e8_hbm,
    out_ref,
    zs, send1, recv1, send2, recv2, send3, recv3, send4, recv4,
    w_ref, a2_ref, tx_ref, tix_ref, b7_ref, e8_ref,
    k1, k2, bias, chan, xpat,
    ssem1, rsem1, ssem2, rsem2, ssem3, rsem3, ssem4, rsem4, tsem,
):
    ny = npy // 2
    mx = w_ref.shape[-1]
    mex = lax.axis_index("px")
    mey = lax.axis_index("py")
    my_chip = mey // 2
    my_core = mey % 2
    twin = my_chip * 2 + 1 - my_core

    loads = [
        pltpu.make_async_copy(src, dst, tsem.at[i])
        for i, (src, dst) in enumerate(
            [(a2_hbm, a2_ref), (tx_hbm, tx_ref), (e8_hbm, e8_ref), (w_hbm, w_ref), (tix_hbm, tix_ref), (b7_hbm, b7_ref)]
        )
    ]
    barrier = pltpu.get_barrier_semaphore()

    def greet_y(d, carry):
        pl.semaphore_signal(barrier, inc=1, device_id=(mex, lax.rem(mey + d, npy)), device_id_type=MESH)
        return carry

    def greet_x(d, carry):
        pl.semaphore_signal(barrier, inc=1, device_id=(lax.rem(mex + d, npx), mey), device_id_type=MESH)
        return carry

    lax.fori_loop(1, npy, greet_y, 0)
    lax.fori_loop(1, npx, greet_x, 0)
    for load in loads:
        load.start()

    def forward_z(g, carry):
        f4 = f_ref[pl.ds(g * 4, 4)]
        acc = dot(a1_ref[0], jnp.concatenate([f4[0], f4[1]], axis=1), NT)
        acc = acc + dot(a1_ref[1], jnp.concatenate([f4[2], f4[3]], axis=1), NT)
        zs[:, :, pl.ds(g, 1)] = acc.reshape(npy, 2, 1, 8, 128)
        return carry

    lax.fori_loop(0, C // 4, forward_z, 0, unroll=2)
    send1[...] = zs[...].reshape(npy, 128, 128).astype(BF)

    pl.semaphore_wait(barrier, npx + npy - 2)

    def y_copy(src, dst, ssem, rsem, target):
        return pltpu.make_async_remote_copy(
            src_ref=src.at[target], dst_ref=dst.at[mey], send_sem=ssem.at[target], recv_sem=rsem.at[mey],
            device_id=(mex, target), device_id_type=MESH,
        )

    def y_arrive(src, dst, ssem, rsem, source):
        pltpu.make_async_remote_copy(
            src_ref=src.at[source], dst_ref=dst.at[source], send_sem=ssem.at[source], recv_sem=rsem.at[source],
            device_id=(mex, source), device_id_type=MESH,
        ).wait_recv()

    def x_copy(src, dst, ssem, rsem, target):
        return pltpu.make_async_remote_copy(
            src_ref=src.at[target], dst_ref=dst.at[mex], send_sem=ssem.at[target], recv_sem=rsem.at[mex],
            device_id=(target, mey), device_id_type=MESH,
        )

    def x_exchange(src, dst, ssem, rsem):
        def start(d, carry):
            x_copy(src, dst, ssem, rsem, lax.rem(mex + d, npx)).start()
            return carry

        lax.fori_loop(1, npx, start, 0)
        dst[pl.ds(mex, 1)] = src[pl.ds(mex, 1)]

        def arrive(d, carry):
            source = lax.rem(mex + d, npx)
            pltpu.make_async_remote_copy(
                src_ref=src.at[source], dst_ref=dst.at[source], send_sem=ssem.at[source], recv_sem=rsem.at[source],
                device_id=(source, mey), device_id_type=MESH,
            ).wait_recv()
            return carry

        lax.fori_loop(1, npx, arrive, 0)

    def y_peers(far_first):
        offsets = sorted(range(1, ny), key=lambda d: min(d, ny - d), reverse=far_first)
        return [lax.rem(my_chip + d, ny) for d in offsets]

    for chip in y_peers(True):
        for core in range(2):
            y_copy(send1, recv1, ssem1, rsem1, chip * 2 + core).start()
    y_copy(send1, recv1, ssem1, rsem1, twin).start()
    recv1[pl.ds(mey, 1)] = send1[pl.ds(mey, 1)]

    spread = (lax.broadcasted_iota(jnp.int32, (C, C * 8), 1) // 8 == lax.broadcasted_iota(jnp.int32, (C, C * 8), 0))
    rows = dot(win_ref[...], spread.astype(F32).astype(BF), TN)
    same = lax.broadcasted_iota(jnp.int32, (HID, 8, C * 8), 1) == lax.rem(
        lax.broadcasted_iota(jnp.int32, (HID, 8, C * 8), 2), 8
    )
    k1[...] = jnp.where(same, rows[:, None, :], 0.0).reshape(HID * 8, C * 8).astype(BF)
    spread = (
        lax.broadcasted_iota(jnp.int32, (HID, HID * 8), 1) // 8 == lax.broadcasted_iota(jnp.int32, (HID, HID * 8), 0)
    )
    rows = dot(wout_ref[...], spread.astype(F32).astype(BF), NN)
    same = lax.broadcasted_iota(jnp.int32, (C, 8, HID * 8), 1) == lax.rem(
        lax.broadcasted_iota(jnp.int32, (C, 8, HID * 8), 2), 8
    )
    k2[...] = jnp.where(same, rows[:, None, :], 0.0).reshape(C * 8, HID * 8).astype(BF)
    turned = jnp.transpose(jnp.broadcast_to(bin_ref[...], (HID, HID)))
    bias[...] = jnp.broadcast_to(turned[:, None, :], (HID, 8, 128)).reshape(HID * 8, 128)

    def channel(i, carry):
        block = f_ref[:, pl.ds(pl.multiple_of(i * 16, 16), 16), :].astype(F32)
        cells = jnp.concatenate(
            [block[:, :8].reshape(C * 8, 128), block[:, 8:].reshape(C * 8, 128)], axis=1
        ).astype(BF)
        acc = jnp.zeros((C * 8, 256), F32)
        for part in range(4):
            rows = slice(part * 256, part * 256 + 256)
            b = bias[rows]
            hidden = gelu(dot(k1[rows], cells, NN) + jnp.concatenate([b, b], axis=1)).astype(BF)
            acc = acc + dot(k2[:, rows], hidden, NN)
        chan[:, pl.ds(pl.multiple_of(i * 16, 16), 8), :] = acc[:, :128].reshape(C, 8, 128)
        chan[:, pl.ds(pl.multiple_of(i * 16 + 8, 8), 8), :] = acc[:, 128:].reshape(C, 8, 128)
        return carry

    lax.fori_loop(0, 4, channel, 0)

    loads[0].wait()
    lane = lax.broadcasted_iota(jnp.int32, (1, 128), 1)
    sign = jnp.where(lane < 64, 1.0, -1.0)

    def y_part(chip):
        pair = jnp.concatenate([recv1[chip * 2], recv1[chip * 2 + 1]], axis=1)
        return dot(a2_ref[chip], pair, NT)

    y_arrive(send1, recv1, ssem1, rsem1, twin)
    acc = y_part(my_chip)
    for chip in y_peers(False):
        for core in range(2):
            y_arrive(send1, recv1, ssem1, rsem1, chip * 2 + core)
        acc = acc + y_part(chip)
    half = npx * XL
    lines = acc[:half] + sign * pltpu.roll(acc[half:], 64, 1)
    send2[...] = lines.reshape(npx, XL, 128).astype(BF)
    x_exchange(send2, recv2, ssem2, rsem2)

    loads[1].wait()
    loads[2].wait()
    block = recv2[...].astype(F32).reshape(half, 128).astype(BF)
    both = dot(tx_ref[0], block, NN) + dot(tx_ref[1], block, NN)
    spectra = both[:mx] + sign * pltpu.roll(both[mx:], 64, 1)
    high, low = split(spectra)
    xpat[...] = (dot(e8_ref[...], high, NT) + dot(e8_ref[...], low, NT)).reshape(2 * C, 8, mx)

    loads[3].wait()

    def mix(c, carry):
        real, imag = carry
        wr = w_ref[0, c].astype(F32).reshape(8, 8, mx)
        wi = w_ref[1, c].astype(F32).reshape(8, 8, mx)
        xr = xpat[c][None]
        xi = xpat[c + C][None]
        return real + xr * wr - xi * wi, imag + xr * wi + xi * wr

    zero = jnp.zeros((8, 8, mx), F32)
    real, imag = lax.fori_loop(0, C, mix, (zero, zero), unroll=4)
    modes = jnp.concatenate([real.reshape(64, mx), imag.reshape(64, mx)], axis=0)

    loads[4].wait()
    both = dot3(tix_ref, modes, NT)
    cells = both[:half] - sign * pltpu.roll(both[half:], 64, 1)
    send3[...] = cells.reshape(npx, XL, 128).astype(BF)
    x_exchange(send3, recv3, ssem3, rsem3)

    block = recv3[...].astype(F32).reshape(half, 128)
    turned = jnp.concatenate([block, -sign * pltpu.roll(block, 64, 1)], axis=0)
    turned = jnp.transpose(turned).astype(BF)

    def y_back(chip):
        both = dot(turned, a2_ref[chip], NN).astype(BF)
        send4[pl.ds(chip * 2, 1)] = both[:, :128][None]
        send4[pl.ds(chip * 2 + 1, 1)] = both[:, 128:][None]

    for chip in y_peers(True):
        y_back(chip)
        for core in range(2):
            y_copy(send4, recv4, ssem4, rsem4, chip * 2 + core).start()
    y_back(my_chip)
    y_copy(send4, recv4, ssem4, rsem4, twin).start()
    recv4[pl.ds(mey, 1)] = send4[pl.ds(mey, 1)]

    lax.fori_loop(4, 8, channel, 0)

    y_arrive(send4, recv4, ssem4, rsem4, twin)
    for chip in y_peers(False):
        for core in range(2):
            y_arrive(send4, recv4, ssem4, rsem4, chip * 2 + core)

    loads[5].wait()
    for g in range(4):
        lines = jnp.concatenate(
            [recv4[:, 16 * g : 16 * g + 16, :].reshape(npy, 1, 16, 128),
             recv4[:, 64 + 16 * g : 80 + 16 * g, :].reshape(npy, 1, 16, 128)], axis=1
        ).reshape(npy * 32, 128)
        values = dot(lines, b7_ref[...], TN)
        for o in range(8):
            total = values[:, 128 * o : 128 * o + 128] + chan[8 * g + o]
            out_ref[8 * g + o] = gelu(total).astype(BF)

    def sent_y(d, carry):
        target = lax.rem(mey + d, npy)
        y_copy(send1, recv1, ssem1, rsem1, target).wait_send()
        y_copy(send4, recv4, ssem4, rsem4, target).wait_send()
        return carry

    def sent_x(d, carry):
        target = lax.rem(mex + d, npx)
        x_copy(send2, recv2, ssem2, rsem2, target).wait_send()
        x_copy(send3, recv3, ssem3, rsem3, target).wait_send()
        return carry

    lax.fori_loop(1, npy, sent_y, 0)
    lax.fori_loop(1, npx, sent_x, 0)


def body(npx, npy, field, spec_weight, w_in, b_in, w_out):
    mx = spec_weight.shape[4]
    a1, a2, tx, tix, b7, e8 = tables(npx, npy, mx)
    cells = field.reshape(C, XL * YL, NZ)
    weight = jnp.transpose(spec_weight[0], (0, 1, 2, 4, 5, 3)).reshape(2, C, C * K2, mx)
    vmem = pl.BlockSpec(memory_space=pltpu.VMEM)
    anywhere = pl.BlockSpec(memory_space=pl.ANY)
    out = pl.pallas_call(
        functools.partial(kernel, npx, npy),
        out_shape=jax.ShapeDtypeStruct((C, XL * YL, NZ), BF),
        in_specs=[vmem] * 5 + [anywhere] * 6,
        out_specs=vmem,
        scratch_shapes=[
            pltpu.VMEM((npy, 2, 8, 8, 128), F32),
            pltpu.VMEM((npy, 128, 128), BF),
            pltpu.VMEM((npy, 128, 128), BF),
            pltpu.VMEM((npx, XL, 128), BF),
            pltpu.VMEM((npx, XL, 128), BF),
            pltpu.VMEM((npx, XL, 128), BF),
            pltpu.VMEM((npx, XL, 128), BF),
            pltpu.VMEM((npy, 128, 128), BF),
            pltpu.VMEM((npy, 128, 128), BF),
            pltpu.VMEM(weight.shape, BF),
            pltpu.VMEM(a2.shape, BF),
            pltpu.VMEM(tx.shape, BF),
            pltpu.VMEM(tix.shape, BF),
            pltpu.VMEM(b7.shape, BF),
            pltpu.VMEM(e8.shape, BF),
            pltpu.VMEM((HID * 8, C * 8), BF),
            pltpu.VMEM((C * 8, HID * 8), BF),
            pltpu.VMEM((HID * 8, 128), F32),
            pltpu.VMEM((C, XL * YL, NZ), F32),
            pltpu.VMEM((2 * C, 8, mx), F32),
            pltpu.SemaphoreType.DMA((npy,)),
            pltpu.SemaphoreType.DMA((npy,)),
            pltpu.SemaphoreType.DMA((npx,)),
            pltpu.SemaphoreType.DMA((npx,)),
            pltpu.SemaphoreType.DMA((npx,)),
            pltpu.SemaphoreType.DMA((npx,)),
            pltpu.SemaphoreType.DMA((npy,)),
            pltpu.SemaphoreType.DMA((npy,)),
            pltpu.SemaphoreType.DMA((6,)),
        ],
        compiler_params=pltpu.CompilerParams(
            collective_id=0, has_side_effects=True, vmem_limit_bytes=60 * 1024 * 1024
        ),
    )(
        cells, jnp.asarray(a1), w_in[0], b_in, jnp.transpose(w_out[0]), weight,
        jnp.asarray(a2), jnp.asarray(tx), jnp.asarray(tix), jnp.asarray(b7), jnp.asarray(e8),
    )
    return out.reshape(field.shape)


def solution(mesh):
    in_specs = (
        P(None, "px", "py", None),
        P(None, None, None, None, None, "px", "py"),
        P(),
        P(),
        P(),
    )
    return jax.shard_map(
        functools.partial(body, mesh.shape["px"], mesh.shape["py"]),
        mesh=mesh, in_specs=in_specs, out_specs=P(None, "px", "py", None), check_vma=False,
    )
```

```python
import functools
import math

import jax
import jax.numpy as jnp
import ml_dtypes
import numpy as np
from jax import lax
from jax.experimental import pallas as pl
from jax.experimental.pallas import tpu as pltpu
from jax.sharding import PartitionSpec as P

MESH = pl.DeviceIdType.MESH
BF = jnp.bfloat16
F32 = jnp.float32
C = 32
HID = 128
XL = 8
YL = 16
NZ = 128
K2 = 2
NT = (((1,), (1,)), ((), ()))
NN = (((1,), (0,)), ((), ()))
TN = (((0,), (0,)), ((), ()))


def dot(a, b, dims):
    return lax.dot_general(a, b, dims, preferred_element_type=F32)


def signed(count, length):
    index = np.arange(count)
    return np.where(index < count // 2, index, index - count + length)


def angles(positions, freqs, length):
    return 2.0 * math.pi * ((positions[:, None] * freqs[None, :]) % length) / length


def tables(npx, npy, mx):
    nx, ny, my, mz = XL * npx, YL * npy, npx, K2 * npy
    ang = angles(np.arange(NZ), np.arange(mz), NZ)
    fwd = np.stack([np.cos(ang), -np.sin(ang)]) * 0.125
    fwd = fwd.reshape(2, NZ, npy, K2).transpose(2, 0, 3, 1)
    a1 = np.zeros((2, npy, 2, 4, K2, 2, NZ))
    for q in range(2):
        for c in range(2):
            a1[q, :, :, 2 * q + c, :, c, :] = fwd
    a1 = a1.reshape(2, npy * 16, 2 * NZ)
    ang = angles(np.arange(ny), signed(my, ny), ny)
    cs = np.stack([np.cos(ang), np.sin(ang)]).reshape(2, npy // 2, 2, YL, my)
    a2 = np.zeros((npy // 2, 2, my, XL, 2, XL, YL))
    for x in range(XL):
        a2[:, :, :, x, :, x, :] = cs.transpose(1, 0, 4, 2, 3)
    a2b = a2.transpose(0, 4, 2, 3, 1, 5, 6).reshape(npy, my * XL, 2 * XL * YL)
    a2 = a2.reshape(npy // 2, 2 * my * XL, 2 * XL * YL)
    ang = angles(np.arange(nx), signed(mx, nx), nx)
    cs = np.stack([np.cos(ang), np.sin(ang)])
    tx = cs.transpose(0, 2, 1).reshape(2 * mx, nx) / math.sqrt(nx * ny)
    tix = cs.reshape(2 * nx, mx) / math.sqrt(mx * my)
    ang = angles(np.arange(NZ), np.arange(mz), NZ)
    weight = np.where(np.arange(mz) == 0, 1.0, 2.0) * (8.0 / math.sqrt(NZ * mz))
    inv = np.stack([np.cos(ang), -np.sin(ang)]) * weight
    inv = inv.reshape(2, NZ, npy, K2).transpose(2, 0, 3, 1)
    b7 = np.zeros((npy, 2, 8, K2, 8, NZ))
    for o in range(8):
        b7[:, :, o, :, o, :] = inv
    b7 = b7.reshape(npy * 32, 8 * NZ)
    e8 = np.zeros((2 * C, 8, 2 * C, K2))
    for r in range(8):
        e8[np.arange(2 * C), r, np.arange(2 * C), r % 2] = 1.0
    e8 = e8.reshape(2 * C * 8, 2 * C * K2)

    def half(t):
        return t.astype(np.float32).astype(ml_dtypes.bfloat16)

    def two(t):
        high = half(t)
        return np.stack([high, half(t - high.astype(np.float64))])

    return half(a1), half(a2), half(a2b), two(tx), two(tix), half(b7), half(e8)


def split(value):
    high = value.astype(BF)
    return high, (value - high.astype(F32)).astype(BF)


def dot3(table, value, dims):
    high, low = split(value)
    return dot(table[0], high, dims) + dot(table[0], low, dims) + dot(table[1], high, dims)


def gelu(v):
    k = math.sqrt(2.0 / math.pi)
    half = 0.5 * v
    return half + half * jnp.tanh(v * (k + (k * 0.044715) * (v * v)))


def kernel(
    npx, npy,
    f_ref, a1_ref, win_ref, bin_ref, wout_ref, w_hbm, a2_hbm, a2b_hbm, tx_hbm, tix_hbm, b7_hbm, e8_hbm,
    out_ref,
    zs, send1, recv1, send2, recv2, send3, recv3, ring, lines_y,
    w_ref, a2_ref, a2b_ref, tx_ref, tix_ref, b7_ref, e8_ref,
    k1, k2, bias, chan, xpat,
    ssem1, rsem1, ssem2, rsem2, ssem3, rsem3, ring_on, ring_back, ring_twin, ring_in, tsem,
):
    ny = npy // 2
    mx = w_ref.shape[-1]
    mex = lax.axis_index("px")
    mey = lax.axis_index("py")
    my_chip = mey // 2
    my_core = mey % 2
    twin = my_chip * 2 + 1 - my_core

    loads = [
        pltpu.make_async_copy(src, dst, tsem.at[i])
        for i, (src, dst) in enumerate(
            [(a2_hbm, a2_ref), (tx_hbm, tx_ref), (e8_hbm, e8_ref), (w_hbm, w_ref), (tix_hbm, tix_ref), (b7_hbm, b7_ref),
             (a2b_hbm.at[mey], a2b_ref)]
        )
    ]
    barrier = pltpu.get_barrier_semaphore()

    def greet_y(d, carry):
        pl.semaphore_signal(barrier, inc=1, device_id=(mex, lax.rem(mey + d, npy)), device_id_type=MESH)
        return carry

    def greet_x(d, carry):
        pl.semaphore_signal(barrier, inc=1, device_id=(lax.rem(mex + d, npx), mey), device_id_type=MESH)
        return carry

    lax.fori_loop(1, npy, greet_y, 0)
    lax.fori_loop(1, npx, greet_x, 0)
    for load in loads:
        load.start()

    def forward_z(g, carry):
        f4 = f_ref[pl.ds(g * 4, 4)]
        acc = dot(a1_ref[0], jnp.concatenate([f4[0], f4[1]], axis=1), NT)
        acc = acc + dot(a1_ref[1], jnp.concatenate([f4[2], f4[3]], axis=1), NT)
        zs[:, :, pl.ds(g, 1)] = acc.reshape(npy, 2, 1, 8, 128)
        return carry

    lax.fori_loop(0, C // 4, forward_z, 0, unroll=2)
    send1[...] = zs[...].reshape(npy, 128, 128).astype(BF)

    pl.semaphore_wait(barrier, npx + npy - 2)

    def y_copy(src, dst, ssem, rsem, target):
        return pltpu.make_async_remote_copy(
            src_ref=src.at[target], dst_ref=dst.at[mey], send_sem=ssem.at[target], recv_sem=rsem.at[mey],
            device_id=(mex, target), device_id_type=MESH,
        )

    def y_arrive(src, dst, ssem, rsem, source):
        pltpu.make_async_remote_copy(
            src_ref=src.at[source], dst_ref=dst.at[source], send_sem=ssem.at[source], recv_sem=rsem.at[source],
            device_id=(mex, source), device_id_type=MESH,
        ).wait_recv()

    def x_copy(src, dst, ssem, rsem, target):
        return pltpu.make_async_remote_copy(
            src_ref=src.at[target], dst_ref=dst.at[mex], send_sem=ssem.at[target], recv_sem=rsem.at[mex],
            device_id=(target, mey), device_id_type=MESH,
        )

    def x_exchange(src, dst, ssem, rsem, meanwhile):
        def start(d, carry):
            x_copy(src, dst, ssem, rsem, lax.rem(mex + d, npx)).start()
            return carry

        lax.fori_loop(1, npx, start, 0)
        dst[pl.ds(mex, 1)] = src[pl.ds(mex, 1)]
        channel(meanwhile, 0)

        def arrive(d, carry):
            source = lax.rem(mex + d, npx)
            pltpu.make_async_remote_copy(
                src_ref=src.at[source], dst_ref=dst.at[source], send_sem=ssem.at[source], recv_sem=rsem.at[source],
                device_id=(source, mey), device_id_type=MESH,
            ).wait_recv()
            return carry

        lax.fori_loop(1, npx, arrive, 0)

    def y_peers(far_first):
        offsets = sorted(range(1, ny), key=lambda d: min(d, ny - d), reverse=far_first)
        return [lax.rem(my_chip + d, ny) for d in offsets]

    for chip in y_peers(True):
        for core in range(2):
            y_copy(send1, recv1, ssem1, rsem1, chip * 2 + core).start()
    y_copy(send1, recv1, ssem1, rsem1, twin).start()
    recv1[pl.ds(mey, 1)] = send1[pl.ds(mey, 1)]

    spread = (lax.broadcasted_iota(jnp.int32, (C, C * 8), 1) // 8 == lax.broadcasted_iota(jnp.int32, (C, C * 8), 0))
    rows = dot(win_ref[...], spread.astype(F32).astype(BF), TN)
    same = lax.broadcasted_iota(jnp.int32, (HID, 8, C * 8), 1) == lax.rem(
        lax.broadcasted_iota(jnp.int32, (HID, 8, C * 8), 2), 8
    )
    k1[...] = jnp.where(same, rows[:, None, :], 0.0).reshape(HID * 8, C * 8).astype(BF)
    spread = (
        lax.broadcasted_iota(jnp.int32, (HID, HID * 8), 1) // 8 == lax.broadcasted_iota(jnp.int32, (HID, HID * 8), 0)
    )
    rows = dot(wout_ref[...], spread.astype(F32).astype(BF), NN)
    same = lax.broadcasted_iota(jnp.int32, (C, 8, HID * 8), 1) == lax.rem(
        lax.broadcasted_iota(jnp.int32, (C, 8, HID * 8), 2), 8
    )
    k2[...] = jnp.where(same, rows[:, None, :], 0.0).reshape(C * 8, HID * 8).astype(BF)
    turned = jnp.transpose(jnp.broadcast_to(bin_ref[...], (HID, HID)))
    bias[...] = jnp.broadcast_to(turned[:, None, :], (HID, 8, 128)).reshape(HID * 8, 128)

    def channel(i, carry):
        block = f_ref[:, pl.ds(pl.multiple_of(i * 16, 16), 16), :].astype(F32)
        cells = jnp.concatenate(
            [block[:, :8].reshape(C * 8, 128), block[:, 8:].reshape(C * 8, 128)], axis=1
        ).astype(BF)
        acc = jnp.zeros((C * 8, 256), F32)
        for part in range(4):
            rows = slice(part * 256, part * 256 + 256)
            b = bias[rows]
            hidden = gelu(dot(k1[rows], cells, NN) + jnp.concatenate([b, b], axis=1)).astype(BF)
            acc = acc + dot(k2[:, rows], hidden, NN)
        chan[:, pl.ds(pl.multiple_of(i * 16, 16), 8), :] = acc[:, :128].reshape(C, 8, 128)
        chan[:, pl.ds(pl.multiple_of(i * 16 + 8, 8), 8), :] = acc[:, 128:].reshape(C, 8, 128)
        return carry

    lax.fori_loop(0, 2, channel, 0)

    loads[0].wait()
    lane = lax.broadcasted_iota(jnp.int32, (1, 128), 1)
    sign = jnp.where(lane < 64, 1.0, -1.0)

    def y_part(chip):
        pair = jnp.concatenate([recv1[chip * 2], recv1[chip * 2 + 1]], axis=1)
        return dot(a2_ref[chip], pair, NT)

    y_arrive(send1, recv1, ssem1, rsem1, twin)
    acc = y_part(my_chip)
    for chip in y_peers(False):
        for core in range(2):
            y_arrive(send1, recv1, ssem1, rsem1, chip * 2 + core)
        acc = acc + y_part(chip)
    half = npx * XL
    lines = acc[:half] + sign * pltpu.roll(acc[half:], 64, 1)
    send2[...] = lines.reshape(npx, XL, 128).astype(BF)
    x_exchange(send2, recv2, ssem2, rsem2, 2)

    loads[1].wait()
    loads[2].wait()
    block = recv2[...].astype(F32).reshape(half, 128).astype(BF)
    both = dot(tx_ref[0], block, NN) + dot(tx_ref[1], block, NN)
    spectra = both[:mx] + sign * pltpu.roll(both[mx:], 64, 1)
    high, low = split(spectra)
    xpat[...] = (dot(e8_ref[...], high, NT) + dot(e8_ref[...], low, NT)).reshape(2 * C, 8, mx)

    loads[3].wait()

    def mix(c, carry):
        real, imag = carry
        wr = w_ref[0, c].astype(F32).reshape(8, 8, mx)
        wi = w_ref[1, c].astype(F32).reshape(8, 8, mx)
        xr = xpat[c][None]
        xi = xpat[c + C][None]
        return real + xr * wr - xi * wi, imag + xr * wi + xi * wr

    zero = jnp.zeros((8, 8, mx), F32)
    real, imag = lax.fori_loop(0, C, mix, (zero, zero), unroll=4)
    modes = jnp.concatenate([real.reshape(64, mx), imag.reshape(64, mx)], axis=0)

    loads[4].wait()
    both = dot3(tix_ref, modes, NT)
    cells = both[:half] - sign * pltpu.roll(both[half:], 64, 1)
    send3[...] = cells.reshape(npx, XL, 128).astype(BF)
    x_exchange(send3, recv3, ssem3, rsem3, 3)

    block = jnp.transpose(recv3[...].astype(F32).reshape(half, 128)).astype(BF)
    ring[pl.ds(mey, 1)] = block.reshape(1, 2, 64, half)
    right = lax.rem(my_chip + 1, ny) * 2 + my_core
    left = lax.rem(my_chip + ny - 1, ny) * 2 + my_core

    def ring_copy(p, q, sem, target):
        return pltpu.make_async_remote_copy(
            src_ref=ring.at[p, q], dst_ref=ring.at[p, q], send_sem=sem.at[p, q], recv_sem=ring_in.at[p, q],
            device_id=(mex, target), device_id_type=MESH,
        )

    def cells_back(p):
        both = dot(ring[p].reshape(128, half), a2b_ref[...], NN)
        real = both[:64, :128] - both[64:, 128:]
        imag = both[64:, :128] + both[:64, 128:]
        lines_y[pl.ds(p, 1)] = jnp.concatenate([real, imag], axis=0).astype(BF)[None]

    reach = {("right", 0): ny // 2, ("left", 1): ny // 2, ("right", 1): (ny - 1) // 2, ("left", 0): (ny - 1) // 2}
    order = [("right", 0), ("left", 1), ("right", 1), ("left", 0)]
    sends = []

    def go(p, q, sem, target):
        copy = ring_copy(p, q, sem, target)
        copy.start()
        sends.append(copy)

    for way, q in order:
        if reach[way, q] >= 1:
            go(mey, q, ring_on if way == "right" else ring_back, right if way == "right" else left)
    for q in range(2):
        go(mey, q, ring_twin, twin)
    loads[6].wait()
    cells_back(mey)
    done = 4
    for k in range(1, ny // 2 + 1):
        behind = lax.rem(my_chip + ny - k, ny) * 2
        ahead = lax.rem(my_chip + k, ny) * 2
        for way, q in order:
            if k <= reach[way, q]:
                p = (behind if way == "right" else ahead) + my_core
                ring_copy(p, q, ring_on, twin).wait_recv()
                if k < reach[way, q]:
                    go(p, q, ring_on, right if way == "right" else left)
                go(p, q, ring_twin, twin)
        if done < 8:
            channel(done, 0)
            done += 1
        cells_back(behind + my_core)
        if 2 * k < ny:
            cells_back(ahead + my_core)
    for more in range(done, 8):
        channel(more, 0)
    for k in range(ny // 2 + 1):
        for p in sorted({k, (ny - k) % ny}):
            p = lax.rem(my_chip + p, ny) * 2 + 1 - my_core
            for q in range(2):
                ring_copy(p, q, ring_on, twin).wait_recv()
            cells_back(p)

    loads[5].wait()
    for g in range(4):
        lines = jnp.concatenate(
            [lines_y[:, 16 * g : 16 * g + 16, :].reshape(npy, 1, 16, 128),
             lines_y[:, 64 + 16 * g : 80 + 16 * g, :].reshape(npy, 1, 16, 128)], axis=1
        ).reshape(npy * 32, 128)
        values = dot(lines, b7_ref[...], TN)
        for o in range(8):
            total = values[:, 128 * o : 128 * o + 128] + chan[8 * g + o]
            out_ref[8 * g + o] = gelu(total).astype(BF)

    def sent_y(d, carry):
        target = lax.rem(mey + d, npy)
        y_copy(send1, recv1, ssem1, rsem1, target).wait_send()
        return carry

    def sent_x(d, carry):
        target = lax.rem(mex + d, npx)
        x_copy(send2, recv2, ssem2, rsem2, target).wait_send()
        x_copy(send3, recv3, ssem3, rsem3, target).wait_send()
        return carry

    lax.fori_loop(1, npy, sent_y, 0)
    lax.fori_loop(1, npx, sent_x, 0)
    for copy in sends:
        copy.wait_send()


def body(npx, npy, field, spec_weight, w_in, b_in, w_out):
    mx = spec_weight.shape[4]
    a1, a2, a2b, tx, tix, b7, e8 = tables(npx, npy, mx)
    cells = field.reshape(C, XL * YL, NZ)
    weight = jnp.transpose(spec_weight[0], (0, 1, 2, 4, 5, 3)).reshape(2, C, C * K2, mx)
    vmem = pl.BlockSpec(memory_space=pltpu.VMEM)
    anywhere = pl.BlockSpec(memory_space=pl.ANY)
    out = pl.pallas_call(
        functools.partial(kernel, npx, npy),
        out_shape=jax.ShapeDtypeStruct((C, XL * YL, NZ), BF),
        in_specs=[vmem] * 5 + [anywhere] * 7,
        out_specs=vmem,
        scratch_shapes=[
            pltpu.VMEM((npy, 2, 8, 8, 128), F32),
            pltpu.VMEM((npy, 128, 128), BF),
            pltpu.VMEM((npy, 128, 128), BF),
            pltpu.VMEM((npx, XL, 128), BF),
            pltpu.VMEM((npx, XL, 128), BF),
            pltpu.VMEM((npx, XL, 128), BF),
            pltpu.VMEM((npx, XL, 128), BF),
            pltpu.VMEM((npy, 2, 64, npx * XL), BF),
            pltpu.VMEM((npy, 128, 128), BF),
            pltpu.VMEM(weight.shape, BF),
            pltpu.VMEM(a2.shape, BF),
            pltpu.VMEM(a2b.shape[1:], BF),
            pltpu.VMEM(tx.shape, BF),
            pltpu.VMEM(tix.shape, BF),
            pltpu.VMEM(b7.shape, BF),
            pltpu.VMEM(e8.shape, BF),
            pltpu.VMEM((HID * 8, C * 8), BF),
            pltpu.VMEM((C * 8, HID * 8), BF),
            pltpu.VMEM((HID * 8, 128), F32),
            pltpu.VMEM((C, XL * YL, NZ), F32),
            pltpu.VMEM((2 * C, 8, mx), F32),
            pltpu.SemaphoreType.DMA((npy,)),
            pltpu.SemaphoreType.DMA((npy,)),
            pltpu.SemaphoreType.DMA((npx,)),
            pltpu.SemaphoreType.DMA((npx,)),
            pltpu.SemaphoreType.DMA((npx,)),
            pltpu.SemaphoreType.DMA((npx,)),
            pltpu.SemaphoreType.DMA((npy, 2)),
            pltpu.SemaphoreType.DMA((npy, 2)),
            pltpu.SemaphoreType.DMA((npy, 2)),
            pltpu.SemaphoreType.DMA((npy, 2)),
            pltpu.SemaphoreType.DMA((7,)),
        ],
        compiler_params=pltpu.CompilerParams(
            collective_id=0, has_side_effects=True, vmem_limit_bytes=60 * 1024 * 1024
        ),
    )(
        cells, jnp.asarray(a1), w_in[0], b_in, jnp.transpose(w_out[0]), weight,
        jnp.asarray(a2), jnp.asarray(a2b), jnp.asarray(tx), jnp.asarray(tix), jnp.asarray(b7), jnp.asarray(e8),
    )
    return out.reshape(field.shape)


def solution(mesh):
    in_specs = (
        P(None, "px", "py", None),
        P(None, None, None, None, None, "px", "py"),
        P(),
        P(),
        P(),
    )
    return jax.shard_map(
        functools.partial(body, mesh.shape["px"], mesh.shape["py"]),
        mesh=mesh, in_specs=in_specs, out_specs=P(None, "px", "py", None), check_vma=False,
    )
```

```python
import functools
import math

import jax
import jax.numpy as jnp
import ml_dtypes
import numpy as np
from jax import lax
from jax.experimental import pallas as pl
from jax.experimental.pallas import tpu as pltpu
from jax.sharding import PartitionSpec as P

MESH = pl.DeviceIdType.MESH
BF = jnp.bfloat16
F32 = jnp.float32
C = 32
HID = 128
XL = 8
YL = 16
NZ = 128
K2 = 2
NT = (((1,), (1,)), ((), ()))
NN = (((1,), (0,)), ((), ()))
TN = (((0,), (0,)), ((), ()))


def chips(npx):
    zc = max(npx // 4, min(npx, 2))
    return npx // zc, zc


def dot(a, b, dims):
    return lax.dot_general(a, b, dims, preferred_element_type=F32)


def signed(count, length):
    index = np.arange(count)
    return np.where(index < count // 2, index, index - count + length)


def angles(positions, freqs, length):
    return 2.0 * math.pi * ((positions[:, None] * freqs[None, :]) % length) / length


def tables(npx, npy, mx):
    nx, ny, my, mz = XL * npx, YL * npy, npx, K2 * npy
    ang = angles(np.arange(NZ), np.arange(mz), NZ)
    fwd = np.stack([np.cos(ang), -np.sin(ang)]) * 0.125
    fwd = fwd.reshape(2, NZ, npy, K2).transpose(2, 0, 3, 1)
    a1 = np.zeros((2, npy, 2, 4, K2, 2, NZ))
    for q in range(2):
        for c in range(2):
            a1[q, :, :, 2 * q + c, :, c, :] = fwd
    a1 = a1.reshape(2, npy * 16, 2 * NZ)
    ang = angles(np.arange(ny), signed(my, ny), ny)
    cs = np.stack([np.cos(ang), np.sin(ang)]).reshape(2, npy // 2, 2, YL, my)
    a2 = np.zeros((npy // 2, 2, my, XL, 2, XL, YL))
    for x in range(XL):
        a2[:, :, :, x, :, x, :] = cs.transpose(1, 0, 4, 2, 3)
    a2 = a2.reshape(npy // 2, 2 * my * XL, 2 * XL * YL)
    ang = angles(np.arange(nx), signed(mx, nx), nx)
    cs = np.stack([np.cos(ang), np.sin(ang)])
    tx = cs.transpose(0, 2, 1).reshape(2 * mx, nx) / math.sqrt(nx * ny)
    tix = cs.reshape(2 * nx, mx) / math.sqrt(mx * my)
    ang = angles(np.arange(NZ), np.arange(mz), NZ)
    weight = np.where(np.arange(mz) == 0, 1.0, 2.0) * (8.0 / math.sqrt(NZ * mz))
    inv = np.stack([np.cos(ang), -np.sin(ang)]) * weight
    inv = inv.reshape(2, NZ, npy, K2).transpose(2, 0, 3, 1)
    b7 = np.zeros((npy, 2, 8, K2, 8, NZ))
    for o in range(8):
        b7[:, :, o, :, o, :] = inv
    b7 = b7.reshape(npy * 32, 8 * NZ)
    e8 = np.zeros((2 * C, 8, 2 * C, K2))
    for r in range(8):
        e8[np.arange(2 * C), r, np.arange(2 * C), r % 2] = 1.0
    e8 = e8.reshape(2 * C * 8, 2 * C * K2)

    def half(t):
        return t.astype(np.float32).astype(ml_dtypes.bfloat16)

    def two(t):
        high = half(t)
        return np.stack([high, half(t - high.astype(np.float64))])

    return half(a1), half(a2), two(tx), two(tix), half(b7), half(e8)


def split(value):
    high = value.astype(BF)
    return high, (value - high.astype(F32)).astype(BF)


def dot3(table, value, dims):
    high, low = split(value)
    return dot(table[0], high, dims) + dot(table[0], low, dims) + dot(table[1], high, dims)


def gelu(v):
    k = math.sqrt(2.0 / math.pi)
    half = 0.5 * v
    return half + half * jnp.tanh(v * (k + (k * 0.044715) * (v * v)))


def kernel(
    npx, npy,
    f_hbm, a1_hbm, win_hbm, bin_hbm, wout_hbm, w_hbm, a2_hbm, tx_hbm, tix_hbm, e8_hbm,
    recv4, chan,
    zs, send1, recv1, send2, mid2, recv2, send3, mid3, recv3, send4,
    f_ref, a1_ref, win_ref, bin_ref, wout_ref, w_ref, a2_ref, tx_ref, tix_ref, e8_ref,
    k1, k2, bias, xpat,
    ssem1, rsem1, sems2, sems3, ssem4, rsem4, tsem,
):
    ny = npy // 2
    mx = w_ref.shape[-1]
    xc, zc = chips(npx)
    sent = []
    mex = lax.axis_index("px")
    mey = lax.axis_index("py")
    my_chip = mey // 2
    my_core = mey % 2
    twin = my_chip * 2 + 1 - my_core
    mex_x = mex // zc
    mex_z = mex % zc

    def load(i, src, dst):
        return pltpu.make_async_copy(src, dst, tsem.at[i])

    cells_in = [load(0, a1_hbm, a1_ref)] + [
        load(1 + i, f_hbm.at[pl.ds(i * 8, 8)], f_ref.at[pl.ds(i * 8, 8)]) for i in range(4)
    ]
    pairs = [(win_hbm, win_ref), (bin_hbm, bin_ref), (wout_hbm, wout_ref), (a2_hbm, a2_ref), (tx_hbm, tx_ref),
             (e8_hbm, e8_ref), (w_hbm, w_ref), (tix_hbm, tix_ref)]
    loads = [load(5 + i, src, dst) for i, (src, dst) in enumerate(pairs)]
    barrier = pltpu.get_barrier_semaphore()

    def greet_y(d, carry):
        pl.semaphore_signal(barrier, inc=1, device_id=(mex, lax.rem(mey + d, npy)), device_id_type=MESH)
        return carry

    for load in cells_in + loads:
        load.start()
    lax.fori_loop(1, npy, greet_y, 0)
    for d in range(1, zc):
        pl.semaphore_signal(
            barrier, inc=1, device_id=(mex_x * zc + lax.rem(mex_z + d, zc), mey), device_id_type=MESH
        )
    for d in range(1, xc):
        pl.semaphore_signal(
            barrier, inc=1, device_id=(lax.rem(mex_x + d, xc) * zc + mex_z, mey), device_id_type=MESH
        )

    def forward_z(g, carry):
        f4 = f_ref[pl.ds(g * 4, 4)]
        acc = dot(a1_ref[0], jnp.concatenate([f4[0], f4[1]], axis=1), NT)
        acc = acc + dot(a1_ref[1], jnp.concatenate([f4[2], f4[3]], axis=1), NT)
        zs[:, :, pl.ds(g, 1)] = acc.reshape(npy, 2, 1, 8, 128)
        return carry

    cells_in[0].wait()
    for i in range(4):
        cells_in[1 + i].wait()
        lax.fori_loop(2 * i, 2 * i + 2, forward_z, 0, unroll=2)
    send1[...] = zs[...].reshape(npy, 128, 128).astype(BF)

    pl.semaphore_wait(barrier, npy + zc + xc - 3)

    def y_copy(src, dst, ssem, rsem, target):
        return pltpu.make_async_remote_copy(
            src_ref=src.at[target], dst_ref=dst.at[mey], send_sem=ssem.at[target], recv_sem=rsem.at[mey],
            device_id=(mex, target), device_id_type=MESH,
        )

    def y_arrive(src, dst, ssem, rsem, source):
        pltpu.make_async_remote_copy(
            src_ref=src.at[source], dst_ref=dst.at[source], send_sem=ssem.at[source], recv_sem=rsem.at[source],
            device_id=(mex, source), device_id_type=MESH,
        ).wait_recv()

    def x_exchange(src, mid, dst, sems):
        def hop(first, target, slot):
            if first:
                return pltpu.make_async_remote_copy(
                    src_ref=src.at[:, target], dst_ref=mid.at[:, slot], send_sem=sems.at[0, target],
                    recv_sem=sems.at[1, slot], device_id=(mex_x * zc + target, mey), device_id_type=MESH,
                )
            return pltpu.make_async_remote_copy(
                src_ref=mid.at[target], dst_ref=dst.at[slot], send_sem=sems.at[2, target],
                recv_sem=sems.at[3, slot], device_id=(target * zc + mex_z, mey), device_id_type=MESH,
            )

        for first, own, count in ((True, mex_z, zc), (False, mex_x, xc)):
            others = [lax.rem(own + d, count) for d in sorted(range(1, count), key=lambda d: -min(d, count - d))]
            for other in others:
                hop(first, other, own).start()
            if first:
                mid[:, pl.ds(own, 1)] = src[:, pl.ds(own, 1)]
            else:
                dst[pl.ds(own, 1)] = mid[pl.ds(own, 1)]
            for other in others:
                hop(first, other, other).wait_recv()
            for other in others:
                sent.append(hop(first, other, own))

    def y_peers(far_first):
        offsets = sorted(range(1, ny), key=lambda d: min(d, ny - d), reverse=far_first)
        return [lax.rem(my_chip + d, ny) for d in offsets]

    for chip in y_peers(True):
        for core in range(2):
            y_copy(send1, recv1, ssem1, rsem1, chip * 2 + core).start()
    y_copy(send1, recv1, ssem1, rsem1, twin).start()
    recv1[pl.ds(mey, 1)] = send1[pl.ds(mey, 1)]

    for i in range(3):
        loads[i].wait()
    spread = (lax.broadcasted_iota(jnp.int32, (C, C * 8), 1) >> 3 == lax.broadcasted_iota(jnp.int32, (C, C * 8), 0))
    rows = dot(win_ref[...], spread.astype(F32).astype(BF), TN)
    same = lax.broadcasted_iota(jnp.int32, (HID, 8, C * 8), 1) == (
        lax.broadcasted_iota(jnp.int32, (HID, 8, C * 8), 2) & 7
    )
    k1[...] = jnp.where(same, rows[:, None, :], 0.0).reshape(HID * 8, C * 8).astype(BF)
    spread = (
        lax.broadcasted_iota(jnp.int32, (HID, HID * 8), 1) >> 3 == lax.broadcasted_iota(jnp.int32, (HID, HID * 8), 0)
    )
    rows = dot(wout_ref[...], spread.astype(F32).astype(BF), NN)
    same = lax.broadcasted_iota(jnp.int32, (C, 8, HID * 8), 1) == (
        lax.broadcasted_iota(jnp.int32, (C, 8, HID * 8), 2) & 7
    )
    k2[...] = jnp.where(same, rows[:, None, :], 0.0).reshape(C * 8, HID * 8).astype(BF)
    turned = jnp.transpose(jnp.broadcast_to(bin_ref[...], (HID, HID)))
    bias[...] = jnp.broadcast_to(turned[:, None, :], (HID, 8, 128)).reshape(HID * 8, 128)

    def channel(i, carry):
        block = f_ref[:, pl.ds(pl.multiple_of(i * 16, 16), 16), :].astype(F32)
        cells = jnp.concatenate(
            [block[:, :8].reshape(C * 8, 128), block[:, 8:].reshape(C * 8, 128)], axis=1
        ).astype(BF)
        acc = jnp.zeros((C * 8, 256), F32)
        for part in range(4):
            rows = slice(part * 256, part * 256 + 256)
            b = bias[rows]
            hidden = gelu(dot(k1[rows], cells, NN) + jnp.concatenate([b, b], axis=1)).astype(BF)
            acc = acc + dot(k2[:, rows], hidden, NN)
        chan[:, pl.ds(pl.multiple_of(i * 16, 16), 8), :] = acc[:, :128].reshape(C, 8, 128)
        chan[:, pl.ds(pl.multiple_of(i * 16 + 8, 8), 8), :] = acc[:, 128:].reshape(C, 8, 128)
        return carry

    lax.fori_loop(0, 4, channel, 0)

    loads[3].wait()
    lane = lax.broadcasted_iota(jnp.int32, (1, 128), 1)
    sign = jnp.where(lane < 64, 1.0, -1.0)

    def y_part(chip):
        pair = jnp.concatenate([recv1[chip * 2], recv1[chip * 2 + 1]], axis=1)
        return dot(a2_ref[chip], pair, NT)

    y_arrive(send1, recv1, ssem1, rsem1, twin)
    acc = y_part(my_chip)
    for chip in y_peers(False):
        for core in range(2):
            y_arrive(send1, recv1, ssem1, rsem1, chip * 2 + core)
        acc = acc + y_part(chip)
    half = npx * XL
    lines = acc[:half] + sign * pltpu.roll(acc[half:], 64, 1)
    send2[...] = lines.reshape(xc, zc, XL, 128).astype(BF)
    x_exchange(send2, mid2, recv2, sems2)

    loads[4].wait()
    loads[5].wait()
    block = recv2[...].astype(F32).reshape(half, 128).astype(BF)
    both = dot(tx_ref[0], block, NN) + dot(tx_ref[1], block, NN)
    spectra = both[:mx] + sign * pltpu.roll(both[mx:], 64, 1)
    high, low = split(spectra)
    xpat[...] = (dot(e8_ref[...], high, NT) + dot(e8_ref[...], low, NT)).reshape(2 * C, 8, mx)

    loads[6].wait()

    def mix(c, carry):
        real, imag = carry
        wr = w_ref[0, c].astype(F32).reshape(8, 8, mx)
        wi = w_ref[1, c].astype(F32).reshape(8, 8, mx)
        xr = xpat[c][None]
        xi = xpat[c + C][None]
        return real + xr * wr - xi * wi, imag + xr * wi + xi * wr

    zero = jnp.zeros((8, 8, mx), F32)
    real, imag = lax.fori_loop(0, C, mix, (zero, zero), unroll=4)
    modes = jnp.concatenate([real.reshape(64, mx), imag.reshape(64, mx)], axis=0)

    loads[7].wait()
    both = dot3(tix_ref, modes, NT)
    cells = both[:half] - sign * pltpu.roll(both[half:], 64, 1)
    send3[...] = cells.reshape(xc, zc, XL, 128).astype(BF)
    x_exchange(send3, mid3, recv3, sems3)

    block = recv3[...].astype(F32).reshape(half, 128)
    turned = jnp.concatenate([block, -sign * pltpu.roll(block, 64, 1)], axis=0)
    turned = jnp.transpose(turned).astype(BF)

    def y_back(chip):
        both = dot(turned, a2_ref[chip], NN).astype(BF)
        send4[pl.ds(chip * 2, 1)] = both[:, :128][None]
        send4[pl.ds(chip * 2 + 1, 1)] = both[:, 128:][None]

    for chip in y_peers(True):
        y_back(chip)
        for core in range(2):
            y_copy(send4, recv4, ssem4, rsem4, chip * 2 + core).start()
    y_back(my_chip)
    y_copy(send4, recv4, ssem4, rsem4, twin).start()
    recv4[pl.ds(mey, 1)] = send4[pl.ds(mey, 1)]

    lax.fori_loop(4, 8, channel, 0)

    y_arrive(send4, recv4, ssem4, rsem4, twin)
    for chip in y_peers(False):
        for core in range(2):
            y_arrive(send4, recv4, ssem4, rsem4, chip * 2 + core)

    def sent_y(d, carry):
        target = lax.rem(mey + d, npy)
        y_copy(send1, recv1, ssem1, rsem1, target).wait_send()
        y_copy(send4, recv4, ssem4, rsem4, target).wait_send()
        return carry

    lax.fori_loop(1, npy, sent_y, 0)
    for copy in sent:
        copy.wait_send()


def finish(npy, recv4, chan, b7_ref, out_hbm, done, sems):
    copies = []
    for g in range(4):
        lines = jnp.concatenate(
            [recv4[:, 16 * g : 16 * g + 16, :].reshape(npy, 1, 16, 128),
             recv4[:, 64 + 16 * g : 80 + 16 * g, :].reshape(npy, 1, 16, 128)], axis=1
        ).reshape(npy * 32, 128)
        values = dot(lines, b7_ref[...], TN)
        for o in range(8):
            total = values[:, 128 * o : 128 * o + 128] + chan[8 * g + o]
            done[8 * g + o] = gelu(total).astype(BF)
        block = pl.ds(8 * g, 8)
        copies.append(pltpu.make_async_copy(done.at[block], out_hbm.at[block], sems.at[g]))
        copies[-1].start()
    for copy in copies:
        copy.wait()


def body(npx, npy, field, spec_weight, w_in, b_in, w_out):
    mx = spec_weight.shape[4]
    a1, a2, tx, tix, b7, e8 = tables(npx, npy, mx)
    cells = field.reshape(C, XL * YL, NZ)
    weight = jnp.transpose(spec_weight[0], (0, 1, 2, 4, 5, 3)).reshape(2, C, C * K2, mx)
    vmem = pl.BlockSpec(memory_space=pltpu.VMEM)
    hbm = pl.BlockSpec(memory_space=pltpu.HBM)
    xc, zc = chips(npx)
    exchange = [pltpu.VMEM((xc, zc, XL, 128), BF)] * 3
    loaded = [
        cells, jnp.asarray(a1), w_in[0], b_in, jnp.transpose(w_out[0]), weight,
        jnp.asarray(a2), jnp.asarray(tx), jnp.asarray(tix), jnp.asarray(e8),
    ]
    loaded = [pltpu.with_memory_space_constraint(a, pltpu.HBM) for a in loaded]
    lines, chan = pl.pallas_call(
        functools.partial(kernel, npx, npy),
        out_shape=(
            pltpu.VMEM((npy, 128, 128), BF),
            pltpu.VMEM((C, XL * YL, NZ), F32),
        ),
        in_specs=[hbm] * len(loaded),
        out_specs=(vmem, vmem),
        scratch_shapes=[
            pltpu.VMEM((npy, 2, 8, 8, 128), F32),
            pltpu.VMEM((npy, 128, 128), BF),
            pltpu.VMEM((npy, 128, 128), BF),
            *exchange,
            *exchange,
            pltpu.VMEM((npy, 128, 128), BF),
            *[pltpu.VMEM(a.shape, a.dtype) for a in loaded],
            pltpu.VMEM((HID * 8, C * 8), BF),
            pltpu.VMEM((C * 8, HID * 8), BF),
            pltpu.VMEM((HID * 8, 128), F32),
            pltpu.VMEM((2 * C, 8, mx), F32),
            pltpu.SemaphoreType.DMA((npy,)),
            pltpu.SemaphoreType.DMA((npy,)),
            pltpu.SemaphoreType.DMA((4, max(xc, zc))),
            pltpu.SemaphoreType.DMA((4, max(xc, zc))),
            pltpu.SemaphoreType.DMA((npy,)),
            pltpu.SemaphoreType.DMA((npy,)),
            pltpu.SemaphoreType.DMA((13,)),
        ],
        compiler_params=pltpu.CompilerParams(
            collective_id=0, has_side_effects=True, vmem_limit_bytes=32 * 1024 * 1024
        ),
    )(*loaded)
    out = pl.pallas_call(
        functools.partial(finish, npy),
        out_shape=jax.ShapeDtypeStruct((C, XL * YL, NZ), BF),
        in_specs=[vmem] * 3,
        out_specs=hbm,
        scratch_shapes=[pltpu.VMEM((C, XL * YL, NZ), BF), pltpu.SemaphoreType.DMA((4,))],
        compiler_params=pltpu.CompilerParams(vmem_limit_bytes=16 * 1024 * 1024),
    )(lines, chan, jnp.asarray(b7))
    return out.reshape(field.shape)


def solution(mesh):
    in_specs = (
        P(None, "px", "py", None),
        P(None, None, None, None, None, "px", "py"),
        P(),
        P(),
        P(),
    )
    return jax.shard_map(
        functools.partial(body, mesh.shape["px"], mesh.shape["py"]),
        mesh=mesh, in_specs=in_specs, out_specs=P(None, "px", "py", None), check_vma=False,
    )
```

```python
import functools
import math

import jax
import jax.numpy as jnp
import ml_dtypes
import numpy as np
from jax import lax
from jax.experimental import pallas as pl
from jax.experimental.pallas import tpu as pltpu
from jax.sharding import PartitionSpec as P

MESH = pl.DeviceIdType.MESH
BF = jnp.bfloat16
F32 = jnp.float32
C = 32
HID = 128
XL = 8
YL = 16
NZ = 128
K2 = 2
NT = (((1,), (1,)), ((), ()))
NN = (((1,), (0,)), ((), ()))
TN = (((0,), (0,)), ((), ()))


def chips(npx):
    zc = max(npx // 4, min(npx, 2))
    return npx // zc, zc


def dot(a, b, dims):
    return lax.dot_general(a, b, dims, preferred_element_type=F32)


def signed(count, length):
    index = np.arange(count)
    return np.where(index < count // 2, index, index - count + length)


def angles(positions, freqs, length):
    return 2.0 * math.pi * ((positions[:, None] * freqs[None, :]) % length) / length


def tables(npx, npy, mx):
    nx, ny, my, mz = XL * npx, YL * npy, npx, K2 * npy
    ang = angles(np.arange(NZ), np.arange(mz), NZ)
    fwd = np.stack([np.cos(ang), -np.sin(ang)]) * 0.125
    fwd = fwd.reshape(2, NZ, npy, K2).transpose(2, 0, 3, 1)
    a1 = np.zeros((2, npy, 2, 4, K2, 2, NZ))
    for q in range(2):
        for c in range(2):
            a1[q, :, :, 2 * q + c, :, c, :] = fwd
    a1 = a1.reshape(2, npy * 16, 2 * NZ)
    ang = angles(np.arange(ny), signed(my, ny), ny)
    cs = np.stack([np.cos(ang), np.sin(ang)]).reshape(2, npy // 2, 2, YL, my)
    a2 = np.zeros((npy // 2, 2, my, XL, 2, XL, YL))
    for x in range(XL):
        a2[:, :, :, x, :, x, :] = cs.transpose(1, 0, 4, 2, 3)
    a2b = a2.transpose(0, 4, 2, 3, 1, 5, 6).reshape(npy, my * XL, 2 * XL * YL)
    a2 = a2.reshape(npy // 2, 2 * my * XL, 2 * XL * YL)
    ang = angles(np.arange(nx), signed(mx, nx), nx)
    cs = np.stack([np.cos(ang), np.sin(ang)])
    tx = cs.transpose(0, 2, 1).reshape(2 * mx, nx) / math.sqrt(nx * ny)
    tix = cs.reshape(2 * nx, mx) / math.sqrt(mx * my)
    ang = angles(np.arange(NZ), np.arange(mz), NZ)
    weight = np.where(np.arange(mz) == 0, 1.0, 2.0) * (8.0 / math.sqrt(NZ * mz))
    inv = np.stack([np.cos(ang), -np.sin(ang)]) * weight
    inv = inv.reshape(2, NZ, npy, K2).transpose(2, 0, 3, 1)
    b7 = np.zeros((npy, 2, 8, K2, 8, NZ))
    for o in range(8):
        b7[:, :, o, :, o, :] = inv
    b7 = b7.reshape(npy * 32, 8 * NZ)
    e8 = np.zeros((2 * C, 8, 2 * C, K2))
    for r in range(8):
        e8[np.arange(2 * C), r, np.arange(2 * C), r % 2] = 1.0
    e8 = e8.reshape(2 * C * 8, 2 * C * K2)

    def half(t):
        return t.astype(np.float32).astype(ml_dtypes.bfloat16)

    def two(t):
        high = half(t)
        return np.stack([high, half(t - high.astype(np.float64))])

    return half(a1), half(a2), half(a2b), two(tx), two(tix), half(b7), half(e8)


def split(value):
    high = value.astype(BF)
    return high, (value - high.astype(F32)).astype(BF)


def dot3(table, value, dims):
    high, low = split(value)
    return dot(table[0], high, dims) + dot(table[0], low, dims) + dot(table[1], high, dims)


def gelu(v):
    k = math.sqrt(2.0 / math.pi)
    half = 0.5 * v
    return half + half * jnp.tanh(v * (k + (k * 0.044715) * (v * v)))


def kernel(
    npx, npy,
    f_hbm, a1_hbm, win_hbm, bin_hbm, wout_hbm, w_hbm, a2_hbm, tx_hbm, tix_hbm, e8_hbm, a2b_hbm,
    lines_y, chan,
    zs, send1, recv1, send2, mid2, recv2, send3, mid3, recv3, ring,
    f_ref, a1_ref, win_ref, bin_ref, wout_ref, w_ref, a2_ref, tx_ref, tix_ref, e8_ref, a2b_ref,
    k1, k2, bias, xpat,
    ssem1, rsem1, sems2, sems3, ring_on, ring_back, ring_twin, ring_in, tsem,
):
    ny = npy // 2
    mx = w_ref.shape[-1]
    xc, zc = chips(npx)
    sent = []
    mex = lax.axis_index("px")
    mey = lax.axis_index("py")
    my_chip = mey // 2
    my_core = mey % 2
    twin = my_chip * 2 + 1 - my_core
    mex_x = mex // zc
    mex_z = mex % zc

    def load(i, src, dst):
        return pltpu.make_async_copy(src, dst, tsem.at[i])

    cells_in = [load(0, a1_hbm, a1_ref)] + [
        load(1 + i, f_hbm.at[pl.ds(i * 8, 8)], f_ref.at[pl.ds(i * 8, 8)]) for i in range(4)
    ]
    pairs = [(win_hbm, win_ref), (bin_hbm, bin_ref), (wout_hbm, wout_ref), (a2_hbm, a2_ref), (tx_hbm, tx_ref),
             (e8_hbm, e8_ref), (w_hbm, w_ref), (tix_hbm, tix_ref), (a2b_hbm.at[mey], a2b_ref)]
    loads = [load(5 + i, src, dst) for i, (src, dst) in enumerate(pairs)]
    barrier = pltpu.get_barrier_semaphore()

    def greet_y(d, carry):
        pl.semaphore_signal(barrier, inc=1, device_id=(mex, lax.rem(mey + d, npy)), device_id_type=MESH)
        return carry

    for load in cells_in + loads:
        load.start()
    lax.fori_loop(1, npy, greet_y, 0)
    for d in range(1, zc):
        pl.semaphore_signal(
            barrier, inc=1, device_id=(mex_x * zc + lax.rem(mex_z + d, zc), mey), device_id_type=MESH
        )
    for d in range(1, xc):
        pl.semaphore_signal(
            barrier, inc=1, device_id=(lax.rem(mex_x + d, xc) * zc + mex_z, mey), device_id_type=MESH
        )

    def forward_z(g, carry):
        f4 = f_ref[pl.ds(g * 4, 4)]
        acc = dot(a1_ref[0], jnp.concatenate([f4[0], f4[1]], axis=1), NT)
        acc = acc + dot(a1_ref[1], jnp.concatenate([f4[2], f4[3]], axis=1), NT)
        zs[:, :, pl.ds(g, 1)] = acc.reshape(npy, 2, 1, 8, 128)
        return carry

    cells_in[0].wait()
    for i in range(4):
        cells_in[1 + i].wait()
        lax.fori_loop(2 * i, 2 * i + 2, forward_z, 0, unroll=2)
    send1[...] = zs[...].reshape(npy, 128, 128).astype(BF)

    pl.semaphore_wait(barrier, npy + zc + xc - 3)

    def y_copy(src, dst, ssem, rsem, target):
        return pltpu.make_async_remote_copy(
            src_ref=src.at[target], dst_ref=dst.at[mey], send_sem=ssem.at[target], recv_sem=rsem.at[mey],
            device_id=(mex, target), device_id_type=MESH,
        )

    def y_arrive(src, dst, ssem, rsem, source):
        pltpu.make_async_remote_copy(
            src_ref=src.at[source], dst_ref=dst.at[source], send_sem=ssem.at[source], recv_sem=rsem.at[source],
            device_id=(mex, source), device_id_type=MESH,
        ).wait_recv()

    def x_exchange(src, mid, dst, sems, meanwhile):
        def hop(first, target, slot):
            if first:
                return pltpu.make_async_remote_copy(
                    src_ref=src.at[:, target], dst_ref=mid.at[:, slot], send_sem=sems.at[0, target],
                    recv_sem=sems.at[1, slot], device_id=(mex_x * zc + target, mey), device_id_type=MESH,
                )
            return pltpu.make_async_remote_copy(
                src_ref=mid.at[target], dst_ref=dst.at[slot], send_sem=sems.at[2, target],
                recv_sem=sems.at[3, slot], device_id=(target * zc + mex_z, mey), device_id_type=MESH,
            )

        for first, own, count in ((True, mex_z, zc), (False, mex_x, xc)):
            others = [lax.rem(own + d, count) for d in sorted(range(1, count), key=lambda d: -min(d, count - d))]
            for other in others:
                hop(first, other, own).start()
            if first:
                mid[:, pl.ds(own, 1)] = src[:, pl.ds(own, 1)]
            else:
                dst[pl.ds(own, 1)] = mid[pl.ds(own, 1)]
            channel(meanwhile if first else meanwhile + 1, 0)
            for other in others:
                hop(first, other, other).wait_recv()
            for other in others:
                sent.append(hop(first, other, own))

    def y_peers(far_first):
        offsets = sorted(range(1, ny), key=lambda d: min(d, ny - d), reverse=far_first)
        return [lax.rem(my_chip + d, ny) for d in offsets]

    for chip in y_peers(True):
        for core in range(2):
            y_copy(send1, recv1, ssem1, rsem1, chip * 2 + core).start()
    y_copy(send1, recv1, ssem1, rsem1, twin).start()
    recv1[pl.ds(mey, 1)] = send1[pl.ds(mey, 1)]

    for i in range(3):
        loads[i].wait()
    spread = (lax.broadcasted_iota(jnp.int32, (C, C * 8), 1) >> 3 == lax.broadcasted_iota(jnp.int32, (C, C * 8), 0))
    rows = dot(win_ref[...], spread.astype(F32).astype(BF), TN)
    same = lax.broadcasted_iota(jnp.int32, (HID, 8, C * 8), 1) == (
        lax.broadcasted_iota(jnp.int32, (HID, 8, C * 8), 2) & 7
    )
    k1[...] = jnp.where(same, rows[:, None, :], 0.0).reshape(HID * 8, C * 8).astype(BF)
    spread = (
        lax.broadcasted_iota(jnp.int32, (HID, HID * 8), 1) >> 3 == lax.broadcasted_iota(jnp.int32, (HID, HID * 8), 0)
    )
    rows = dot(wout_ref[...], spread.astype(F32).astype(BF), NN)
    same = lax.broadcasted_iota(jnp.int32, (C, 8, HID * 8), 1) == (
        lax.broadcasted_iota(jnp.int32, (C, 8, HID * 8), 2) & 7
    )
    k2[...] = jnp.where(same, rows[:, None, :], 0.0).reshape(C * 8, HID * 8).astype(BF)
    turned = jnp.transpose(jnp.broadcast_to(bin_ref[...], (HID, HID)))
    bias[...] = jnp.broadcast_to(turned[:, None, :], (HID, 8, 128)).reshape(HID * 8, 128)

    def channel(i, carry):
        block = f_ref[:, pl.ds(pl.multiple_of(i * 16, 16), 16), :].astype(F32)
        cells = jnp.concatenate(
            [block[:, :8].reshape(C * 8, 128), block[:, 8:].reshape(C * 8, 128)], axis=1
        ).astype(BF)
        acc = jnp.zeros((C * 8, 256), F32)
        for part in range(4):
            rows = slice(part * 256, part * 256 + 256)
            b = bias[rows]
            hidden = gelu(dot(k1[rows], cells, NN) + jnp.concatenate([b, b], axis=1)).astype(BF)
            acc = acc + dot(k2[:, rows], hidden, NN)
        chan[:, pl.ds(pl.multiple_of(i * 16, 16), 8), :] = acc[:, :128].reshape(C, 8, 128)
        chan[:, pl.ds(pl.multiple_of(i * 16 + 8, 8), 8), :] = acc[:, 128:].reshape(C, 8, 128)
        return carry

    lax.fori_loop(0, 4, channel, 0)

    loads[3].wait()
    lane = lax.broadcasted_iota(jnp.int32, (1, 128), 1)
    sign = jnp.where(lane < 64, 1.0, -1.0)

    def y_part(chip):
        pair = jnp.concatenate([recv1[chip * 2], recv1[chip * 2 + 1]], axis=1)
        return dot(a2_ref[chip], pair, NT)

    y_arrive(send1, recv1, ssem1, rsem1, twin)
    acc = y_part(my_chip)
    for chip in y_peers(False):
        for core in range(2):
            y_arrive(send1, recv1, ssem1, rsem1, chip * 2 + core)
        acc = acc + y_part(chip)
    half = npx * XL
    lines = acc[:half] + sign * pltpu.roll(acc[half:], 64, 1)
    send2[...] = lines.reshape(xc, zc, XL, 128).astype(BF)
    x_exchange(send2, mid2, recv2, sems2, 4)

    loads[4].wait()
    loads[5].wait()
    block = recv2[...].astype(F32).reshape(half, 128).astype(BF)
    both = dot(tx_ref[0], block, NN) + dot(tx_ref[1], block, NN)
    spectra = both[:mx] + sign * pltpu.roll(both[mx:], 64, 1)
    high, low = split(spectra)
    xpat[...] = (dot(e8_ref[...], high, NT) + dot(e8_ref[...], low, NT)).reshape(2 * C, 8, mx)

    loads[6].wait()

    def mix(c, carry):
        real, imag = carry
        wr = w_ref[0, c].astype(F32).reshape(8, 8, mx)
        wi = w_ref[1, c].astype(F32).reshape(8, 8, mx)
        xr = xpat[c][None]
        xi = xpat[c + C][None]
        return real + xr * wr - xi * wi, imag + xr * wi + xi * wr

    zero = jnp.zeros((8, 8, mx), F32)
    real, imag = lax.fori_loop(0, C, mix, (zero, zero), unroll=4)
    modes = jnp.concatenate([real.reshape(64, mx), imag.reshape(64, mx)], axis=0)

    loads[7].wait()
    both = dot3(tix_ref, modes, NT)
    cells = both[:half] - sign * pltpu.roll(both[half:], 64, 1)
    send3[...] = cells.reshape(xc, zc, XL, 128).astype(BF)
    x_exchange(send3, mid3, recv3, sems3, 6)

    block = jnp.transpose(recv3[...].astype(F32).reshape(half, 128)).astype(BF)
    ring[pl.ds(mey, 1)] = block.reshape(1, 2, 64, half)
    right = lax.rem(my_chip + 1, ny) * 2 + my_core
    left = lax.rem(my_chip + ny - 1, ny) * 2 + my_core

    def ring_copy(p, q, sem, target):
        return pltpu.make_async_remote_copy(
            src_ref=ring.at[p, q], dst_ref=ring.at[p, q], send_sem=sem.at[p, q], recv_sem=ring_in.at[p, q],
            device_id=(mex, target), device_id_type=MESH,
        )

    def cells_back(ps):
        blocks = jnp.concatenate([ring[p].reshape(128, half) for p in ps], axis=0)
        both = dot(blocks, a2b_ref[...], NN)
        for i, p in enumerate(ps):
            b = both[128 * i : 128 * i + 128]
            real = b[:64, :128] - b[64:, 128:]
            imag = b[64:, :128] + b[:64, 128:]
            lines_y[pl.ds(p, 1)] = jnp.concatenate([real, imag], axis=0).astype(BF)[None]

    reach = {("right", 0): ny // 2, ("left", 1): ny // 2, ("right", 1): (ny - 1) // 2, ("left", 0): (ny - 1) // 2}
    order = [("right", 0), ("left", 1), ("right", 1), ("left", 0)]

    def go(p, q, sem, target):
        copy = ring_copy(p, q, sem, target)
        copy.start()
        sent.append(copy)

    def at(k, core):
        return [lax.rem(my_chip + d, ny) * 2 + core for d in sorted({(ny - k) % ny, k % ny}, reverse=True)]

    def twins(k):
        ps = at(k, 1 - my_core)
        for p in ps:
            for q in range(2):
                ring_copy(p, q, ring_on, twin).wait_recv()
        cells_back(ps)

    for way, q in order:
        if reach[way, q] >= 1:
            go(mey, q, ring_on if way == "right" else ring_back, right if way == "right" else left)
    for q in range(2):
        go(mey, q, ring_twin, twin)
    loads[8].wait()
    cells_back([mey])
    for k in range(1, ny // 2 + 1):
        ps = at(k, my_core)
        for i, (way, q) in enumerate(order):
            if k <= reach[way, q]:
                p = ps[0] if way == "right" else ps[-1]
                ring_copy(p, q, ring_on, twin).wait_recv()
                if k < reach[way, q]:
                    go(p, q, ring_on, right if way == "right" else left)
                go(p, q, ring_twin, twin)
            if i == 1:
                twins(k - 1)
        cells_back(ps)
    twins(ny // 2)

    def sent_y(d, carry):
        target = lax.rem(mey + d, npy)
        y_copy(send1, recv1, ssem1, rsem1, target).wait_send()
        return carry

    lax.fori_loop(1, npy, sent_y, 0)
    for copy in sent:
        copy.wait_send()


def finish(npy, recv4, chan, b7_ref, out_hbm, done, sems):
    copies = []
    for g in range(4):
        lines = jnp.concatenate(
            [recv4[:, 16 * g : 16 * g + 16, :].reshape(npy, 1, 16, 128),
             recv4[:, 64 + 16 * g : 80 + 16 * g, :].reshape(npy, 1, 16, 128)], axis=1
        ).reshape(npy * 32, 128)
        values = dot(lines, b7_ref[...], TN)
        for o in range(8):
            total = values[:, 128 * o : 128 * o + 128] + chan[8 * g + o]
            done[8 * g + o] = gelu(total).astype(BF)
        block = pl.ds(8 * g, 8)
        copies.append(pltpu.make_async_copy(done.at[block], out_hbm.at[block], sems.at[g]))
        copies[-1].start()
    for copy in copies:
        copy.wait()


def body(npx, npy, field, spec_weight, w_in, b_in, w_out):
    mx = spec_weight.shape[4]
    a1, a2, a2b, tx, tix, b7, e8 = tables(npx, npy, mx)
    cells = field.reshape(C, XL * YL, NZ)
    weight = jnp.transpose(spec_weight[0], (0, 1, 2, 4, 5, 3)).reshape(2, C, C * K2, mx)
    vmem = pl.BlockSpec(memory_space=pltpu.VMEM)
    hbm = pl.BlockSpec(memory_space=pltpu.HBM)
    xc, zc = chips(npx)
    exchange = [pltpu.VMEM((xc, zc, XL, 128), BF)] * 3
    loaded = [
        cells, jnp.asarray(a1), w_in[0], b_in, jnp.transpose(w_out[0]), weight,
        jnp.asarray(a2), jnp.asarray(tx), jnp.asarray(tix), jnp.asarray(e8), jnp.asarray(a2b),
    ]
    loaded = [pltpu.with_memory_space_constraint(a, pltpu.HBM) for a in loaded]
    lines, chan = pl.pallas_call(
        functools.partial(kernel, npx, npy),
        out_shape=(
            pltpu.VMEM((npy, 128, 128), BF),
            pltpu.VMEM((C, XL * YL, NZ), F32),
        ),
        in_specs=[hbm] * len(loaded),
        out_specs=(vmem, vmem),
        scratch_shapes=[
            pltpu.VMEM((npy, 2, 8, 8, 128), F32),
            pltpu.VMEM((npy, 128, 128), BF),
            pltpu.VMEM((npy, 128, 128), BF),
            *exchange,
            *exchange,
            pltpu.VMEM((npy, 2, 64, npx * XL), BF),
            *[pltpu.VMEM(a.shape, a.dtype) for a in loaded[:-1]],
            pltpu.VMEM(a2b.shape[1:], BF),
            pltpu.VMEM((HID * 8, C * 8), BF),
            pltpu.VMEM((C * 8, HID * 8), BF),
            pltpu.VMEM((HID * 8, 128), F32),
            pltpu.VMEM((2 * C, 8, mx), F32),
            pltpu.SemaphoreType.DMA((npy,)),
            pltpu.SemaphoreType.DMA((npy,)),
            pltpu.SemaphoreType.DMA((4, max(xc, zc))),
            pltpu.SemaphoreType.DMA((4, max(xc, zc))),
            pltpu.SemaphoreType.DMA((npy, 2)),
            pltpu.SemaphoreType.DMA((npy, 2)),
            pltpu.SemaphoreType.DMA((npy, 2)),
            pltpu.SemaphoreType.DMA((npy, 2)),
            pltpu.SemaphoreType.DMA((14,)),
        ],
        compiler_params=pltpu.CompilerParams(
            collective_id=0, has_side_effects=True, vmem_limit_bytes=32 * 1024 * 1024
        ),
    )(*loaded)
    out = pl.pallas_call(
        functools.partial(finish, npy),
        out_shape=jax.ShapeDtypeStruct((C, XL * YL, NZ), BF),
        in_specs=[vmem] * 3,
        out_specs=hbm,
        scratch_shapes=[pltpu.VMEM((C, XL * YL, NZ), BF), pltpu.SemaphoreType.DMA((4,))],
        compiler_params=pltpu.CompilerParams(vmem_limit_bytes=16 * 1024 * 1024),
    )(lines, chan, jnp.asarray(b7))
    return out.reshape(field.shape)


def solution(mesh):
    in_specs = (
        P(None, "px", "py", None),
        P(None, None, None, None, None, "px", "py"),
        P(),
        P(),
        P(),
    )
    return jax.shard_map(
        functools.partial(body, mesh.shape["px"], mesh.shape["py"]),
        mesh=mesh, in_specs=in_specs, out_specs=P(None, "px", "py", None), check_vma=False,
    )
```

```python
import functools
import math

import jax
import jax.numpy as jnp
import ml_dtypes
import numpy as np
from jax import lax
from jax.experimental import pallas as pl
from jax.experimental.pallas import tpu as pltpu
from jax.sharding import PartitionSpec as P

MESH = pl.DeviceIdType.MESH
BF = jnp.bfloat16
F32 = jnp.float32
C = 32
HID = 128
XL = 8
YL = 16
NZ = 128
K2 = 2
NT = (((1,), (1,)), ((), ()))
NN = (((1,), (0,)), ((), ()))
TN = (((0,), (0,)), ((), ()))


def dot(a, b, dims):
    return lax.dot_general(a, b, dims, preferred_element_type=F32)


def signed(count, length):
    index = np.arange(count)
    return np.where(index < count // 2, index, index - count + length)


def angles(positions, freqs, length):
    return 2.0 * math.pi * ((positions[:, None] * freqs[None, :]) % length) / length


def tables(npx, npy, mx):
    nx, ny, my, mz = XL * npx, YL * npy, npx, K2 * npy
    ang = angles(np.arange(NZ), np.arange(mz), NZ)
    fwd = np.stack([np.cos(ang), -np.sin(ang)]) * 0.125
    fwd = fwd.reshape(2, NZ, npy, K2).transpose(2, 0, 3, 1)
    a1 = np.zeros((2, npy, 2, 4, K2, 2, NZ))
    for q in range(2):
        for c in range(2):
            a1[q, :, :, 2 * q + c, :, c, :] = fwd
    a1 = a1.reshape(2, npy * 16, 2 * NZ)
    ang = angles(np.arange(ny), signed(my, ny), ny)
    cs = np.stack([np.cos(ang), np.sin(ang)]).reshape(2, npy // 2, 2, YL, my)
    a2 = np.zeros((npy // 2, 2, my, XL, 2, XL, YL))
    for x in range(XL):
        a2[:, :, :, x, :, x, :] = cs.transpose(1, 0, 4, 2, 3)
    a2 = a2.reshape(npy // 2, 2 * my * XL, 2 * XL * YL)
    ang = angles(np.arange(nx), signed(mx, nx), nx)
    cs = np.stack([np.cos(ang), np.sin(ang)])
    tx = cs.transpose(0, 2, 1).reshape(2 * mx, nx) / math.sqrt(nx * ny)
    tix = cs.reshape(2 * nx, mx) / math.sqrt(mx * my)
    ang = angles(np.arange(NZ), np.arange(mz), NZ)
    weight = np.where(np.arange(mz) == 0, 1.0, 2.0) * (8.0 / math.sqrt(NZ * mz))
    inv = np.stack([np.cos(ang), -np.sin(ang)]) * weight
    inv = inv.reshape(2, NZ, npy, K2).transpose(2, 0, 3, 1)
    b7 = np.zeros((npy, 2, 8, K2, 8, NZ))
    for o in range(8):
        b7[:, :, o, :, o, :] = inv
    b7 = b7.reshape(npy * 32, 8 * NZ)
    e8 = np.zeros((2 * C, 8, 2 * C, K2))
    for r in range(8):
        e8[np.arange(2 * C), r, np.arange(2 * C), r % 2] = 1.0
    e8 = e8.reshape(2 * C * 8, 2 * C * K2)

    def half(t):
        return t.astype(np.float32).astype(ml_dtypes.bfloat16)

    def two(t):
        high = half(t)
        return np.stack([high, half(t - high.astype(np.float64))])

    return half(a1), half(a2), two(tx), two(tix), half(b7), half(e8)


def split(value):
    high = value.astype(BF)
    return high, (value - high.astype(F32)).astype(BF)


def dot3(table, value, dims):
    high, low = split(value)
    return dot(table[0], high, dims) + dot(table[0], low, dims) + dot(table[1], high, dims)


def gelu(v):
    k = math.sqrt(2.0 / math.pi)
    half = 0.5 * v
    return half + half * jnp.tanh(v * (k + (k * 0.044715) * (v * v)))


def kernel(
    npx, npy,
    f_hbm, a1_hbm, win_hbm, bin_hbm, wout_hbm, w_hbm, a2_hbm, tx_hbm, tix_hbm, e8_hbm,
    recv4, chan,
    zs, send1, recv1, send2, recv2, send3, recv3, send4,
    f_ref, a1_ref, win_ref, bin_ref, wout_ref, w_ref, a2_ref, tx_ref, tix_ref, e8_ref,
    k1, k2, bias, xpat,
    ssem1, rsem1, sems2, sems3, ssem4, rsem4, tsem,
):
    ny = npy // 2
    mx = w_ref.shape[-1]
    sent = []
    mex = lax.axis_index("px")
    mey = lax.axis_index("py")
    my_chip = mey // 2
    my_core = mey % 2
    twin = my_chip * 2 + 1 - my_core

    def load(i, src, dst):
        return pltpu.make_async_copy(src, dst, tsem.at[i])

    cells_in = [load(0, a1_hbm, a1_ref)] + [
        load(1 + i, f_hbm.at[pl.ds(i * 8, 8)], f_ref.at[pl.ds(i * 8, 8)]) for i in range(4)
    ]
    pairs = [(win_hbm, win_ref), (bin_hbm, bin_ref), (wout_hbm, wout_ref), (a2_hbm, a2_ref), (tx_hbm, tx_ref),
             (e8_hbm, e8_ref), (w_hbm, w_ref), (tix_hbm, tix_ref)]
    loads = [load(5 + i, src, dst) for i, (src, dst) in enumerate(pairs)]
    barrier = pltpu.get_barrier_semaphore()

    for load in cells_in + loads:
        load.start()
    x_peers = [(mex + d) & (npx - 1) for d in range(1, npx)]
    y_peers_all = [(mey + d) & (npy - 1) for d in range(1, npy)]
    for peer in y_peers_all:
        pl.semaphore_signal(barrier, inc=1, device_id=(mex, peer), device_id_type=MESH)
    for peer in x_peers:
        pl.semaphore_signal(barrier, inc=1, device_id=(peer, mey), device_id_type=MESH)

    def forward_z(g, carry):
        f4 = f_ref[pl.ds(g * 4, 4)]
        acc = dot(a1_ref[0], jnp.concatenate([f4[0], f4[1]], axis=1), NT)
        acc = acc + dot(a1_ref[1], jnp.concatenate([f4[2], f4[3]], axis=1), NT)
        zs[:, :, pl.ds(g, 1)] = acc.reshape(npy, 2, 1, 8, 128)
        return carry

    cells_in[0].wait()
    for i in range(4):
        cells_in[1 + i].wait()
        lax.fori_loop(2 * i, 2 * i + 2, forward_z, 0, unroll=2)
    send1[...] = zs[...].reshape(npy, 128, 128).astype(BF)

    pl.semaphore_wait(barrier, npy + npx - 2)

    def y_copy(src, dst, ssem, rsem, target):
        return pltpu.make_async_remote_copy(
            src_ref=src.at[target], dst_ref=dst.at[mey], send_sem=ssem.at[target], recv_sem=rsem.at[mey],
            device_id=(mex, target), device_id_type=MESH,
        )

    def y_arrive(src, dst, ssem, rsem, source):
        pltpu.make_async_remote_copy(
            src_ref=src.at[source], dst_ref=dst.at[source], send_sem=ssem.at[source], recv_sem=rsem.at[source],
            device_id=(mex, source), device_id_type=MESH,
        ).wait_recv()

    def x_exchange(src, dst, sems):
        for other in x_peers:
            pltpu.make_async_remote_copy(
                src_ref=src.at[other], dst_ref=dst.at[mex], send_sem=sems.at[0], recv_sem=sems.at[1],
                device_id=(other, mey), device_id_type=MESH,
            ).start()
        dst[pl.ds(mex, 1)] = src[pl.ds(mex, 1)]
        whole = pltpu.make_async_remote_copy(
            src_ref=src.at[pl.ds(0, npx - 1)], dst_ref=dst.at[pl.ds(0, npx - 1)], send_sem=sems.at[0],
            recv_sem=sems.at[1], device_id=(x_peers[0], mey), device_id_type=MESH,
        )
        whole.wait_recv()
        sent.append(whole)

    def y_peers(far_first):
        offsets = sorted(range(1, ny), key=lambda d: min(d, ny - d), reverse=far_first)
        return [lax.rem(my_chip + d, ny) for d in offsets]

    for chip in y_peers(True):
        for core in range(2):
            y_copy(send1, recv1, ssem1, rsem1, chip * 2 + core).start()
    y_copy(send1, recv1, ssem1, rsem1, twin).start()
    recv1[pl.ds(mey, 1)] = send1[pl.ds(mey, 1)]

    for i in range(3):
        loads[i].wait()
    spread = (lax.broadcasted_iota(jnp.int32, (C, C * 8), 1) >> 3 == lax.broadcasted_iota(jnp.int32, (C, C * 8), 0))
    rows = dot(win_ref[...], spread.astype(F32).astype(BF), TN)
    same = lax.broadcasted_iota(jnp.int32, (HID, 8, C * 8), 1) == (
        lax.broadcasted_iota(jnp.int32, (HID, 8, C * 8), 2) & 7
    )
    k1[...] = jnp.where(same, rows[:, None, :], 0.0).reshape(HID * 8, C * 8).astype(BF)
    spread = (
        lax.broadcasted_iota(jnp.int32, (HID, HID * 8), 1) >> 3 == lax.broadcasted_iota(jnp.int32, (HID, HID * 8), 0)
    )
    rows = dot(wout_ref[...], spread.astype(F32).astype(BF), NN)
    same = lax.broadcasted_iota(jnp.int32, (C, 8, HID * 8), 1) == (
        lax.broadcasted_iota(jnp.int32, (C, 8, HID * 8), 2) & 7
    )
    k2[...] = jnp.where(same, rows[:, None, :], 0.0).reshape(C * 8, HID * 8).astype(BF)
    turned = jnp.transpose(jnp.broadcast_to(bin_ref[...], (HID, HID)))
    bias[...] = jnp.broadcast_to(turned[:, None, :], (HID, 8, 128)).reshape(HID * 8, 128)

    def channel(i, carry):
        block = f_ref[:, pl.ds(pl.multiple_of(i * 16, 16), 16), :].astype(F32)
        cells = jnp.concatenate(
            [block[:, :8].reshape(C * 8, 128), block[:, 8:].reshape(C * 8, 128)], axis=1
        ).astype(BF)
        acc = jnp.zeros((C * 8, 256), F32)
        for part in range(4):
            rows = slice(part * 256, part * 256 + 256)
            b = bias[rows]
            hidden = gelu(dot(k1[rows], cells, NN) + jnp.concatenate([b, b], axis=1)).astype(BF)
            acc = acc + dot(k2[:, rows], hidden, NN)
        chan[:, pl.ds(pl.multiple_of(i * 16, 16), 8), :] = acc[:, :128].reshape(C, 8, 128)
        chan[:, pl.ds(pl.multiple_of(i * 16 + 8, 8), 8), :] = acc[:, 128:].reshape(C, 8, 128)
        return carry

    lax.fori_loop(0, 4, channel, 0)

    loads[3].wait()
    lane = lax.broadcasted_iota(jnp.int32, (1, 128), 1)
    sign = jnp.where(lane < 64, 1.0, -1.0)

    def y_part(chip):
        pair = jnp.concatenate([recv1[chip * 2], recv1[chip * 2 + 1]], axis=1)
        return dot(a2_ref[chip], pair, NT)

    y_arrive(send1, recv1, ssem1, rsem1, twin)
    acc = y_part(my_chip)
    for chip in y_peers(False):
        for core in range(2):
            y_arrive(send1, recv1, ssem1, rsem1, chip * 2 + core)
        acc = acc + y_part(chip)
    half = npx * XL
    lines = acc[:half] + sign * pltpu.roll(acc[half:], 64, 1)
    send2[...] = lines.reshape(npx, XL, 128).astype(BF)
    x_exchange(send2, recv2, sems2)

    loads[4].wait()
    loads[5].wait()
    block = recv2[...].astype(F32).reshape(half, 128).astype(BF)
    both = dot(tx_ref[0], block, NN) + dot(tx_ref[1], block, NN)
    spectra = both[:mx] + sign * pltpu.roll(both[mx:], 64, 1)
    high, low = split(spectra)
    xpat[...] = (dot(e8_ref[...], high, NT) + dot(e8_ref[...], low, NT)).reshape(2 * C, 8, mx)

    loads[6].wait()

    def mix(c, carry):
        real, imag = carry
        wr = w_ref[0, c].astype(F32).reshape(8, 8, mx)
        wi = w_ref[1, c].astype(F32).reshape(8, 8, mx)
        xr = xpat[c][None]
        xi = xpat[c + C][None]
        return real + xr * wr - xi * wi, imag + xr * wi + xi * wr

    zero = jnp.zeros((8, 8, mx), F32)
    real, imag = lax.fori_loop(0, C, mix, (zero, zero), unroll=4)
    modes = jnp.concatenate([real.reshape(64, mx), imag.reshape(64, mx)], axis=0)

    loads[7].wait()
    both = dot3(tix_ref, modes, NT)
    cells = both[:half] - sign * pltpu.roll(both[half:], 64, 1)
    send3[...] = cells.reshape(npx, XL, 128).astype(BF)
    x_exchange(send3, recv3, sems3)

    block = recv3[...].astype(F32).reshape(half, 128)
    turned = jnp.concatenate([block, -sign * pltpu.roll(block, 64, 1)], axis=0)
    turned = jnp.transpose(turned).astype(BF)

    def y_back(chip):
        both = dot(turned, a2_ref[chip], NN).astype(BF)
        send4[pl.ds(chip * 2, 1)] = both[:, :128][None]
        send4[pl.ds(chip * 2 + 1, 1)] = both[:, 128:][None]

    for chip in y_peers(True):
        y_back(chip)
        for core in range(2):
            y_copy(send4, recv4, ssem4, rsem4, chip * 2 + core).start()
    y_back(my_chip)
    y_copy(send4, recv4, ssem4, rsem4, twin).start()
    recv4[pl.ds(mey, 1)] = send4[pl.ds(mey, 1)]

    lax.fori_loop(4, 8, channel, 0)

    y_arrive(send4, recv4, ssem4, rsem4, twin)
    for chip in y_peers(False):
        for core in range(2):
            y_arrive(send4, recv4, ssem4, rsem4, chip * 2 + core)

    def sent_y(d, carry):
        target = lax.rem(mey + d, npy)
        y_copy(send1, recv1, ssem1, rsem1, target).wait_send()
        y_copy(send4, recv4, ssem4, rsem4, target).wait_send()
        return carry

    lax.fori_loop(1, npy, sent_y, 0)
    for copy in sent:
        copy.wait_send()


def finish(npy, recv4, chan, b7_ref, out_hbm, done, sems):
    copies = []
    for g in range(4):
        lines = jnp.concatenate(
            [recv4[:, 16 * g : 16 * g + 16, :].reshape(npy, 1, 16, 128),
             recv4[:, 64 + 16 * g : 80 + 16 * g, :].reshape(npy, 1, 16, 128)], axis=1
        ).reshape(npy * 32, 128)
        values = dot(lines, b7_ref[...], TN)
        for o in range(8):
            total = values[:, 128 * o : 128 * o + 128] + chan[8 * g + o]
            done[8 * g + o] = gelu(total).astype(BF)
        block = pl.ds(8 * g, 8)
        copies.append(pltpu.make_async_copy(done.at[block], out_hbm.at[block], sems.at[g]))
        copies[-1].start()
    for copy in copies:
        copy.wait()


def body(npx, npy, field, spec_weight, w_in, b_in, w_out):
    mx = spec_weight.shape[4]
    a1, a2, tx, tix, b7, e8 = tables(npx, npy, mx)
    cells = field.reshape(C, XL * YL, NZ)
    weight = jnp.transpose(spec_weight[0], (0, 1, 2, 4, 5, 3)).reshape(2, C, C * K2, mx)
    vmem = pl.BlockSpec(memory_space=pltpu.VMEM)
    hbm = pl.BlockSpec(memory_space=pltpu.HBM)
    exchange = [pltpu.VMEM((npx, XL, 128), BF)] * 2
    loaded = [
        cells, jnp.asarray(a1), w_in[0], b_in, jnp.transpose(w_out[0]), weight,
        jnp.asarray(a2), jnp.asarray(tx), jnp.asarray(tix), jnp.asarray(e8),
    ]
    loaded = [pltpu.with_memory_space_constraint(a, pltpu.HBM) for a in loaded]
    lines, chan = pl.pallas_call(
        functools.partial(kernel, npx, npy),
        out_shape=(
            pltpu.VMEM((npy, 128, 128), BF),
            pltpu.VMEM((C, XL * YL, NZ), F32),
        ),
        in_specs=[hbm] * len(loaded),
        out_specs=(vmem, vmem),
        scratch_shapes=[
            pltpu.VMEM((npy, 2, 8, 8, 128), F32),
            pltpu.VMEM((npy, 128, 128), BF),
            pltpu.VMEM((npy, 128, 128), BF),
            *exchange,
            *exchange,
            pltpu.VMEM((npy, 128, 128), BF),
            *[pltpu.VMEM(a.shape, a.dtype) for a in loaded],
            pltpu.VMEM((HID * 8, C * 8), BF),
            pltpu.VMEM((C * 8, HID * 8), BF),
            pltpu.VMEM((HID * 8, 128), F32),
            pltpu.VMEM((2 * C, 8, mx), F32),
            pltpu.SemaphoreType.DMA((npy,)),
            pltpu.SemaphoreType.DMA((npy,)),
            pltpu.SemaphoreType.DMA((2,)),
            pltpu.SemaphoreType.DMA((2,)),
            pltpu.SemaphoreType.DMA((npy,)),
            pltpu.SemaphoreType.DMA((npy,)),
            pltpu.SemaphoreType.DMA((13,)),
        ],
        compiler_params=pltpu.CompilerParams(
            collective_id=0, has_side_effects=True, vmem_limit_bytes=32 * 1024 * 1024
        ),
    )(*loaded)
    out = pl.pallas_call(
        functools.partial(finish, npy),
        out_shape=jax.ShapeDtypeStruct((C, XL * YL, NZ), BF),
        in_specs=[vmem] * 3,
        out_specs=hbm,
        scratch_shapes=[pltpu.VMEM((C, XL * YL, NZ), BF), pltpu.SemaphoreType.DMA((4,))],
        compiler_params=pltpu.CompilerParams(vmem_limit_bytes=16 * 1024 * 1024),
    )(lines, chan, jnp.asarray(b7))
    return out.reshape(field.shape)


def solution(mesh):
    in_specs = (
        P(None, "px", "py", None),
        P(None, None, None, None, None, "px", "py"),
        P(),
        P(),
        P(),
    )
    return jax.shard_map(
        functools.partial(body, mesh.shape["px"], mesh.shape["py"]),
        mesh=mesh, in_specs=in_specs, out_specs=P(None, "px", "py", None), check_vma=False,
    )
```

```python
import functools
import math

import jax
import jax.numpy as jnp
import ml_dtypes
import numpy as np
from jax import lax
from jax.experimental import pallas as pl
from jax.experimental.pallas import tpu as pltpu
from jax.sharding import PartitionSpec as P

MESH = pl.DeviceIdType.MESH
BF = jnp.bfloat16
F32 = jnp.float32
C = 32
HID = 128
XL = 8
YL = 16
NZ = 128
K2 = 2
NT = (((1,), (1,)), ((), ()))
NN = (((1,), (0,)), ((), ()))
TN = (((0,), (0,)), ((), ()))


def dot(a, b, dims):
    return lax.dot_general(a, b, dims, preferred_element_type=F32)


def signed(count, length):
    index = np.arange(count)
    return np.where(index < count // 2, index, index - count + length)


def angles(positions, freqs, length):
    return 2.0 * math.pi * ((positions[:, None] * freqs[None, :]) % length) / length


def tables(npx, npy, mx):
    nx, ny, my, mz = XL * npx, YL * npy, npx, K2 * npy
    ang = angles(np.arange(NZ), np.arange(mz), NZ)
    fwd = np.stack([np.cos(ang), -np.sin(ang)]) * 0.125
    fwd = fwd.reshape(2, NZ, npy, K2).transpose(2, 0, 3, 1)
    a1 = np.zeros((2, npy, 2, 4, K2, 2, NZ))
    for q in range(2):
        for c in range(2):
            a1[q, :, :, 2 * q + c, :, c, :] = fwd
    a1 = a1.reshape(2, npy * 16, 2 * NZ)
    ang = angles(np.arange(ny), signed(my, ny), ny)
    cs = np.stack([np.cos(ang), np.sin(ang)]).reshape(2, npy // 2, 2, YL, my)
    a2 = np.zeros((npy // 2, 2, my, XL, 2, XL, YL))
    for x in range(XL):
        a2[:, :, :, x, :, x, :] = cs.transpose(1, 0, 4, 2, 3)
    a2 = a2.reshape(npy // 2, 2 * my * XL, 2 * XL * YL)
    ang = angles(np.arange(nx), signed(mx, nx), nx)
    cs = np.stack([np.cos(ang), np.sin(ang)])
    tx = cs.transpose(0, 2, 1).reshape(2 * mx, nx) / math.sqrt(nx * ny)
    tix = cs.reshape(2 * nx, mx) / math.sqrt(mx * my)
    ang = angles(np.arange(NZ), np.arange(mz), NZ)
    weight = np.where(np.arange(mz) == 0, 1.0, 2.0) * (8.0 / math.sqrt(NZ * mz))
    inv = np.stack([np.cos(ang), -np.sin(ang)]) * weight
    inv = inv.reshape(2, NZ, npy, K2).transpose(2, 0, 3, 1)
    b7 = np.zeros((npy, 2, 8, K2, 8, NZ))
    for o in range(8):
        b7[:, :, o, :, o, :] = inv
    b7 = b7.reshape(npy * 32, 8 * NZ)
    e8 = np.zeros((2 * C, 8, 2 * C, K2))
    for r in range(8):
        e8[np.arange(2 * C), r, np.arange(2 * C), r % 2] = 1.0
    e8 = e8.reshape(2 * C * 8, 2 * C * K2)

    def half(t):
        return t.astype(np.float32).astype(ml_dtypes.bfloat16)

    def two(t):
        high = half(t)
        return np.stack([high, half(t - high.astype(np.float64))])

    return half(a1), half(a2), two(tx), two(tix), half(b7), half(e8)


def split(value):
    high = value.astype(BF)
    return high, (value - high.astype(F32)).astype(BF)


def dot3(table, value, dims):
    high, low = split(value)
    return dot(table[0], high, dims) + dot(table[0], low, dims) + dot(table[1], high, dims)


def gelu(v):
    k = math.sqrt(2.0 / math.pi)
    half = 0.5 * v
    return half + half * jnp.tanh(v * (k + (k * 0.044715) * (v * v)))


def kernel(
    npx, npy,
    f_hbm, a1_hbm, win_hbm, bin_hbm, wout_hbm, w_hbm, a2_hbm, tx_hbm, tix_hbm, e8_hbm,
    recv4, chan,
    zs, send1, recv1, relay1, relay4, send2, recv2, send3, recv3, send4,
    f_ref, a1_ref, win_ref, bin_ref, wout_ref, w_ref, a2_ref, tx_ref, tix_ref, e8_ref,
    k1, k2, bias, xpat,
    ssem1, rsem1, rlsem1, sems2, sems3, ssem4, rsem4, rlsem4, tsem,
):
    ny = npy // 2
    mx = w_ref.shape[-1]
    sent = []
    mex = lax.axis_index("px")
    mey = lax.axis_index("py")
    my_chip = mey // 2
    my_core = mey % 2
    twin = my_chip * 2 + 1 - my_core

    def load(i, src, dst):
        return pltpu.make_async_copy(src, dst, tsem.at[i])

    cells_in = [load(0, a1_hbm, a1_ref)] + [
        load(1 + i, f_hbm.at[pl.ds(i * 8, 8)], f_ref.at[pl.ds(i * 8, 8)]) for i in range(4)
    ]
    pairs = [(win_hbm, win_ref), (bin_hbm, bin_ref), (wout_hbm, wout_ref), (a2_hbm, a2_ref), (tx_hbm, tx_ref),
             (e8_hbm, e8_ref), (w_hbm, w_ref), (tix_hbm, tix_ref)]
    loads = [load(5 + i, src, dst) for i, (src, dst) in enumerate(pairs)]
    barrier = pltpu.get_barrier_semaphore()

    for load in cells_in:
        load.start()
    x_peers = [(mex + d) & (npx - 1) for d in range(1, npx)]
    y_peers_all = [(mey + d) & (npy - 1) for d in range(1, npy)]
    for peer in y_peers_all:
        pl.semaphore_signal(barrier, inc=1, device_id=(mex, peer), device_id_type=MESH)
    for peer in x_peers:
        pl.semaphore_signal(barrier, inc=1, device_id=(peer, mey), device_id_type=MESH)

    def forward_z(g, carry):
        f4 = f_ref[pl.ds(g * 4, 4)]
        acc = dot(a1_ref[0], jnp.concatenate([f4[0], f4[1]], axis=1), NT)
        acc = acc + dot(a1_ref[1], jnp.concatenate([f4[2], f4[3]], axis=1), NT)
        zs[:, :, pl.ds(g, 1)] = acc.reshape(npy, 2, 1, 8, 128)
        return carry

    cells_in[0].wait()
    for i in range(4):
        cells_in[1 + i].wait()
        lax.fori_loop(2 * i, 2 * i + 2, forward_z, 0, unroll=2)
    for load in loads:
        load.start()
    send1[...] = zs[...].reshape(npy, 128, 128).astype(BF)

    pl.semaphore_wait(barrier, npy + npx - 2)

    def y_copy(src, dst, ssem, rsem, target):
        return pltpu.make_async_remote_copy(
            src_ref=src.at[target], dst_ref=dst.at[mey], send_sem=ssem.at[target], recv_sem=rsem.at[mey],
            device_id=(mex, target), device_id_type=MESH,
        )

    def y_arrive(src, dst, ssem, rsem, source):
        pltpu.make_async_remote_copy(
            src_ref=src.at[source], dst_ref=dst.at[source], send_sem=ssem.at[source], recv_sem=rsem.at[source],
            device_id=(mex, source), device_id_type=MESH,
        ).wait_recv()

    def x_exchange(src, dst, sems):
        for other in x_peers:
            pltpu.make_async_remote_copy(
                src_ref=src.at[other], dst_ref=dst.at[mex], send_sem=sems.at[0], recv_sem=sems.at[1],
                device_id=(other, mey), device_id_type=MESH,
            ).start()
        dst[pl.ds(mex, 1)] = src[pl.ds(mex, 1)]
        whole = pltpu.make_async_remote_copy(
            src_ref=src.at[pl.ds(0, npx - 1)], dst_ref=dst.at[pl.ds(0, npx - 1)], send_sem=sems.at[0],
            recv_sem=sems.at[1], device_id=(x_peers[0], mey), device_id_type=MESH,
        )
        whole.wait_recv()
        sent.append(whole)

    step = ny // 4
    quarter = [lax.rem(my_chip + step, ny) * 2 + my_core, lax.rem(my_chip + ny - step, ny) * 2 + my_core]
    opposite = lax.rem(my_chip + ny // 2, ny) * 2

    def to_relay(src, relay, sems, way):
        return pltpu.make_async_remote_copy(
            src_ref=src.at[opposite + way], dst_ref=relay.at[way], send_sem=sems.at[0, way], recv_sem=sems.at[1, way],
            device_id=(mex, quarter[way]), device_id_type=MESH,
        )

    def from_relay(relay, dst, sems, rsem, way):
        source = quarter[1 - way]
        target = (quarter[way] - my_core) + way
        return pltpu.make_async_remote_copy(
            src_ref=relay.at[way], dst_ref=dst.at[source], send_sem=sems.at[2, way], recv_sem=rsem.at[source],
            device_id=(mex, target), device_id_type=MESH,
        )

    def forward(src, relay, dst, sems, rsem):
        for way in range(2):
            to_relay(src, relay, sems, way).wait_recv()
            from_relay(relay, dst, sems, rsem, way).start()
            sent.append(to_relay(src, relay, sems, way))
            sent.append(from_relay(relay, dst, sems, rsem, way))

    def y_peers(far_first):
        offsets = sorted(range(1, ny), key=lambda d: min(d, ny - d), reverse=far_first)
        return [lax.rem(my_chip + d, ny) for d in offsets]

    for way in range(2):
        to_relay(send1, relay1, rlsem1, way).start()
    for chip in y_peers(True)[1:]:
        for core in range(2):
            y_copy(send1, recv1, ssem1, rsem1, chip * 2 + core).start()
    y_copy(send1, recv1, ssem1, rsem1, twin).start()
    recv1[pl.ds(mey, 1)] = send1[pl.ds(mey, 1)]

    for i in range(3):
        loads[i].wait()
    spread = (lax.broadcasted_iota(jnp.int32, (C, C * 8), 1) >> 3 == lax.broadcasted_iota(jnp.int32, (C, C * 8), 0))
    rows = dot(win_ref[...], spread.astype(F32).astype(BF), TN)
    same = lax.broadcasted_iota(jnp.int32, (HID, 8, C * 8), 1) == (
        lax.broadcasted_iota(jnp.int32, (HID, 8, C * 8), 2) & 7
    )
    k1[...] = jnp.where(same, rows[:, None, :], 0.0).reshape(HID * 8, C * 8).astype(BF)
    spread = (
        lax.broadcasted_iota(jnp.int32, (HID, HID * 8), 1) >> 3 == lax.broadcasted_iota(jnp.int32, (HID, HID * 8), 0)
    )
    rows = dot(wout_ref[...], spread.astype(F32).astype(BF), NN)
    same = lax.broadcasted_iota(jnp.int32, (C, 8, HID * 8), 1) == (
        lax.broadcasted_iota(jnp.int32, (C, 8, HID * 8), 2) & 7
    )
    k2[...] = jnp.where(same, rows[:, None, :], 0.0).reshape(C * 8, HID * 8).astype(BF)
    turned = jnp.transpose(jnp.broadcast_to(bin_ref[...], (HID, HID)))
    bias[...] = jnp.broadcast_to(turned[:, None, :], (HID, 8, 128)).reshape(HID * 8, 128)

    forward(send1, relay1, recv1, rlsem1, rsem1)

    def channel(i, carry):
        block = f_ref[:, pl.ds(pl.multiple_of(i * 16, 16), 16), :].astype(F32)
        cells = jnp.concatenate(
            [block[:, :8].reshape(C * 8, 128), block[:, 8:].reshape(C * 8, 128)], axis=1
        ).astype(BF)
        acc = jnp.zeros((C * 8, 256), F32)
        for part in range(4):
            rows = slice(part * 256, part * 256 + 256)
            b = bias[rows]
            hidden = gelu(dot(k1[rows], cells, NN) + jnp.concatenate([b, b], axis=1)).astype(BF)
            acc = acc + dot(k2[:, rows], hidden, NN)
        chan[:, pl.ds(pl.multiple_of(i * 16, 16), 8), :] = acc[:, :128].reshape(C, 8, 128)
        chan[:, pl.ds(pl.multiple_of(i * 16 + 8, 8), 8), :] = acc[:, 128:].reshape(C, 8, 128)
        return carry

    lax.fori_loop(0, 4, channel, 0)

    loads[3].wait()
    lane = lax.broadcasted_iota(jnp.int32, (1, 128), 1)
    sign = jnp.where(lane < 64, 1.0, -1.0)

    def y_part(chip):
        pair = jnp.concatenate([recv1[chip * 2], recv1[chip * 2 + 1]], axis=1)
        return dot(a2_ref[chip], pair, NT)

    y_arrive(send1, recv1, ssem1, rsem1, twin)
    acc = y_part(my_chip)
    for chip in y_peers(False):
        for core in range(2):
            y_arrive(send1, recv1, ssem1, rsem1, chip * 2 + core)
        acc = acc + y_part(chip)
    half = npx * XL
    lines = acc[:half] + sign * pltpu.roll(acc[half:], 64, 1)
    send2[...] = lines.reshape(npx, XL, 128).astype(BF)
    x_exchange(send2, recv2, sems2)

    loads[4].wait()
    loads[5].wait()
    block = recv2[...].astype(F32).reshape(half, 128).astype(BF)
    both = dot(tx_ref[0], block, NN) + dot(tx_ref[1], block, NN)
    spectra = both[:mx] + sign * pltpu.roll(both[mx:], 64, 1)
    high, low = split(spectra)
    xpat[...] = (dot(e8_ref[...], high, NT) + dot(e8_ref[...], low, NT)).reshape(2 * C, 8, mx)

    loads[6].wait()

    def mix(c, carry):
        real, imag = carry
        wr = w_ref[0, c].astype(F32).reshape(8, 8, mx)
        wi = w_ref[1, c].astype(F32).reshape(8, 8, mx)
        xr = xpat[c][None]
        xi = xpat[c + C][None]
        return real + xr * wr - xi * wi, imag + xr * wi + xi * wr

    zero = jnp.zeros((8, 8, mx), F32)
    real, imag = lax.fori_loop(0, C, mix, (zero, zero), unroll=4)
    modes = jnp.concatenate([real.reshape(64, mx), imag.reshape(64, mx)], axis=0)

    loads[7].wait()
    both = dot3(tix_ref, modes, NT)
    cells = both[:half] - sign * pltpu.roll(both[half:], 64, 1)
    send3[...] = cells.reshape(npx, XL, 128).astype(BF)
    x_exchange(send3, recv3, sems3)

    block = recv3[...].astype(F32).reshape(half, 128)
    turned = jnp.concatenate([block, -sign * pltpu.roll(block, 64, 1)], axis=0)
    turned = jnp.transpose(turned).astype(BF)

    def y_back(chip):
        both = dot(turned, a2_ref[chip], NN).astype(BF)
        send4[pl.ds(chip * 2, 1)] = both[:, :128][None]
        send4[pl.ds(chip * 2 + 1, 1)] = both[:, 128:][None]

    for i, chip in enumerate(y_peers(True)):
        y_back(chip)
        for core in range(2):
            if i:
                y_copy(send4, recv4, ssem4, rsem4, chip * 2 + core).start()
            else:
                to_relay(send4, relay4, rlsem4, core).start()
    y_back(my_chip)
    y_copy(send4, recv4, ssem4, rsem4, twin).start()
    recv4[pl.ds(mey, 1)] = send4[pl.ds(mey, 1)]

    channel(4, 0)
    channel(5, 0)
    forward(send4, relay4, recv4, rlsem4, rsem4)
    lax.fori_loop(6, 8, channel, 0)

    y_arrive(send4, recv4, ssem4, rsem4, twin)
    for chip in y_peers(False):
        for core in range(2):
            y_arrive(send4, recv4, ssem4, rsem4, chip * 2 + core)

    sent.append(y_copy(send1, recv1, ssem1, rsem1, twin))
    sent.append(y_copy(send4, recv4, ssem4, rsem4, twin))
    for chip in y_peers(True)[1:]:
        for core in range(2):
            sent.append(y_copy(send1, recv1, ssem1, rsem1, chip * 2 + core))
            sent.append(y_copy(send4, recv4, ssem4, rsem4, chip * 2 + core))
    for copy in sent:
        copy.wait_send()


def finish(npy, recv4, chan, b7_ref, out_hbm, done, sems):
    copies = []
    for g in range(4):
        lines = jnp.concatenate(
            [recv4[:, 16 * g : 16 * g + 16, :].reshape(npy, 1, 16, 128),
             recv4[:, 64 + 16 * g : 80 + 16 * g, :].reshape(npy, 1, 16, 128)], axis=1
        ).reshape(npy * 32, 128)
        values = dot(lines, b7_ref[...], TN)
        for o in range(8):
            total = values[:, 128 * o : 128 * o + 128] + chan[8 * g + o]
            done[8 * g + o] = gelu(total).astype(BF)
        block = pl.ds(8 * g, 8)
        copies.append(pltpu.make_async_copy(done.at[block], out_hbm.at[block], sems.at[g]))
        copies[-1].start()
    for copy in copies:
        copy.wait()


def body(npx, npy, field, spec_weight, w_in, b_in, w_out):
    mx = spec_weight.shape[4]
    a1, a2, tx, tix, b7, e8 = tables(npx, npy, mx)
    cells = field.reshape(C, XL * YL, NZ)
    weight = jnp.transpose(spec_weight[0], (0, 1, 2, 4, 5, 3)).reshape(2, C, C * K2, mx)
    vmem = pl.BlockSpec(memory_space=pltpu.VMEM)
    hbm = pl.BlockSpec(memory_space=pltpu.HBM)
    exchange = [pltpu.VMEM((npx, XL, 128), BF)] * 2
    loaded = [
        cells, jnp.asarray(a1), w_in[0], b_in, jnp.transpose(w_out[0]), weight,
        jnp.asarray(a2), jnp.asarray(tx), jnp.asarray(tix), jnp.asarray(e8),
    ]
    loaded = [pltpu.with_memory_space_constraint(a, pltpu.HBM) for a in loaded]
    lines, chan = pl.pallas_call(
        functools.partial(kernel, npx, npy),
        out_shape=(
            pltpu.VMEM((npy, 128, 128), BF),
            pltpu.VMEM((C, XL * YL, NZ), F32),
        ),
        in_specs=[hbm] * len(loaded),
        out_specs=(vmem, vmem),
        scratch_shapes=[
            pltpu.VMEM((npy, 2, 8, 8, 128), F32),
            pltpu.VMEM((npy, 128, 128), BF),
            pltpu.VMEM((npy, 128, 128), BF),
            pltpu.VMEM((2, 128, 128), BF),
            pltpu.VMEM((2, 128, 128), BF),
            *exchange,
            *exchange,
            pltpu.VMEM((npy, 128, 128), BF),
            *[pltpu.VMEM(a.shape, a.dtype) for a in loaded],
            pltpu.VMEM((HID * 8, C * 8), BF),
            pltpu.VMEM((C * 8, HID * 8), BF),
            pltpu.VMEM((HID * 8, 128), F32),
            pltpu.VMEM((2 * C, 8, mx), F32),
            pltpu.SemaphoreType.DMA((npy,)),
            pltpu.SemaphoreType.DMA((npy,)),
            pltpu.SemaphoreType.DMA((3, 2)),
            pltpu.SemaphoreType.DMA((2,)),
            pltpu.SemaphoreType.DMA((2,)),
            pltpu.SemaphoreType.DMA((npy,)),
            pltpu.SemaphoreType.DMA((npy,)),
            pltpu.SemaphoreType.DMA((3, 2)),
            pltpu.SemaphoreType.DMA((13,)),
        ],
        compiler_params=pltpu.CompilerParams(
            collective_id=0, has_side_effects=True, vmem_limit_bytes=32 * 1024 * 1024
        ),
    )(*loaded)
    out = pl.pallas_call(
        functools.partial(finish, npy),
        out_shape=jax.ShapeDtypeStruct((C, XL * YL, NZ), BF),
        in_specs=[vmem] * 3,
        out_specs=hbm,
        scratch_shapes=[pltpu.VMEM((C, XL * YL, NZ), BF), pltpu.SemaphoreType.DMA((4,))],
        compiler_params=pltpu.CompilerParams(vmem_limit_bytes=16 * 1024 * 1024),
    )(lines, chan, jnp.asarray(b7))
    return out.reshape(field.shape)


def solution(mesh):
    in_specs = (
        P(None, "px", "py", None),
        P(None, None, None, None, None, "px", "py"),
        P(),
        P(),
        P(),
    )
    return jax.shard_map(
        functools.partial(body, mesh.shape["px"], mesh.shape["py"]),
        mesh=mesh, in_specs=in_specs, out_specs=P(None, "px", "py", None), check_vma=False,
    )
```

```python
import functools
import math

import jax
import jax.numpy as jnp
import ml_dtypes
import numpy as np
from jax import lax
from jax.experimental import pallas as pl
from jax.experimental.pallas import tpu as pltpu
from jax.sharding import PartitionSpec as P

MESH = pl.DeviceIdType.MESH
BF = jnp.bfloat16
F32 = jnp.float32
C = 32
HID = 128
XL = 8
YL = 16
NZ = 128
K2 = 2
NT = (((1,), (1,)), ((), ()))
NN = (((1,), (0,)), ((), ()))
TN = (((0,), (0,)), ((), ()))


def dot(a, b, dims):
    return lax.dot_general(a, b, dims, preferred_element_type=F32)


def signed(count, length):
    index = np.arange(count)
    return np.where(index < count // 2, index, index - count + length)


def angles(positions, freqs, length):
    return 2.0 * math.pi * ((positions[:, None] * freqs[None, :]) % length) / length


def tables(npx, npy, mx):
    nx, ny, my, mz = XL * npx, YL * npy, npx, K2 * npy
    ang = angles(np.arange(NZ), np.arange(mz), NZ)
    fwd = np.stack([np.cos(ang), -np.sin(ang)]) * 0.125
    fwd = fwd.reshape(2, NZ, npy, K2).transpose(2, 0, 3, 1)
    a1 = np.zeros((2, npy, 2, 4, K2, 2, NZ))
    for q in range(2):
        for c in range(2):
            a1[q, :, :, 2 * q + c, :, c, :] = fwd
    a1 = a1.reshape(2, npy * 16, 2 * NZ)
    ang = angles(np.arange(ny), signed(my, ny), ny)
    cs = np.stack([np.cos(ang), np.sin(ang)]).reshape(2, npy // 2, 2, YL, my)
    a2 = np.zeros((npy // 2, 2, my, XL, 2, XL, YL))
    for x in range(XL):
        a2[:, :, :, x, :, x, :] = cs.transpose(1, 0, 4, 2, 3)
    a2 = a2.reshape(npy // 2, 2 * my * XL, 2 * XL * YL)
    ang = angles(np.arange(nx), signed(mx, nx), nx)
    cs = np.stack([np.cos(ang), np.sin(ang)])
    tx = cs.transpose(0, 2, 1).reshape(2 * mx, nx) / math.sqrt(nx * ny)
    tix = cs.reshape(2 * nx, mx) / math.sqrt(mx * my)
    ang = angles(np.arange(NZ), np.arange(mz), NZ)
    weight = np.where(np.arange(mz) == 0, 1.0, 2.0) * (8.0 / math.sqrt(NZ * mz))
    inv = np.stack([np.cos(ang), -np.sin(ang)]) * weight
    inv = inv.reshape(2, NZ, npy, K2).transpose(2, 0, 3, 1)
    b7 = np.zeros((npy, 2, 8, K2, 8, NZ))
    for o in range(8):
        b7[:, :, o, :, o, :] = inv
    b7 = b7.reshape(npy * 32, 8 * NZ)
    e8 = np.zeros((2 * C, 8, 2 * C, K2))
    for r in range(8):
        e8[np.arange(2 * C), r, np.arange(2 * C), r % 2] = 1.0
    e8 = e8.reshape(2 * C * 8, 2 * C * K2)

    def half(t):
        return t.astype(np.float32).astype(ml_dtypes.bfloat16)

    return half(a1), half(a2), half(tx), half(tix), half(b7), half(e8)


def gelu(v):
    k = math.sqrt(2.0 / math.pi)
    half = 0.5 * v
    return half + half * jnp.tanh(v * (k + (k * 0.044715) * (v * v)))


def kernel(
    npx, npy,
    f_hbm, a1_hbm, win_hbm, bin_hbm, wout_hbm, w_hbm, a2_hbm, tx_hbm, tix_hbm, e8_hbm,
    recv4, chan,
    zs, send1, recv1, relay1, relay4, send2, recv2, send3, recv3, send4,
    f_ref, a1_ref, win_ref, bin_ref, wout_ref, w_ref, a2_ref, tx_ref, tix_ref, e8_ref,
    k1, k2, bias, xpat,
    ssem1, rsem1, rlsem1, sems2, sems3, ssem4, rsem4, rlsem4, tsem,
):
    ny = npy // 2
    mx = w_ref.shape[-1]
    sent = []
    mex = lax.axis_index("px")
    mey = lax.axis_index("py")
    my_chip = mey // 2
    my_core = mey % 2
    twin = my_chip * 2 + 1 - my_core

    def load(i, src, dst):
        return pltpu.make_async_copy(src, dst, tsem.at[i])

    cells_in = [load(0, a1_hbm, a1_ref)] + [
        load(1 + i, f_hbm.at[pl.ds(i * 8, 8)], f_ref.at[pl.ds(i * 8, 8)]) for i in range(4)
    ]
    pairs = [(win_hbm, win_ref), (bin_hbm, bin_ref), (wout_hbm, wout_ref), (a2_hbm, a2_ref), (tx_hbm, tx_ref),
             (e8_hbm, e8_ref), (w_hbm, w_ref), (tix_hbm, tix_ref)]
    loads = [load(5 + i, src, dst) for i, (src, dst) in enumerate(pairs)]
    barrier = pltpu.get_barrier_semaphore()

    for load in cells_in:
        load.start()
    x_peers = [(mex + d) & (npx - 1) for d in range(1, npx)]
    y_peers_all = [(mey + d) & (npy - 1) for d in range(1, npy)]
    for peer in y_peers_all:
        pl.semaphore_signal(barrier, inc=1, device_id=(mex, peer), device_id_type=MESH)
    for peer in x_peers:
        pl.semaphore_signal(barrier, inc=1, device_id=(peer, mey), device_id_type=MESH)

    def forward_z(g, carry):
        f4 = f_ref[pl.ds(g * 4, 4)]
        acc = dot(a1_ref[0], jnp.concatenate([f4[0], f4[1]], axis=1), NT)
        acc = acc + dot(a1_ref[1], jnp.concatenate([f4[2], f4[3]], axis=1), NT)
        zs[:, :, pl.ds(g, 1)] = acc.reshape(npy, 2, 1, 8, 128)
        return carry

    cells_in[0].wait()
    for i in range(4):
        cells_in[1 + i].wait()
        lax.fori_loop(2 * i, 2 * i + 2, forward_z, 0, unroll=2)
    for load in loads:
        load.start()
    send1[...] = zs[...].reshape(npy, 128, 128).astype(BF)

    pl.semaphore_wait(barrier, npy + npx - 2)

    def y_copy(src, dst, ssem, rsem, target, many=True):
        return pltpu.make_async_remote_copy(
            src_ref=src.at[target], dst_ref=dst.at[mey], send_sem=ssem.at[0],
            recv_sem=rsem.at[mey if many else 0], device_id=(mex, target), device_id_type=MESH,
        )

    def y_whole(src, dst, ssem, rsem):
        return pltpu.make_async_remote_copy(
            src_ref=src.at[pl.ds(0, npy - 1)], dst_ref=dst.at[pl.ds(0, npy - 1)], send_sem=ssem.at[0],
            recv_sem=rsem.at[0], device_id=(mex, twin), device_id_type=MESH,
        )

    def y_arrive(src, dst, ssem, rsem, source):
        pltpu.make_async_remote_copy(
            src_ref=src.at[source], dst_ref=dst.at[source], send_sem=ssem.at[0], recv_sem=rsem.at[source],
            device_id=(mex, source), device_id_type=MESH,
        ).wait_recv()

    def x_exchange(src, dst, sems):
        for other in x_peers:
            pltpu.make_async_remote_copy(
                src_ref=src.at[other], dst_ref=dst.at[mex], send_sem=sems.at[0], recv_sem=sems.at[1],
                device_id=(other, mey), device_id_type=MESH,
            ).start()
        dst[pl.ds(mex, 1)] = src[pl.ds(mex, 1)]
        whole = pltpu.make_async_remote_copy(
            src_ref=src.at[pl.ds(0, npx - 1)], dst_ref=dst.at[pl.ds(0, npx - 1)], send_sem=sems.at[0],
            recv_sem=sems.at[1], device_id=(x_peers[0], mey), device_id_type=MESH,
        )
        whole.wait_recv()
        sent.append(whole)

    step = ny // 4
    quarter = [lax.rem(my_chip + step, ny) * 2 + my_core, lax.rem(my_chip + ny - step, ny) * 2 + my_core]
    opposite = lax.rem(my_chip + ny // 2, ny) * 2

    def to_relay(src, relay, ssem, sems, way):
        return pltpu.make_async_remote_copy(
            src_ref=src.at[opposite + way], dst_ref=relay.at[way], send_sem=ssem.at[0], recv_sem=sems.at[1, way],
            device_id=(mex, quarter[way]), device_id_type=MESH,
        )

    def from_relay(relay, dst, sems, rsem, way, many):
        source = quarter[1 - way]
        target = (quarter[way] - my_core) + way
        return pltpu.make_async_remote_copy(
            src_ref=relay.at[way], dst_ref=dst.at[source], send_sem=sems.at[0, way],
            recv_sem=rsem.at[source if many else 0],
            device_id=(mex, target), device_id_type=MESH,
        )

    def forward(src, relay, dst, ssem, sems, rsem, many):
        for way in range(2):
            to_relay(src, relay, ssem, sems, way).wait_recv()
            from_relay(relay, dst, sems, rsem, way, many).start()
            sent.append(from_relay(relay, dst, sems, rsem, way, many))

    def y_peers(far_first):
        offsets = sorted(range(1, ny), key=lambda d: min(d, ny - d), reverse=far_first)
        return [lax.rem(my_chip + d, ny) for d in offsets]

    for way in range(2):
        to_relay(send1, relay1, ssem1, rlsem1, way).start()
    for chip in y_peers(True)[1:]:
        for core in range(2):
            y_copy(send1, recv1, ssem1, rsem1, chip * 2 + core).start()
    y_copy(send1, recv1, ssem1, rsem1, twin).start()
    recv1[pl.ds(mey, 1)] = send1[pl.ds(mey, 1)]

    for i in range(3):
        loads[i].wait()
    spread = (lax.broadcasted_iota(jnp.int32, (C, C * 8), 1) >> 3 == lax.broadcasted_iota(jnp.int32, (C, C * 8), 0))
    rows = dot(win_ref[...], spread.astype(F32).astype(BF), TN)
    same = lax.broadcasted_iota(jnp.int32, (HID, 8, C * 8), 1) == (
        lax.broadcasted_iota(jnp.int32, (HID, 8, C * 8), 2) & 7
    )
    k1[...] = jnp.where(same, rows[:, None, :], 0.0).reshape(HID * 8, C * 8).astype(BF)
    spread = (
        lax.broadcasted_iota(jnp.int32, (HID, HID * 8), 1) >> 3 == lax.broadcasted_iota(jnp.int32, (HID, HID * 8), 0)
    )
    rows = dot(wout_ref[...], spread.astype(F32).astype(BF), NN)
    same = lax.broadcasted_iota(jnp.int32, (C, 8, HID * 8), 1) == (
        lax.broadcasted_iota(jnp.int32, (C, 8, HID * 8), 2) & 7
    )
    k2[...] = jnp.where(same, rows[:, None, :], 0.0).reshape(C * 8, HID * 8).astype(BF)
    turned = jnp.transpose(jnp.broadcast_to(bin_ref[...], (HID, HID)))
    bias[...] = jnp.broadcast_to(turned[:, None, :], (HID, 8, 128)).reshape(HID * 8, 128)

    forward(send1, relay1, recv1, ssem1, rlsem1, rsem1, True)

    def channel(i, carry):
        block = f_ref[:, pl.ds(pl.multiple_of(i * 16, 16), 16), :].astype(F32)
        cells = jnp.concatenate(
            [block[:, :8].reshape(C * 8, 128), block[:, 8:].reshape(C * 8, 128)], axis=1
        ).astype(BF)
        acc = jnp.zeros((C * 8, 256), F32)
        for part in range(4):
            rows = slice(part * 256, part * 256 + 256)
            b = bias[rows]
            hidden = gelu(dot(k1[rows], cells, NN) + jnp.concatenate([b, b], axis=1)).astype(BF)
            acc = acc + dot(k2[:, rows], hidden, NN)
        chan[:, pl.ds(pl.multiple_of(i * 16, 16), 8), :] = acc[:, :128].reshape(C, 8, 128)
        chan[:, pl.ds(pl.multiple_of(i * 16 + 8, 8), 8), :] = acc[:, 128:].reshape(C, 8, 128)
        return carry

    lax.fori_loop(0, 4, channel, 0)

    loads[3].wait()
    lane = lax.broadcasted_iota(jnp.int32, (1, 128), 1)
    sign = jnp.where(lane < 64, 1.0, -1.0)

    def y_part(chip):
        pair = jnp.concatenate([recv1[chip * 2], recv1[chip * 2 + 1]], axis=1)
        return dot(a2_ref[chip], pair, NT)

    y_arrive(send1, recv1, ssem1, rsem1, twin)
    acc = y_part(my_chip)
    for chip in y_peers(False):
        for core in range(2):
            y_arrive(send1, recv1, ssem1, rsem1, chip * 2 + core)
        acc = acc + y_part(chip)
    half = npx * XL
    lines = acc[:half] + sign * pltpu.roll(acc[half:], 64, 1)
    send2[...] = lines.reshape(npx, XL, 128).astype(BF)
    x_exchange(send2, recv2, sems2)

    loads[4].wait()
    loads[5].wait()
    block = recv2[...].astype(F32).reshape(half, 128).astype(BF)
    both = dot(tx_ref[...], block, NN)
    spectra = both[:mx] + sign * pltpu.roll(both[mx:], 64, 1)
    xpat[...] = dot(e8_ref[...], spectra.astype(BF), NT).reshape(2 * C, 8, mx)

    loads[6].wait()

    def mix(c, carry):
        real, imag = carry
        wr = w_ref[0, c].astype(F32).reshape(8, 8, mx)
        wi = w_ref[1, c].astype(F32).reshape(8, 8, mx)
        xr = xpat[c][None]
        xi = xpat[c + C][None]
        return real + xr * wr - xi * wi, imag + xr * wi + xi * wr

    zero = jnp.zeros((8, 8, mx), F32)
    real, imag = lax.fori_loop(0, C, mix, (zero, zero), unroll=4)
    modes = jnp.concatenate([real.reshape(64, mx), imag.reshape(64, mx)], axis=0)

    loads[7].wait()
    both = dot(tix_ref[...], modes.astype(BF), NT)
    cells = both[:half] - sign * pltpu.roll(both[half:], 64, 1)
    send3[...] = cells.reshape(npx, XL, 128).astype(BF)
    x_exchange(send3, recv3, sems3)

    turned = jnp.transpose(recv3[...].astype(F32).reshape(half, 128))
    turned = jnp.concatenate(
        [turned, jnp.concatenate([-turned[64:], turned[:64]], axis=0)], axis=1
    ).astype(BF)

    def y_back(chip):
        both = dot(turned, a2_ref[chip], NN).astype(BF)
        send4[pl.ds(chip * 2, 1)] = both[:, :128][None]
        send4[pl.ds(chip * 2 + 1, 1)] = both[:, 128:][None]

    for i, chip in enumerate(y_peers(True)):
        y_back(chip)
        for core in range(2):
            if i:
                y_copy(send4, recv4, ssem4, rsem4, chip * 2 + core, False).start()
            else:
                to_relay(send4, relay4, ssem4, rlsem4, core).start()
    y_back(my_chip)
    y_copy(send4, recv4, ssem4, rsem4, twin, False).start()
    recv4[pl.ds(mey, 1)] = send4[pl.ds(mey, 1)]

    channel(4, 0)
    channel(5, 0)
    sent.append(y_whole(send1, recv1, ssem1, rsem1))
    for copy in sent:
        copy.wait_send()
    sent.clear()
    forward(send4, relay4, recv4, ssem4, rlsem4, rsem4, False)
    lax.fori_loop(6, 8, channel, 0)

    y_whole(send4, recv4, ssem4, rsem4).wait_recv()
    sent.append(y_whole(send4, recv4, ssem4, rsem4))
    for copy in sent:
        copy.wait_send()


def finish(npy, recv4, chan, b7_ref, out_hbm, done, sems):
    copies = []
    for g in range(4):
        lines = jnp.concatenate(
            [recv4[:, 16 * g : 16 * g + 16, :].reshape(npy, 1, 16, 128),
             recv4[:, 64 + 16 * g : 80 + 16 * g, :].reshape(npy, 1, 16, 128)], axis=1
        ).reshape(npy * 32, 128)
        values = dot(lines, b7_ref[...], TN)
        for o in range(8):
            total = values[:, 128 * o : 128 * o + 128] + chan[8 * g + o]
            done[8 * g + o] = gelu(total).astype(BF)
        block = pl.ds(8 * g, 8)
        copies.append(pltpu.make_async_copy(done.at[block], out_hbm.at[block], sems.at[g]))
        copies[-1].start()
    for copy in copies:
        copy.wait()


def body(npx, npy, field, spec_weight, w_in, b_in, w_out):
    mx = spec_weight.shape[4]
    a1, a2, tx, tix, b7, e8 = tables(npx, npy, mx)
    cells = field.reshape(C, XL * YL, NZ)
    weight = jnp.transpose(spec_weight[0], (0, 1, 2, 4, 5, 3)).reshape(2, C, C * K2, mx)
    vmem = pl.BlockSpec(memory_space=pltpu.VMEM)
    hbm = pl.BlockSpec(memory_space=pltpu.HBM)
    exchange = [pltpu.VMEM((npx, XL, 128), BF)] * 2
    loaded = [
        cells, jnp.asarray(a1), w_in[0], b_in, jnp.transpose(w_out[0]), weight,
        jnp.asarray(a2), jnp.asarray(tx), jnp.asarray(tix), jnp.asarray(e8),
    ]
    loaded = [pltpu.with_memory_space_constraint(a, pltpu.HBM) for a in loaded]
    lines, chan = pl.pallas_call(
        functools.partial(kernel, npx, npy),
        out_shape=(
            pltpu.VMEM((npy, 128, 128), BF),
            pltpu.VMEM((C, XL * YL, NZ), F32),
        ),
        in_specs=[hbm] * len(loaded),
        out_specs=(vmem, vmem),
        scratch_shapes=[
            pltpu.VMEM((npy, 2, 8, 8, 128), F32),
            pltpu.VMEM((npy, 128, 128), BF),
            pltpu.VMEM((npy, 128, 128), BF),
            pltpu.VMEM((2, 128, 128), BF),
            pltpu.VMEM((2, 128, 128), BF),
            *exchange,
            *exchange,
            pltpu.VMEM((npy, 128, 128), BF),
            *[pltpu.VMEM(a.shape, a.dtype) for a in loaded],
            pltpu.VMEM((HID * 8, C * 8), BF),
            pltpu.VMEM((C * 8, HID * 8), BF),
            pltpu.VMEM((HID * 8, 128), F32),
            pltpu.VMEM((2 * C, 8, mx), F32),
            pltpu.SemaphoreType.DMA((1,)),
            pltpu.SemaphoreType.DMA((npy,)),
            pltpu.SemaphoreType.DMA((2, 2)),
            pltpu.SemaphoreType.DMA((2,)),
            pltpu.SemaphoreType.DMA((2,)),
            pltpu.SemaphoreType.DMA((1,)),
            pltpu.SemaphoreType.DMA((1,)),
            pltpu.SemaphoreType.DMA((2, 2)),
            pltpu.SemaphoreType.DMA((13,)),
        ],
        compiler_params=pltpu.CompilerParams(
            collective_id=0, has_side_effects=True, vmem_limit_bytes=32 * 1024 * 1024
        ),
    )(*loaded)
    out = pl.pallas_call(
        functools.partial(finish, npy),
        out_shape=jax.ShapeDtypeStruct((C, XL * YL, NZ), BF),
        in_specs=[vmem] * 3,
        out_specs=hbm,
        scratch_shapes=[pltpu.VMEM((C, XL * YL, NZ), BF), pltpu.SemaphoreType.DMA((4,))],
        compiler_params=pltpu.CompilerParams(vmem_limit_bytes=16 * 1024 * 1024),
    )(lines, chan, jnp.asarray(b7))
    return out.reshape(field.shape)


def solution(mesh):
    in_specs = (
        P(None, "px", "py", None),
        P(None, None, None, None, None, "px", "py"),
        P(),
        P(),
        P(),
    )
    return jax.shard_map(
        functools.partial(body, mesh.shape["px"], mesh.shape["py"]),
        mesh=mesh, in_specs=in_specs, out_specs=P(None, "px", "py", None), check_vma=False,
    )
```

```python
import functools
import math

import jax
import jax.numpy as jnp
import ml_dtypes
import numpy as np
from jax import lax
from jax.experimental import pallas as pl
from jax.experimental.pallas import tpu as pltpu
from jax.sharding import PartitionSpec as P

MESH = pl.DeviceIdType.MESH
BF = jnp.bfloat16
F32 = jnp.float32
C = 32
HID = 128
XL = 8
YL = 16
NZ = 128
K2 = 2
NT = (((1,), (1,)), ((), ()))
NN = (((1,), (0,)), ((), ()))
TN = (((0,), (0,)), ((), ()))


def dot(a, b, dims):
    return lax.dot_general(a, b, dims, preferred_element_type=F32)


def signed(count, length):
    index = np.arange(count)
    return np.where(index < count // 2, index, index - count + length)


def angles(positions, freqs, length):
    return 2.0 * math.pi * ((positions[:, None] * freqs[None, :]) % length) / length


def tables(npx, npy, mx):
    nx, ny, my, mz = XL * npx, YL * npy, npx, K2 * npy
    ang = angles(np.arange(NZ), np.arange(mz), NZ)
    fwd = np.stack([np.cos(ang), -np.sin(ang)]) * 0.125
    fwd = fwd.reshape(2, NZ, npy, K2).transpose(2, 3, 0, 1)
    a1 = np.zeros((2, npy, K2, 2, 4, 2, NZ))
    for q in range(2):
        for c in range(2):
            a1[q, :, :, :, 2 * q + c, c, :] = fwd
    a1 = a1.reshape(2, npy * 16, 2 * NZ)
    ang = angles(np.arange(ny), signed(my, ny), ny)
    cs = np.stack([np.cos(ang), np.sin(ang)]).reshape(2, npy // 2, 2, YL, my)
    a2 = np.zeros((npy // 2, 2, my, XL, 2, XL, YL))
    for x in range(XL):
        a2[:, :, :, x, :, x, :] = cs.transpose(1, 0, 4, 2, 3)
    a2 = a2.reshape(npy // 2, 2 * my * XL, 2 * XL * YL)
    ang = angles(np.arange(nx), signed(mx, nx), nx)
    cs = np.stack([np.cos(ang), np.sin(ang)])
    tx = cs.transpose(0, 2, 1).reshape(2 * mx, nx) / math.sqrt(nx * ny)
    tix = cs.reshape(2 * nx, mx) / math.sqrt(mx * my)
    ang = angles(np.arange(NZ), np.arange(mz), NZ)
    weight = np.where(np.arange(mz) == 0, 1.0, 2.0) * (8.0 / math.sqrt(NZ * mz))
    inv = np.stack([np.cos(ang), -np.sin(ang)]) * weight
    inv = inv.reshape(2, NZ, npy, K2).transpose(3, 2, 0, 1)
    b7 = np.zeros((K2, npy, 2, 2, 4, 8, NZ))
    for o in range(8):
        b7[:, :, o // 4, :, o % 4, o, :] = inv
    b7 = b7.reshape(npy * 32, 8 * NZ)
    e8 = np.zeros((2, C, 8, 2, C // 4, 2, 4))
    for c in range(C):
        for ri in range(2):
            e8[ri, c, :, 0, c // 4, ri, c % 4] = 1.0
    e8 = e8.reshape(2 * C * 8, 128)
    pick = np.zeros((K2, 2, C // 4, 2, 4, 2, C, K2))
    for o in range(C):
        for ri in range(2):
            for k in range(K2):
                pick[k, :, o // 4, ri, o % 4, ri, o, k] = 1.0
    pick = pick.reshape(K2, 128, 128)

    def half(t):
        return t.astype(np.float32).astype(ml_dtypes.bfloat16)

    return half(a1), half(a2), half(tx), half(tix), half(b7), half(e8), half(pick)


def gelu(v):
    k = math.sqrt(2.0 / math.pi)
    half = 0.5 * v
    return half + half * jnp.tanh(v * (k + (k * 0.044715) * (v * v)))


def kernel(
    npx, npy,
    f_hbm, a1_hbm, win_hbm, bin_hbm, wout_hbm, w_hbm, a2_hbm, tx_hbm, tix_hbm, e8_hbm, pick_hbm,
    recv4, chan,
    zs, send1, recv1, send2, recv2, send3, recv3, send4,
    f_ref, a1_ref, win_ref, bin_ref, wout_ref, w_ref, a2_ref, tx_ref, tix_ref, e8_ref, pick_ref,
    k1, k2, bias, xpat,
    ssem1, rsem1, sems2, sems3, ssem4, rsem4, tsem,
):
    ny = npy // 2
    mx = w_ref.shape[-1]
    sent = []
    mex = lax.axis_index("px")
    mey = lax.axis_index("py")
    my_chip = mey // 2
    my_core = mey % 2
    twin = my_chip * 2 + 1 - my_core

    def load(i, src, dst):
        return pltpu.make_async_copy(src, dst, tsem.at[i])

    cells_in = [load(0, a1_hbm, a1_ref)] + [
        load(1 + i, f_hbm.at[pl.ds(i * 8, 8)], f_ref.at[pl.ds(i * 8, 8)]) for i in range(4)
    ]
    pairs = [(win_hbm, win_ref), (bin_hbm, bin_ref), (wout_hbm, wout_ref), (a2_hbm, a2_ref), (tx_hbm, tx_ref),
             (e8_hbm, e8_ref), (w_hbm, w_ref), (tix_hbm, tix_ref), (pick_hbm, pick_ref)]
    loads = [load(5 + i, src, dst) for i, (src, dst) in enumerate(pairs)]
    barrier = pltpu.get_barrier_semaphore()

    for load in cells_in:
        load.start()
    x_peers = [(mex + d) & (npx - 1) for d in range(1, npx)]
    y_peers_all = [(mey + d) & (npy - 1) for d in range(1, npy)]
    for peer in y_peers_all:
        pl.semaphore_signal(barrier, inc=1, device_id=(mex, peer), device_id_type=MESH)
    for peer in x_peers:
        pl.semaphore_signal(barrier, inc=1, device_id=(peer, mey), device_id_type=MESH)

    def forward_z(g, carry):
        f4 = f_ref[pl.ds(g * 4, 4)]
        acc = dot(a1_ref[0], jnp.concatenate([f4[0], f4[1]], axis=1), NT)
        acc = acc + dot(a1_ref[1], jnp.concatenate([f4[2], f4[3]], axis=1), NT)
        zs[:, :, pl.ds(g, 1)] = acc.reshape(npy, K2, 1, 8, 128)
        return carry

    cells_in[0].wait()
    for i in range(4):
        cells_in[1 + i].wait()
        lax.fori_loop(2 * i, 2 * i + 2, forward_z, 0, unroll=2)
    for load in loads:
        load.start()
    for k in range(K2):
        send1[k] = zs[:, k].reshape(npy, 64, 128).astype(BF)

    pl.semaphore_wait(barrier, npy + npx - 2)

    def y_copy(k, src, dst, ssem, rsem, target, many=True):
        return pltpu.make_async_remote_copy(
            src_ref=src.at[k, target], dst_ref=dst.at[k, mey], send_sem=ssem.at[k],
            recv_sem=rsem.at[k, mey if many else 0], device_id=(mex, target), device_id_type=MESH,
        )

    def y_whole(k, src, dst, ssem, rsem):
        return pltpu.make_async_remote_copy(
            src_ref=src.at[k, pl.ds(0, npy - 1)], dst_ref=dst.at[k, pl.ds(0, npy - 1)], send_sem=ssem.at[k],
            recv_sem=rsem.at[k, 0], device_id=(mex, twin), device_id_type=MESH,
        )

    def y_arrive(k, source):
        pltpu.make_async_remote_copy(
            src_ref=send1.at[k, source], dst_ref=recv1.at[k, source], send_sem=ssem1.at[k],
            recv_sem=rsem1.at[k, source], device_id=(mex, source), device_id_type=MESH,
        ).wait_recv()

    def x_start(k, src, dst, sems):
        for other in x_peers:
            pltpu.make_async_remote_copy(
                src_ref=src.at[k, other], dst_ref=dst.at[k, mex], send_sem=sems.at[k, 0], recv_sem=sems.at[k, 1],
                device_id=(other, mey), device_id_type=MESH,
            ).start()
        dst[k, pl.ds(mex, 1)] = src[k, pl.ds(mex, 1)]

    def x_whole(k, src, dst, sems):
        return pltpu.make_async_remote_copy(
            src_ref=src.at[k, pl.ds(0, npx - 1)], dst_ref=dst.at[k, pl.ds(0, npx - 1)], send_sem=sems.at[k, 0],
            recv_sem=sems.at[k, 1], device_id=(x_peers[0], mey), device_id_type=MESH,
        )

    def y_peers(far_first):
        offsets = sorted(range(1, ny), key=lambda d: min(d, ny - d), reverse=far_first)
        return [lax.rem(my_chip + d, ny) for d in offsets]

    for k in range(K2):
        for chip in y_peers(True):
            for core in range(2):
                y_copy(k, send1, recv1, ssem1, rsem1, chip * 2 + core).start()
        y_copy(k, send1, recv1, ssem1, rsem1, twin).start()
        recv1[k, pl.ds(mey, 1)] = send1[k, pl.ds(mey, 1)]

    for i in range(3):
        loads[i].wait()
    spread = (lax.broadcasted_iota(jnp.int32, (C, C * 8), 1) >> 3 == lax.broadcasted_iota(jnp.int32, (C, C * 8), 0))
    rows = dot(win_ref[...], spread.astype(F32).astype(BF), TN)
    same = lax.broadcasted_iota(jnp.int32, (HID, 8, C * 8), 1) == (
        lax.broadcasted_iota(jnp.int32, (HID, 8, C * 8), 2) & 7
    )
    k1[...] = jnp.where(same, rows[:, None, :], 0.0).reshape(HID * 8, C * 8).astype(BF)
    spread = (
        lax.broadcasted_iota(jnp.int32, (HID, HID * 8), 1) >> 3 == lax.broadcasted_iota(jnp.int32, (HID, HID * 8), 0)
    )
    rows = dot(wout_ref[...], spread.astype(F32).astype(BF), NN)
    same = lax.broadcasted_iota(jnp.int32, (C, 8, HID * 8), 1) == (
        lax.broadcasted_iota(jnp.int32, (C, 8, HID * 8), 2) & 7
    )
    k2[...] = jnp.where(same, rows[:, None, :], 0.0).reshape(C * 8, HID * 8).astype(BF)
    turned = jnp.transpose(jnp.broadcast_to(bin_ref[...], (HID, HID)))
    bias[...] = jnp.broadcast_to(turned[:, None, :], (HID, 8, 128)).reshape(HID * 8, 128)

    def channel(i, carry):
        block = f_ref[:, pl.ds(pl.multiple_of(i * 16, 16), 16), :].astype(F32)
        cells = jnp.concatenate(
            [block[:, :8].reshape(C * 8, 128), block[:, 8:].reshape(C * 8, 128)], axis=1
        ).astype(BF)
        acc = jnp.zeros((C * 8, 256), F32)
        for part in range(4):
            rows = slice(part * 256, part * 256 + 256)
            b = bias[rows]
            hidden = gelu(dot(k1[rows], cells, NN) + jnp.concatenate([b, b], axis=1)).astype(BF)
            acc = acc + dot(k2[:, rows], hidden, NN)
        chan[:, pl.ds(pl.multiple_of(i * 16, 16), 8), :] = acc[:, :128].reshape(C, 8, 128)
        chan[:, pl.ds(pl.multiple_of(i * 16 + 8, 8), 8), :] = acc[:, 128:].reshape(C, 8, 128)
        return carry

    half = npx * XL
    lane = lax.broadcasted_iota(jnp.int32, (1, 128), 1)
    real_lane = (lane & 4) == 0
    sign = jnp.where(real_lane, 1.0, -1.0)

    def swap(v):
        return jnp.where(real_lane, pltpu.roll(v, 124, 1), pltpu.roll(v, 4, 1))

    def along_y(k):
        def part(chip):
            pair = jnp.concatenate([recv1[k, chip * 2], recv1[k, chip * 2 + 1]], axis=1)
            return dot(a2_ref[chip], jnp.concatenate([pair, pair], axis=0), NT)

        y_arrive(k, twin)
        acc = part(my_chip)
        for chip in y_peers(False):
            for core in range(2):
                y_arrive(k, chip * 2 + core)
            acc = acc + part(chip)
        lines = acc[:half] + sign * swap(acc[half:])
        send2[k] = lines.reshape(npx, XL, 128).astype(BF)
        x_start(k, send2, recv2, sems2)

    def mixed(k):
        x_whole(k, send2, recv2, sems2).wait_recv()
        block = recv2[k].astype(F32).reshape(half, 128).astype(BF)
        both = dot(tx_ref[...], block, NN)
        spectra = both[:mx] + sign * swap(both[mx:])
        xpat[...] = dot(e8_ref[...], spectra.astype(BF), NT).reshape(2 * C, 8, mx)

        def mix(c, carry):
            real, imag = carry
            wr = w_ref[0, c].astype(F32).reshape(8, 8, mx)
            wi = w_ref[1, c].astype(F32).reshape(8, 8, mx)
            xr = xpat[c][None]
            xi = xpat[c + C][None]
            return real + xr * wr - xi * wi, imag + xr * wi + xi * wr

        zero = jnp.zeros((8, 8, mx), F32)
        real, imag = lax.fori_loop(0, C, mix, (zero, zero), unroll=4)
        modes = jnp.concatenate([real.reshape(64, mx), imag.reshape(64, mx)], axis=0).astype(BF)
        modes = dot(pick_ref[k], modes, NN).astype(BF)

        both = dot(tix_ref[...], modes, NT)
        cells = both[:half] - sign * swap(both[half:])
        send3[k] = cells.reshape(npx, XL, 128).astype(BF)
        x_start(k, send3, recv3, sems3)

    def back_y(k):
        x_whole(k, send3, recv3, sems3).wait_recv()
        block = recv3[k].astype(F32).reshape(half, 128)
        turned = jnp.concatenate([block, -sign * swap(block)], axis=0)
        turned = jnp.transpose(turned)[:64].astype(BF)

        def cells(chip):
            both = dot(turned, a2_ref[chip], NN).astype(BF)
            send4[k, pl.ds(chip * 2, 1)] = both[:, :128][None]
            send4[k, pl.ds(chip * 2 + 1, 1)] = both[:, 128:][None]

        for chip in y_peers(True):
            cells(chip)
            for core in range(2):
                y_copy(k, send4, recv4, ssem4, rsem4, chip * 2 + core, False).start()
        cells(my_chip)
        y_copy(k, send4, recv4, ssem4, rsem4, twin, False).start()
        recv4[k, pl.ds(mey, 1)] = send4[k, pl.ds(mey, 1)]

    lax.fori_loop(0, 2, channel, 0)
    for i in range(3, 9):
        loads[i].wait()
    along_y(0)
    lax.fori_loop(2, 4, channel, 0)
    along_y(1)
    mixed(0)
    mixed(1)
    back_y(0)
    channel(4, 0)
    back_y(1)
    lax.fori_loop(5, 8, channel, 0)
    for k in range(K2):
        y_whole(k, send1, recv1, ssem1, rsem1).wait_send()
        x_whole(k, send2, recv2, sems2).wait_send()
        x_whole(k, send3, recv3, sems3).wait_send()
    for k in range(K2):
        y_whole(k, send4, recv4, ssem4, rsem4).wait_recv()
        sent.append(y_whole(k, send4, recv4, ssem4, rsem4))
    for copy in sent:
        copy.wait_send()


def finish(npy, recv4, chan, b7_ref, out_hbm, done, sems):
    copies = []
    for g in range(4):
        lines = recv4[:, :, 16 * g : 16 * g + 16, :].reshape(npy * 32, 128)
        values = dot(lines, b7_ref[...], TN)
        for o in range(8):
            total = values[:, 128 * o : 128 * o + 128] + chan[8 * g + o]
            done[8 * g + o] = gelu(total).astype(BF)
        block = pl.ds(8 * g, 8)
        copies.append(pltpu.make_async_copy(done.at[block], out_hbm.at[block], sems.at[g]))
        copies[-1].start()
    for copy in copies:
        copy.wait()


def body(npx, npy, field, spec_weight, w_in, b_in, w_out):
    mx = spec_weight.shape[4]
    a1, a2, tx, tix, b7, e8, pick = tables(npx, npy, mx)
    cells = field.reshape(C, XL * YL, NZ)
    weight = jnp.transpose(spec_weight[0], (0, 1, 2, 4, 5, 3)).reshape(2, C, C * K2, mx)
    vmem = pl.BlockSpec(memory_space=pltpu.VMEM)
    hbm = pl.BlockSpec(memory_space=pltpu.HBM)
    exchange = [pltpu.VMEM((K2, npx, XL, 128), BF)] * 2
    loaded = [
        cells, jnp.asarray(a1), w_in[0], b_in, jnp.transpose(w_out[0]), weight,
        jnp.asarray(a2), jnp.asarray(tx), jnp.asarray(tix), jnp.asarray(e8), jnp.asarray(pick),
    ]
    loaded = [pltpu.with_memory_space_constraint(a, pltpu.HBM) for a in loaded]
    lines, chan = pl.pallas_call(
        functools.partial(kernel, npx, npy),
        out_shape=(
            pltpu.VMEM((K2, npy, 64, 128), BF),
            pltpu.VMEM((C, XL * YL, NZ), F32),
        ),
        in_specs=[hbm] * len(loaded),
        out_specs=(vmem, vmem),
        scratch_shapes=[
            pltpu.VMEM((npy, K2, 8, 8, 128), F32),
            pltpu.VMEM((K2, npy, 64, 128), BF),
            pltpu.VMEM((K2, npy, 64, 128), BF),
            *exchange,
            *exchange,
            pltpu.VMEM((K2, npy, 64, 128), BF),
            *[pltpu.VMEM(a.shape, a.dtype) for a in loaded],
            pltpu.VMEM((HID * 8, C * 8), BF),
            pltpu.VMEM((C * 8, HID * 8), BF),
            pltpu.VMEM((HID * 8, 128), F32),
            pltpu.VMEM((2 * C, 8, mx), F32),
            pltpu.SemaphoreType.DMA((K2,)),
            pltpu.SemaphoreType.DMA((K2, npy)),
            pltpu.SemaphoreType.DMA((K2, 2)),
            pltpu.SemaphoreType.DMA((K2, 2)),
            pltpu.SemaphoreType.DMA((K2,)),
            pltpu.SemaphoreType.DMA((K2, 1)),
            pltpu.SemaphoreType.DMA((14,)),
        ],
        compiler_params=pltpu.CompilerParams(
            collective_id=0, has_side_effects=True, vmem_limit_bytes=32 * 1024 * 1024
        ),
    )(*loaded)
    out = pl.pallas_call(
        functools.partial(finish, npy),
        out_shape=jax.ShapeDtypeStruct((C, XL * YL, NZ), BF),
        in_specs=[vmem] * 3,
        out_specs=hbm,
        scratch_shapes=[pltpu.VMEM((C, XL * YL, NZ), BF), pltpu.SemaphoreType.DMA((4,))],
        compiler_params=pltpu.CompilerParams(vmem_limit_bytes=16 * 1024 * 1024),
    )(lines, chan, jnp.asarray(b7))
    return out.reshape(field.shape)


def solution(mesh):
    in_specs = (
        P(None, "px", "py", None),
        P(None, None, None, None, None, "px", "py"),
        P(),
        P(),
        P(),
    )
    return jax.shard_map(
        functools.partial(body, mesh.shape["px"], mesh.shape["py"]),
        mesh=mesh, in_specs=in_specs, out_specs=P(None, "px", "py", None), check_vma=False,
    )
```

```python
import functools
import math

import jax
import jax.numpy as jnp
import ml_dtypes
import numpy as np
from jax import lax
from jax.experimental import pallas as pl
from jax.experimental.pallas import tpu as pltpu
from jax.sharding import PartitionSpec as P

MESH = pl.DeviceIdType.MESH
BF = jnp.bfloat16
F32 = jnp.float32
C = 32
HID = 128
XL = 8
YL = 16
NZ = 128
K2 = 2
NT = (((1,), (1,)), ((), ()))
NN = (((1,), (0,)), ((), ()))
TN = (((0,), (0,)), ((), ()))


def dot(a, b, dims):
    return lax.dot_general(a, b, dims, preferred_element_type=F32)


def signed(count, length):
    index = np.arange(count)
    return np.where(index < count // 2, index, index - count + length)


def angles(positions, freqs, length):
    return 2.0 * math.pi * ((positions[:, None] * freqs[None, :]) % length) / length


def tables(npx, npy, mx):
    nx, ny, my, mz = XL * npx, YL * npy, npx, K2 * npy
    ang = angles(np.arange(NZ), np.arange(mz), NZ)
    fwd = np.stack([np.cos(ang), -np.sin(ang)]) * 0.125
    fwd = fwd.reshape(2, NZ, npy, K2).transpose(3, 2, 0, 1)
    a1 = np.zeros((2, K2, npy, 2, 4, 2, NZ))
    for q in range(2):
        for c in range(2):
            a1[q, :, :, :, 2 * q + c, c, :] = fwd
    a1 = a1.reshape(2, npy * 16, 2 * NZ)
    ang = angles(np.arange(ny), signed(my, ny), ny)
    cs = np.stack([np.cos(ang), np.sin(ang)]).reshape(2, npy // 2, 2, YL, my)
    a2 = np.zeros((npy // 2, 2, my, XL, 2, XL, YL))
    for x in range(XL):
        a2[:, :, :, x, :, x, :] = cs.transpose(1, 0, 4, 2, 3)
    a2 = a2.reshape(npy // 2, 2 * my * XL, 2 * XL * YL)
    ang = angles(np.arange(nx), signed(mx, nx), nx)
    cs = np.stack([np.cos(ang), np.sin(ang)])
    tx = cs.transpose(0, 2, 1).reshape(2 * mx, nx) / math.sqrt(nx * ny)
    tix = cs.reshape(2 * nx, mx) / math.sqrt(mx * my)
    ang = angles(np.arange(NZ), np.arange(mz), NZ)
    weight = np.where(np.arange(mz) == 0, 1.0, 2.0) * (8.0 / math.sqrt(NZ * mz))
    inv = np.stack([np.cos(ang), -np.sin(ang)]) * weight
    inv = inv.reshape(2, NZ, npy, K2).transpose(3, 2, 0, 1)
    b7 = np.zeros((K2, npy, 2, 2, 4, 8, NZ))
    for o in range(8):
        b7[:, :, o // 4, :, o % 4, o, :] = inv
    b7 = b7.reshape(K2, npy * 16, 8 * NZ)
    e8 = np.zeros((2, C, 8, 2, C // 4, 2, 4))
    for c in range(C):
        for ri in range(2):
            e8[ri, c, :, 0, c // 4, ri, c % 4] = 1.0
    e8 = e8.reshape(2 * C * 8, 128)
    pick = np.zeros((K2, 2, C // 4, 2, 4, 2, C, K2))
    for o in range(C):
        for ri in range(2):
            for k in range(K2):
                pick[k, :, o // 4, ri, o % 4, ri, o, k] = 1.0
    pick = pick.reshape(K2, 128, 128)

    def half(t):
        return t.astype(np.float32).astype(ml_dtypes.bfloat16)

    return half(a1), half(a2), half(tx), half(tix), half(b7), half(e8), half(pick)


def gelu(v):
    k = math.sqrt(2.0 / math.pi)
    half = 0.5 * v
    return half + half * jnp.tanh(v * (k + (k * 0.044715) * (v * v)))


def kernel(
    npx, npy,
    f_hbm, a1_hbm, win_hbm, bin_hbm, wout_hbm, w_hbm, a2_hbm, tx_hbm, tix_hbm, e8_hbm, pick_hbm, b7_hbm,
    recv4, chan,
    zs, send1, recv1, send2, recv2, send3, recv3, send4,
    f_ref, a1_ref, win_ref, bin_ref, wout_ref, w_ref, a2_ref, tx_ref, tix_ref, e8_ref, pick_ref, b7_ref,
    k1, k2, bias, xpat,
    ssem1, rsem1, sems2, sems3, ssem4, rsem4, tsem,
):
    ny = npy // 2
    mx = w_ref.shape[-1]
    sent = []
    mex = lax.axis_index("px")
    mey = lax.axis_index("py")
    my_chip = mey // 2
    my_core = mey % 2
    twin = my_chip * 2 + 1 - my_core

    def load(i, src, dst):
        return pltpu.make_async_copy(src, dst, tsem.at[i])

    cells_in = [load(0, a1_hbm, a1_ref)] + [
        load(1 + i, f_hbm.at[pl.ds(i * 8, 8)], f_ref.at[pl.ds(i * 8, 8)]) for i in range(4)
    ]
    pairs = [(win_hbm, win_ref), (bin_hbm, bin_ref), (wout_hbm, wout_ref), (a2_hbm, a2_ref), (tx_hbm, tx_ref),
             (e8_hbm, e8_ref), (w_hbm, w_ref), (tix_hbm, tix_ref), (pick_hbm, pick_ref), (b7_hbm, b7_ref)]
    loads = [load(5 + i, src, dst) for i, (src, dst) in enumerate(pairs)]
    barrier = pltpu.get_barrier_semaphore()

    for load in cells_in:
        load.start()
    x_peers = [(mex + d) & (npx - 1) for d in range(1, npx)]
    y_peers_all = [(mey + d) & (npy - 1) for d in range(1, npy)]
    for peer in y_peers_all:
        pl.semaphore_signal(barrier, inc=1, device_id=(mex, peer), device_id_type=MESH)
    for peer in x_peers:
        pl.semaphore_signal(barrier, inc=1, device_id=(peer, mey), device_id_type=MESH)

    def forward_z(k, groups):
        def four(g, carry):
            f4 = f_ref[pl.ds(g * 4, 4)]
            rows = slice(k * npy * 8, (k + 1) * npy * 8)
            acc = dot(a1_ref[0, rows], jnp.concatenate([f4[0], f4[1]], axis=1), NT)
            acc = acc + dot(a1_ref[1, rows], jnp.concatenate([f4[2], f4[3]], axis=1), NT)
            zs[:, pl.ds(g, 1)] = acc.reshape(npy, 1, 8, 128)
            return carry

        lax.fori_loop(groups[0], groups[1], four, 0, unroll=2)

    cells_in[0].wait()
    for i in range(4):
        cells_in[1 + i].wait()
        forward_z(0, (2 * i, 2 * i + 2))
    send1[0] = zs[...].reshape(npy, 64, 128).astype(BF)

    pl.semaphore_wait(barrier, npy + npx - 2)

    def y_copy(k, src, dst, ssem, rsem, target, many=True):
        return pltpu.make_async_remote_copy(
            src_ref=src.at[k, target], dst_ref=dst.at[k, mey], send_sem=ssem.at[k],
            recv_sem=rsem.at[k, mey if many else 0], device_id=(mex, target), device_id_type=MESH,
        )

    def y_whole(k, src, dst, ssem, rsem):
        return pltpu.make_async_remote_copy(
            src_ref=src.at[k, pl.ds(0, npy - 1)], dst_ref=dst.at[k, pl.ds(0, npy - 1)], send_sem=ssem.at[k],
            recv_sem=rsem.at[k, 0], device_id=(mex, twin), device_id_type=MESH,
        )

    def y_arrive(k, source):
        pltpu.make_async_remote_copy(
            src_ref=send1.at[k, source], dst_ref=recv1.at[k, source], send_sem=ssem1.at[k],
            recv_sem=rsem1.at[k, source], device_id=(mex, source), device_id_type=MESH,
        ).wait_recv()

    def x_start(k, src, dst, sems):
        for other in x_peers:
            pltpu.make_async_remote_copy(
                src_ref=src.at[k, other], dst_ref=dst.at[k, mex], send_sem=sems.at[k, 0], recv_sem=sems.at[k, 1],
                device_id=(other, mey), device_id_type=MESH,
            ).start()
        dst[k, pl.ds(mex, 1)] = src[k, pl.ds(mex, 1)]

    def x_whole(k, src, dst, sems):
        return pltpu.make_async_remote_copy(
            src_ref=src.at[k, pl.ds(0, npx - 1)], dst_ref=dst.at[k, pl.ds(0, npx - 1)], send_sem=sems.at[k, 0],
            recv_sem=sems.at[k, 1], device_id=(x_peers[0], mey), device_id_type=MESH,
        )

    def y_peers(far_first):
        offsets = sorted(range(1, ny), key=lambda d: min(d, ny - d), reverse=far_first)
        return [lax.rem(my_chip + d, ny) for d in offsets]

    for k in range(K2):
        for chip in y_peers(True):
            for core in range(2):
                y_copy(k, send1, recv1, ssem1, rsem1, chip * 2 + core).start()
        y_copy(k, send1, recv1, ssem1, rsem1, twin).start()
        recv1[k, pl.ds(mey, 1)] = send1[k, pl.ds(mey, 1)]
        if k == 0:
            for load in loads:
                load.start()
            forward_z(1, (0, C // 4))
            send1[1] = zs[...].reshape(npy, 64, 128).astype(BF)

    for i in range(3):
        loads[i].wait()
    spread = (lax.broadcasted_iota(jnp.int32, (C, C * 8), 1) >> 3 == lax.broadcasted_iota(jnp.int32, (C, C * 8), 0))
    rows = dot(win_ref[...], spread.astype(F32).astype(BF), TN)
    same = lax.broadcasted_iota(jnp.int32, (HID, 8, C * 8), 1) == (
        lax.broadcasted_iota(jnp.int32, (HID, 8, C * 8), 2) & 7
    )
    k1[...] = jnp.where(same, rows[:, None, :], 0.0).reshape(HID * 8, C * 8).astype(BF)
    spread = (
        lax.broadcasted_iota(jnp.int32, (HID, HID * 8), 1) >> 3 == lax.broadcasted_iota(jnp.int32, (HID, HID * 8), 0)
    )
    rows = dot(wout_ref[...], spread.astype(F32).astype(BF), NN)
    same = lax.broadcasted_iota(jnp.int32, (C, 8, HID * 8), 1) == (
        lax.broadcasted_iota(jnp.int32, (C, 8, HID * 8), 2) & 7
    )
    k2[...] = jnp.where(same, rows[:, None, :], 0.0).reshape(C * 8, HID * 8).astype(BF)
    turned = jnp.transpose(jnp.broadcast_to(bin_ref[...], (HID, HID)))
    bias[...] = jnp.broadcast_to(turned[:, None, :], (HID, 8, 128)).reshape(HID * 8, 128)

    def channel(i, carry):
        block = f_ref[:, pl.ds(pl.multiple_of(i * 16, 16), 16), :].astype(F32)
        cells = jnp.concatenate(
            [block[:, :8].reshape(C * 8, 128), block[:, 8:].reshape(C * 8, 128)], axis=1
        ).astype(BF)
        acc = jnp.zeros((C * 8, 256), F32)
        for part in range(4):
            rows = slice(part * 256, part * 256 + 256)
            b = bias[rows]
            hidden = gelu(dot(k1[rows], cells, NN) + jnp.concatenate([b, b], axis=1)).astype(BF)
            acc = acc + dot(k2[:, rows], hidden, NN)
        chan[:, pl.ds(pl.multiple_of(i * 16, 16), 8), :] = acc[:, :128].reshape(C, 8, 128)
        chan[:, pl.ds(pl.multiple_of(i * 16 + 8, 8), 8), :] = acc[:, 128:].reshape(C, 8, 128)
        return carry

    half = npx * XL
    lane = lax.broadcasted_iota(jnp.int32, (1, 128), 1)
    real_lane = (lane & 4) == 0
    sign = jnp.where(real_lane, 1.0, -1.0)

    def swap(v):
        return jnp.where(real_lane, pltpu.roll(v, 124, 1), pltpu.roll(v, 4, 1))

    def along_y(k):
        def part(chip):
            pair = jnp.concatenate([recv1[k, chip * 2], recv1[k, chip * 2 + 1]], axis=1)
            return dot(a2_ref[chip], jnp.concatenate([pair, pair], axis=0), NT)

        y_arrive(k, twin)
        acc = part(my_chip)
        for chip in y_peers(False):
            for core in range(2):
                y_arrive(k, chip * 2 + core)
            acc = acc + part(chip)
        lines = acc[:half] + sign * swap(acc[half:])
        send2[k] = lines.reshape(npx, XL, 128).astype(BF)
        x_start(k, send2, recv2, sems2)

    def mixed(k):
        x_whole(k, send2, recv2, sems2).wait_recv()
        block = recv2[k].astype(F32).reshape(half, 128).astype(BF)
        both = dot(tx_ref[...], block, NN)
        spectra = both[:mx] + sign * swap(both[mx:])
        xpat[...] = dot(e8_ref[...], spectra.astype(BF), NT).reshape(2 * C, 8, mx)

        def mix(c, carry):
            real, imag = carry
            wr = w_ref[0, c].astype(F32).reshape(8, 8, mx)
            wi = w_ref[1, c].astype(F32).reshape(8, 8, mx)
            xr = xpat[c][None]
            xi = xpat[c + C][None]
            return real + xr * wr - xi * wi, imag + xr * wi + xi * wr

        zero = jnp.zeros((8, 8, mx), F32)
        real, imag = lax.fori_loop(0, C, mix, (zero, zero), unroll=4)
        modes = jnp.concatenate([real.reshape(64, mx), imag.reshape(64, mx)], axis=0).astype(BF)
        modes = dot(pick_ref[k], modes, NN).astype(BF)

        both = dot(tix_ref[...], modes, NT)
        cells = both[:half] - sign * swap(both[half:])
        send3[k] = cells.reshape(npx, XL, 128).astype(BF)
        x_start(k, send3, recv3, sems3)

    def back_y(k):
        x_whole(k, send3, recv3, sems3).wait_recv()
        block = recv3[k].astype(F32).reshape(half, 128)
        turned = jnp.concatenate([block, -sign * swap(block)], axis=0)
        turned = jnp.transpose(turned)[:64].astype(BF)

        def cells(chip):
            both = dot(turned, a2_ref[chip], NN).astype(BF)
            send4[k, pl.ds(chip * 2, 1)] = both[:, :128][None]
            send4[k, pl.ds(chip * 2 + 1, 1)] = both[:, 128:][None]

        for chip in y_peers(True):
            cells(chip)
            for core in range(2):
                y_copy(k, send4, recv4, ssem4, rsem4, chip * 2 + core, False).start()
        cells(my_chip)
        y_copy(k, send4, recv4, ssem4, rsem4, twin, False).start()
        recv4[k, pl.ds(mey, 1)] = send4[k, pl.ds(mey, 1)]

    lax.fori_loop(0, 2, channel, 0)
    for i in range(3, 10):
        loads[i].wait()
    along_y(0)
    lax.fori_loop(2, 4, channel, 0)
    along_y(1)
    mixed(0)
    mixed(1)
    back_y(0)
    channel(4, 0)
    back_y(1)
    lax.fori_loop(5, 8, channel, 0)
    for k in range(K2):
        y_whole(k, send1, recv1, ssem1, rsem1).wait_send()
        x_whole(k, send2, recv2, sems2).wait_send()
        x_whole(k, send3, recv3, sems3).wait_send()
    y_whole(0, send4, recv4, ssem4, rsem4).wait_recv()
    for g in range(4):
        values = back_z(recv4, 0, b7_ref, g)
        for o in range(8):
            chan[8 * g + o] = chan[8 * g + o] + values[:, 128 * o : 128 * o + 128]
    y_whole(1, send4, recv4, ssem4, rsem4).wait_recv()
    for k in range(K2):
        sent.append(y_whole(k, send4, recv4, ssem4, rsem4))
    for copy in sent:
        copy.wait_send()


def back_z(lines, k, table, g):
    rows = lines[k, :, 16 * g : 16 * g + 16, :]
    return dot(rows.reshape(rows.shape[0] * 16, 128), table[...], TN)


def finish(recv4, chan, b7_ref, out_hbm, done, sems):
    copies = []
    for g in range(4):
        values = back_z(recv4, 1, b7_ref, g)
        for o in range(8):
            total = values[:, 128 * o : 128 * o + 128] + chan[8 * g + o]
            done[8 * g + o] = gelu(total).astype(BF)
        block = pl.ds(8 * g, 8)
        copies.append(pltpu.make_async_copy(done.at[block], out_hbm.at[block], sems.at[g]))
        copies[-1].start()
    for copy in copies:
        copy.wait()


def body(npx, npy, field, spec_weight, w_in, b_in, w_out):
    mx = spec_weight.shape[4]
    a1, a2, tx, tix, b7, e8, pick = tables(npx, npy, mx)
    cells = field.reshape(C, XL * YL, NZ)
    weight = jnp.transpose(spec_weight[0], (0, 1, 2, 4, 5, 3)).reshape(2, C, C * K2, mx)
    vmem = pl.BlockSpec(memory_space=pltpu.VMEM)
    hbm = pl.BlockSpec(memory_space=pltpu.HBM)
    exchange = [pltpu.VMEM((K2, npx, XL, 128), BF)] * 2
    loaded = [
        cells, jnp.asarray(a1), w_in[0], b_in, jnp.transpose(w_out[0]), weight,
        jnp.asarray(a2), jnp.asarray(tx), jnp.asarray(tix), jnp.asarray(e8), jnp.asarray(pick), jnp.asarray(b7[0]),
    ]
    loaded = [pltpu.with_memory_space_constraint(a, pltpu.HBM) for a in loaded]
    lines, chan = pl.pallas_call(
        functools.partial(kernel, npx, npy),
        out_shape=(
            pltpu.VMEM((K2, npy, 64, 128), BF),
            pltpu.VMEM((C, XL * YL, NZ), F32),
        ),
        in_specs=[hbm] * len(loaded),
        out_specs=(vmem, vmem),
        scratch_shapes=[
            pltpu.VMEM((npy, 8, 8, 128), F32),
            pltpu.VMEM((K2, npy, 64, 128), BF),
            pltpu.VMEM((K2, npy, 64, 128), BF),
            *exchange,
            *exchange,
            pltpu.VMEM((K2, npy, 64, 128), BF),
            *[pltpu.VMEM(a.shape, a.dtype) for a in loaded],
            pltpu.VMEM((HID * 8, C * 8), BF),
            pltpu.VMEM((C * 8, HID * 8), BF),
            pltpu.VMEM((HID * 8, 128), F32),
            pltpu.VMEM((2 * C, 8, mx), F32),
            pltpu.SemaphoreType.DMA((K2,)),
            pltpu.SemaphoreType.DMA((K2, npy)),
            pltpu.SemaphoreType.DMA((K2, 2)),
            pltpu.SemaphoreType.DMA((K2, 2)),
            pltpu.SemaphoreType.DMA((K2,)),
            pltpu.SemaphoreType.DMA((K2, 1)),
            pltpu.SemaphoreType.DMA((15,)),
        ],
        compiler_params=pltpu.CompilerParams(
            collective_id=0, has_side_effects=True, vmem_limit_bytes=32 * 1024 * 1024
        ),
    )(*loaded)
    out = pl.pallas_call(
        finish,
        out_shape=jax.ShapeDtypeStruct((C, XL * YL, NZ), BF),
        in_specs=[vmem] * 3,
        out_specs=hbm,
        scratch_shapes=[pltpu.VMEM((C, XL * YL, NZ), BF), pltpu.SemaphoreType.DMA((4,))],
        compiler_params=pltpu.CompilerParams(vmem_limit_bytes=16 * 1024 * 1024),
    )(lines, chan, jnp.asarray(b7[1]))
    return out.reshape(field.shape)


def solution(mesh):
    in_specs = (
        P(None, "px", "py", None),
        P(None, None, None, None, None, "px", "py"),
        P(),
        P(),
        P(),
    )
    return jax.shard_map(
        functools.partial(body, mesh.shape["px"], mesh.shape["py"]),
        mesh=mesh, in_specs=in_specs, out_specs=P(None, "px", "py", None), check_vma=False,
    )
```

```python
import functools
import math

import jax
import jax.numpy as jnp
import ml_dtypes
import numpy as np
from jax import lax
from jax.experimental import pallas as pl
from jax.experimental.pallas import tpu as pltpu
from jax.sharding import PartitionSpec as P

MESH = pl.DeviceIdType.MESH
BF = jnp.bfloat16
F32 = jnp.float32
C = 32
HID = 128
XL = 8
YL = 16
NZ = 128
K2 = 2
NT = (((1,), (1,)), ((), ()))
NN = (((1,), (0,)), ((), ()))
TN = (((0,), (0,)), ((), ()))


def dot(a, b, dims):
    return lax.dot_general(a, b, dims, preferred_element_type=F32)


def signed(count, length):
    index = np.arange(count)
    return np.where(index < count // 2, index, index - count + length)


def angles(positions, freqs, length):
    return 2.0 * math.pi * ((positions[:, None] * freqs[None, :]) % length) / length


def tables(npx, npy, mx):
    nx, ny, my, mz = XL * npx, YL * npy, npx, K2 * npy
    ang = angles(np.arange(NZ), np.arange(mz), NZ)
    fwd = np.stack([np.cos(ang), -np.sin(ang)]) * 0.125
    fwd = fwd.reshape(2, NZ, npy, K2).transpose(3, 2, 0, 1)
    a1 = np.zeros((2, K2, npy, 2, 4, 2, NZ))
    for q in range(2):
        for c in range(2):
            a1[q, :, :, :, 2 * q + c, c, :] = fwd
    a1 = a1.reshape(2, npy * 16, 2 * NZ)
    ang = angles(np.arange(ny), signed(my, ny), ny)
    cs = np.stack([np.cos(ang), np.sin(ang)]).reshape(2, npy // 2, 2, YL, my)
    a2 = np.zeros((npy // 2, 2, my, XL, 2, XL, YL))
    for x in range(XL):
        a2[:, :, :, x, :, x, :] = cs.transpose(1, 0, 4, 2, 3)
    a2 = a2.reshape(npy // 2, 2 * my * XL, 2 * XL * YL)
    ang = angles(np.arange(nx), signed(mx, nx), nx)
    cs = np.stack([np.cos(ang), np.sin(ang)])
    tx = cs.transpose(0, 2, 1).reshape(2 * mx, nx) / math.sqrt(nx * ny)
    tix = cs.reshape(2 * nx, mx) / math.sqrt(mx * my)
    ang = angles(np.arange(NZ), np.arange(mz), NZ)
    weight = np.where(np.arange(mz) == 0, 1.0, 2.0) * (8.0 / math.sqrt(NZ * mz))
    inv = np.stack([np.cos(ang), -np.sin(ang)]) * weight
    inv = inv.reshape(2, NZ, npy, K2).transpose(3, 2, 0, 1)
    b7 = np.zeros((K2, npy, 2, 2, 4, 8, NZ))
    for o in range(8):
        b7[:, :, o // 4, :, o % 4, o, :] = inv
    b7 = b7.reshape(K2, npy * 16, 8 * NZ)
    e8 = np.zeros((2, C, 8, 2, C // 4, 2, 4))
    for c in range(C):
        for ri in range(2):
            e8[ri, c, :, 0, c // 4, ri, c % 4] = 1.0
    e8 = e8.reshape(2 * C * 8, 128)
    pick = np.zeros((K2, 2, C // 4, 2, 4, 2, C, K2))
    for o in range(C):
        for ri in range(2):
            for k in range(K2):
                pick[k, :, o // 4, ri, o % 4, ri, o, k] = 1.0
    pick = pick.reshape(K2, 128, 128)

    def half(t):
        return t.astype(np.float32).astype(ml_dtypes.bfloat16)

    return half(a1), half(a2), half(tx), half(tix), half(b7), half(e8), half(pick)


def gelu(v):
    k = math.sqrt(2.0 / math.pi)
    half = 0.5 * v
    return half + half * jnp.tanh(v * (k + (k * 0.044715) * (v * v)))


def kernel(
    npx, npy,
    f_hbm, a1_hbm, win_hbm, bin_hbm, wout_hbm, w_hbm, a2_hbm, tx_hbm, tix_hbm, e8_hbm, pick_hbm, b7_hbm,
    recv4, chan,
    zs, send1, recv1, send2, recv2, send3, recv3, send4,
    f_ref, a1_ref, win_ref, bin_ref, wout_ref, w_ref, a2_ref, tx_ref, tix_ref, e8_ref, pick_ref, b7_ref,
    k1, k2, bias, xpat,
    ssem1, rsem1, sems2, sems3, ssem4, rsem4, tsem,
):
    ny = npy // 2
    mx = w_ref.shape[-1]
    sent = []
    mex = lax.axis_index("px")
    mey = lax.axis_index("py")
    my_chip = mey // 2
    my_core = mey % 2
    twin = my_chip * 2 + 1 - my_core

    def load(i, src, dst):
        return pltpu.make_async_copy(src, dst, tsem.at[i])

    cells_in = [load(0, a1_hbm, a1_ref)] + [
        load(1 + i, f_hbm.at[pl.ds(i * 8, 8)], f_ref.at[pl.ds(i * 8, 8)]) for i in range(4)
    ]
    pairs = [(win_hbm, win_ref), (bin_hbm, bin_ref), (wout_hbm, wout_ref), (a2_hbm, a2_ref), (tx_hbm, tx_ref),
             (e8_hbm, e8_ref), (w_hbm, w_ref), (tix_hbm, tix_ref), (pick_hbm, pick_ref), (b7_hbm, b7_ref)]
    loads = [load(5 + i, src, dst) for i, (src, dst) in enumerate(pairs)]
    barrier = pltpu.get_barrier_semaphore()

    for load in cells_in:
        load.start()
    x_peers = [(mex + d) & (npx - 1) for d in range(1, npx)]
    y_peers_all = [(mey + d) & (npy - 1) for d in range(1, npy)]
    for peer in y_peers_all:
        pl.semaphore_signal(barrier, inc=1, device_id=(mex, peer), device_id_type=MESH)
    for peer in x_peers:
        pl.semaphore_signal(barrier, inc=1, device_id=(peer, mey), device_id_type=MESH)

    def forward_z(k, groups):
        def four(g, carry):
            f4 = f_ref[pl.ds(g * 4, 4)]
            rows = slice(k * npy * 8, (k + 1) * npy * 8)
            acc = dot(a1_ref[0, rows], jnp.concatenate([f4[0], f4[1]], axis=1), NT)
            acc = acc + dot(a1_ref[1, rows], jnp.concatenate([f4[2], f4[3]], axis=1), NT)
            zs[:, pl.ds(g, 1)] = acc.reshape(npy, 1, 8, 128)
            return carry

        lax.fori_loop(groups[0], groups[1], four, 0, unroll=2)

    cells_in[0].wait()
    for i in range(4):
        cells_in[1 + i].wait()
        forward_z(0, (2 * i, 2 * i + 2))
    send1[0] = zs[...].reshape(npy, 64, 128).astype(BF)

    pl.semaphore_wait(barrier, npy + npx - 2)

    def y_copy(k, src, dst, ssem, rsem, target, many=True):
        return pltpu.make_async_remote_copy(
            src_ref=src.at[k, target], dst_ref=dst.at[k, mey], send_sem=ssem.at[k],
            recv_sem=rsem.at[k, mey if many else 0], device_id=(mex, target), device_id_type=MESH,
        )

    def y_whole(k, src, dst, ssem, rsem):
        return pltpu.make_async_remote_copy(
            src_ref=src.at[k, pl.ds(0, npy - 1)], dst_ref=dst.at[k, pl.ds(0, npy - 1)], send_sem=ssem.at[k],
            recv_sem=rsem.at[k, 0], device_id=(mex, twin), device_id_type=MESH,
        )

    def y_arrive(k, source):
        pltpu.make_async_remote_copy(
            src_ref=send1.at[k, source], dst_ref=recv1.at[k, source], send_sem=ssem1.at[k],
            recv_sem=rsem1.at[k, source], device_id=(mex, source), device_id_type=MESH,
        ).wait_recv()

    def x_start(k, src, dst, sems):
        for other in x_peers:
            pltpu.make_async_remote_copy(
                src_ref=src.at[k, other], dst_ref=dst.at[k, mex], send_sem=sems.at[k, 0], recv_sem=sems.at[k, 1],
                device_id=(other, mey), device_id_type=MESH,
            ).start()
        dst[k, pl.ds(mex, 1)] = src[k, pl.ds(mex, 1)]

    def x_whole(k, src, dst, sems):
        return pltpu.make_async_remote_copy(
            src_ref=src.at[k, pl.ds(0, npx - 1)], dst_ref=dst.at[k, pl.ds(0, npx - 1)], send_sem=sems.at[k, 0],
            recv_sem=sems.at[k, 1], device_id=(x_peers[0], mey), device_id_type=MESH,
        )

    def y_peers(far_first):
        offsets = sorted(range(1, ny), key=lambda d: min(d, ny - d), reverse=far_first)
        return [lax.rem(my_chip + d, ny) for d in offsets]

    for k in range(K2):
        for chip in y_peers(True):
            for core in range(2):
                y_copy(k, send1, recv1, ssem1, rsem1, chip * 2 + core).start()
        y_copy(k, send1, recv1, ssem1, rsem1, twin).start()
        recv1[k, pl.ds(mey, 1)] = send1[k, pl.ds(mey, 1)]
        if k == 0:
            for load in loads:
                load.start()
            forward_z(1, (0, C // 4))
            send1[1] = zs[...].reshape(npy, 64, 128).astype(BF)

    for i in range(3):
        loads[i].wait()
    spread = (lax.broadcasted_iota(jnp.int32, (C, C * 8), 1) >> 3 == lax.broadcasted_iota(jnp.int32, (C, C * 8), 0))
    rows = dot(win_ref[...], spread.astype(F32).astype(BF), TN)
    same = lax.broadcasted_iota(jnp.int32, (HID, 8, C * 8), 1) == (
        lax.broadcasted_iota(jnp.int32, (HID, 8, C * 8), 2) & 7
    )
    k1[...] = jnp.where(same, rows[:, None, :], 0.0).reshape(HID * 8, C * 8).astype(BF)
    spread = (
        lax.broadcasted_iota(jnp.int32, (HID, HID * 8), 1) >> 3 == lax.broadcasted_iota(jnp.int32, (HID, HID * 8), 0)
    )
    rows = dot(wout_ref[...], spread.astype(F32).astype(BF), NN)
    same = lax.broadcasted_iota(jnp.int32, (C, 8, HID * 8), 1) == (
        lax.broadcasted_iota(jnp.int32, (C, 8, HID * 8), 2) & 7
    )
    k2[...] = jnp.where(same, rows[:, None, :], 0.0).reshape(C * 8, HID * 8).astype(BF)
    turned = jnp.transpose(jnp.broadcast_to(bin_ref[...], (HID, HID)))
    bias[...] = jnp.broadcast_to(turned[:, None, :], (HID, 8, 128)).reshape(HID * 8, 128)

    def channel(i, carry):
        block = f_ref[:, pl.ds(pl.multiple_of(i * 16, 16), 16), :].astype(F32)
        cells = jnp.concatenate(
            [block[:, :8].reshape(C * 8, 128), block[:, 8:].reshape(C * 8, 128)], axis=1
        ).astype(BF)
        acc = jnp.zeros((C * 8, 256), F32)
        for part in range(4):
            rows = slice(part * 256, part * 256 + 256)
            b = bias[rows]
            hidden = gelu(dot(k1[rows], cells, NN) + jnp.concatenate([b, b], axis=1)).astype(BF)
            acc = acc + dot(k2[:, rows], hidden, NN)
        chan[:, pl.ds(pl.multiple_of(i * 16, 16), 8), :] = acc[:, :128].reshape(C, 8, 128)
        chan[:, pl.ds(pl.multiple_of(i * 16 + 8, 8), 8), :] = acc[:, 128:].reshape(C, 8, 128)
        return carry

    half = npx * XL
    lane = lax.broadcasted_iota(jnp.int32, (1, 128), 1)
    real_lane = (lane & 4) == 0
    sign = jnp.where(real_lane, 1.0, -1.0)

    def swap(v):
        return jnp.where(real_lane, pltpu.roll(v, 124, 1), pltpu.roll(v, 4, 1))

    def along_y(k):
        def part(chip):
            pair = jnp.concatenate([recv1[k, chip * 2], recv1[k, chip * 2 + 1]], axis=1)
            return dot(a2_ref[chip], jnp.concatenate([pair, pair], axis=0), NT)

        y_arrive(k, twin)
        acc = part(my_chip)
        for chip in y_peers(False):
            for core in range(2):
                y_arrive(k, chip * 2 + core)
            acc = acc + part(chip)
        lines = acc[:half] + sign * swap(acc[half:])
        send2[k] = lines.reshape(npx, XL, 128).astype(BF)
        x_start(k, send2, recv2, sems2)

    def mixed(k):
        x_whole(k, send2, recv2, sems2).wait_recv()
        block = recv2[k].astype(F32).reshape(half, 128).astype(BF)
        both = dot(tx_ref[...], block, NN)
        spectra = both[:mx] + sign * swap(both[mx:])
        xpat[...] = dot(e8_ref[...], spectra.astype(BF), NT).reshape(2 * C, 8, mx)

        def mix(c, carry):
            real, imag = carry
            wr = w_ref[0, c].astype(F32).reshape(8, 8, mx)
            wi = w_ref[1, c].astype(F32).reshape(8, 8, mx)
            xr = xpat[c][None]
            xi = xpat[c + C][None]
            return real + xr * wr - xi * wi, imag + xr * wi + xi * wr

        zero = jnp.zeros((8, 8, mx), F32)
        real, imag = lax.fori_loop(0, C, mix, (zero, zero), unroll=4)
        modes = jnp.concatenate([real.reshape(64, mx), imag.reshape(64, mx)], axis=0).astype(BF)
        modes = dot(pick_ref[k], modes, NN).astype(BF)

        both = dot(tix_ref[...], modes, NT)
        cells = both[:half] - sign * swap(both[half:])
        send3[k] = cells.reshape(npx, XL, 128).astype(BF)
        x_start(k, send3, recv3, sems3)

    def back_y(k):
        x_whole(k, send3, recv3, sems3).wait_recv()
        block = recv3[k].astype(F32).reshape(half, 128)
        turned = jnp.concatenate([block, -sign * swap(block)], axis=0)
        turned = jnp.transpose(turned)[:64].astype(BF)

        def cells(chip):
            both = dot(turned, a2_ref[chip], NN).astype(BF)
            send4[k, pl.ds(chip * 2, 1)] = both[:, :128][None]
            send4[k, pl.ds(chip * 2 + 1, 1)] = both[:, 128:][None]

        for chip in y_peers(True):
            cells(chip)
            for core in range(2):
                y_copy(k, send4, recv4, ssem4, rsem4, chip * 2 + core, False).start()
        cells(my_chip)
        y_copy(k, send4, recv4, ssem4, rsem4, twin, False).start()
        recv4[k, pl.ds(mey, 1)] = send4[k, pl.ds(mey, 1)]

    lax.fori_loop(0, 2, channel, 0)
    for i in range(3, 10):
        loads[i].wait()
    along_y(0)
    channel(2, 0)
    mixed(0)
    along_y(1)
    mixed(1)
    back_y(0)
    lax.fori_loop(3, 5, channel, 0)
    back_y(1)
    lax.fori_loop(5, 8, channel, 0)
    for k in range(K2):
        y_whole(k, send1, recv1, ssem1, rsem1).wait_send()
        x_whole(k, send2, recv2, sems2).wait_send()
        x_whole(k, send3, recv3, sems3).wait_send()
    y_whole(0, send4, recv4, ssem4, rsem4).wait_recv()
    for g in range(4):
        values = back_z(recv4, 0, b7_ref, g)
        for o in range(8):
            chan[8 * g + o] = chan[8 * g + o] + values[:, 128 * o : 128 * o + 128]
    y_whole(1, send4, recv4, ssem4, rsem4).wait_recv()
    for k in range(K2):
        sent.append(y_whole(k, send4, recv4, ssem4, rsem4))
    for copy in sent:
        copy.wait_send()


def back_z(lines, k, table, g):
    rows = lines[k, :, 16 * g : 16 * g + 16, :]
    return dot(rows.reshape(rows.shape[0] * 16, 128), table[...], TN)


def finish(recv4, chan, b7_ref, out_hbm, done, sems):
    copies = []
    for g in range(4):
        values = back_z(recv4, 1, b7_ref, g)
        for o in range(8):
            total = values[:, 128 * o : 128 * o + 128] + chan[8 * g + o]
            done[8 * g + o] = gelu(total).astype(BF)
        block = pl.ds(8 * g, 8)
        copies.append(pltpu.make_async_copy(done.at[block], out_hbm.at[block], sems.at[g]))
        copies[-1].start()
    for copy in copies:
        copy.wait()


def body(npx, npy, field, spec_weight, w_in, b_in, w_out):
    mx = spec_weight.shape[4]
    a1, a2, tx, tix, b7, e8, pick = tables(npx, npy, mx)
    cells = field.reshape(C, XL * YL, NZ)
    weight = jnp.transpose(spec_weight[0], (0, 1, 2, 4, 5, 3)).reshape(2, C, C * K2, mx)
    vmem = pl.BlockSpec(memory_space=pltpu.VMEM)
    hbm = pl.BlockSpec(memory_space=pltpu.HBM)
    exchange = [pltpu.VMEM((K2, npx, XL, 128), BF)] * 2
    loaded = [
        cells, jnp.asarray(a1), w_in[0], b_in, jnp.transpose(w_out[0]), weight,
        jnp.asarray(a2), jnp.asarray(tx), jnp.asarray(tix), jnp.asarray(e8), jnp.asarray(pick), jnp.asarray(b7[0]),
    ]
    loaded = [pltpu.with_memory_space_constraint(a, pltpu.HBM) for a in loaded]
    lines, chan = pl.pallas_call(
        functools.partial(kernel, npx, npy),
        out_shape=(
            pltpu.VMEM((K2, npy, 64, 128), BF),
            pltpu.VMEM((C, XL * YL, NZ), F32),
        ),
        in_specs=[hbm] * len(loaded),
        out_specs=(vmem, vmem),
        scratch_shapes=[
            pltpu.VMEM((npy, 8, 8, 128), F32),
            pltpu.VMEM((K2, npy, 64, 128), BF),
            pltpu.VMEM((K2, npy, 64, 128), BF),
            *exchange,
            *exchange,
            pltpu.VMEM((K2, npy, 64, 128), BF),
            *[pltpu.VMEM(a.shape, a.dtype) for a in loaded],
            pltpu.VMEM((HID * 8, C * 8), BF),
            pltpu.VMEM((C * 8, HID * 8), BF),
            pltpu.VMEM((HID * 8, 128), F32),
            pltpu.VMEM((2 * C, 8, mx), F32),
            pltpu.SemaphoreType.DMA((K2,)),
            pltpu.SemaphoreType.DMA((K2, npy)),
            pltpu.SemaphoreType.DMA((K2, 2)),
            pltpu.SemaphoreType.DMA((K2, 2)),
            pltpu.SemaphoreType.DMA((K2,)),
            pltpu.SemaphoreType.DMA((K2, 1)),
            pltpu.SemaphoreType.DMA((15,)),
        ],
        compiler_params=pltpu.CompilerParams(
            collective_id=0, has_side_effects=True, vmem_limit_bytes=32 * 1024 * 1024
        ),
    )(*loaded)
    out = pl.pallas_call(
        finish,
        out_shape=jax.ShapeDtypeStruct((C, XL * YL, NZ), BF),
        in_specs=[vmem] * 3,
        out_specs=hbm,
        scratch_shapes=[pltpu.VMEM((C, XL * YL, NZ), BF), pltpu.SemaphoreType.DMA((4,))],
        compiler_params=pltpu.CompilerParams(vmem_limit_bytes=16 * 1024 * 1024),
    )(lines, chan, jnp.asarray(b7[1]))
    return out.reshape(field.shape)


def solution(mesh):
    in_specs = (
        P(None, "px", "py", None),
        P(None, None, None, None, None, "px", "py"),
        P(),
        P(),
        P(),
    )
    return jax.shard_map(
        functools.partial(body, mesh.shape["px"], mesh.shape["py"]),
        mesh=mesh, in_specs=in_specs, out_specs=P(None, "px", "py", None), check_vma=False,
    )
```
